32 devices in a mesh: dp: 8 (over y, x, core), seq: 4 (over z).
Axes of the slice: x: 2, y: 2, z: 4, core: 2. Of those that a mesh axis runs over, the one named last changes fastest.
Arguments:
- patches: bfloat16 [24, 532, 768], P('dp', 'seq'), may hold values from -6 to 6
- segments: int32 [24, 532], P('dp', 'seq'), may hold values from 0 to 3, as said below
- first_gain: bfloat16 [768], replicated, may hold values from 0.099609375 to 1.8984375
- first_bias: bfloat16 [768], replicated, may hold values from -1.75 to 1.75
- input_weight: bfloat16 [768, 2304], replicated, may hold values from -0.3125 to 0.3125
- query_bias: bfloat16 [768], replicated, may hold values from -3 to 3
- value_bias: bfloat16 [768], replicated, may hold values from -3 to 3
- output_weight: bfloat16 [768, 768], replicated, may hold values from -0.875 to 0.875
- output_bias: bfloat16 [768], replicated, may hold values from -1.75 to 1.75
- second_gain: bfloat16 [768], replicated, may hold values from 0.099609375 to 1.8984375
- second_bias: bfloat16 [768], replicated, may hold values from -1.75 to 1.75
- up_weight: bfloat16 [768, 3072], replicated, may hold values from -0.21875 to 0.21875
- up_bias: bfloat16 [3072], replicated, may hold values from -1.75 to 1.75
- down_weight: bfloat16 [3072, 768], replicated, may hold values from -0.109375 to 0.109375
- down_bias: bfloat16 [768], replicated, may hold values from -1.75 to 1.75
- cotangent: bfloat16 [24, 532, 768], P('dp', 'seq'), may hold values from -6 to 6
Outputs:
- block_output: bfloat16 [24, 532, 768], P('dp', 'seq')
- input_grad: float32 [24, 532, 768], P('dp', 'seq')
- first_gain_grad: float32 [768], replicated
- first_bias_grad: float32 [768], replicated
- input_weight_grad: float32 [768, 2304], P('dp', 'seq')
- query_bias_grad: float32 [768], replicated
- value_bias_grad: float32 [768], replicated
- output_weight_grad: float32 [768, 768], P('dp', 'seq')
- output_bias_grad: float32 [768], replicated
- second_gain_grad: float32 [768], replicated
- second_bias_grad: float32 [768], replicated
- up_weight_grad: float32 [768, 3072], P('dp', 'seq')
- up_bias_grad: float32 [3072], replicated
- down_weight_grad: float32 [3072, 768], P('dp', 'seq')
- down_bias_grad: float32 [768], replicated
The draws below stay inside these ranges and needn't reach their ends.
Inputs may be any that keep to these rules, and one draw needn't show every extreme that they name: `segments`: 0 marks the padding at a strip's end and attends only to padding; other ids never fall along a strip and name packed documents; every strip holds padding and document 3; attention stays within equal ids.
All inputs are finite; a program needn't handle non-finite values.
Results may differ from the reference program's by a relative error of at most 0.012.
The reference program's roundings to bfloat16 on the way count: a program that leaves them out, or rounds other values in their place, can miss the bound.
Values may be sent and summed in bfloat16 or wider, within the bound.
A program may use at most 128 MiB of HBM per device.

```python
import jax
import jax.numpy as jnp
from jax import lax

D = 768
HEADS = 12
HEAD_DIM = 64
FF = 3072
PER_DEV = 133
STRIPS_DEV = 3
SEQ_LEN = 532
STRIPS = 24
N_DP = 8


def draw_segments(key, part):
    key = jax.random.fold_in(key, 7)
    keys = jax.random.split(key, 3)
    padding = jax.random.randint(keys[0], (STRIPS, 1), 1, min(4, PER_DEV - 1))
    real_end = SEQ_LEN - padding
    start = jax.random.randint(keys[1], (STRIPS, 1), 0, PER_DEV // 2 + 1)
    finish = real_end - jax.random.randint(keys[2], (STRIPS, 1), 1, PER_DEV // 3 + 2)
    finish = jnp.maximum(finish, 3 * PER_DEV + 1)
    positions = jnp.arange(SEQ_LEN, dtype=jnp.int32)[None, :]
    ids = jnp.where(positions < start, 1, jnp.where(positions < finish, 2, 3))
    ids = jnp.where(positions >= real_end, 0, ids)
    return ids.astype(jnp.int32)


def spiked(values, own_key, source, target, shards_of, factor):
    def block_of(axis_at):
        return (jnp.arange(values.shape[axis_at]) // (values.shape[axis_at] // shards_of)).reshape((-1,) + (1,) * (values.ndim - 1 - axis_at))

    near = jax.random.permutation(own_key, shards_of)[block_of(target)]
    far = (block_of(target) + shards_of // 2) % shards_of
    return jnp.where((block_of(source) == near) | (block_of(source) == far), factor * values, values)


def level_of(rng, shape, pieces, least, largest):
    def one(dim, parts):
        draws = jax.random.uniform(jax.random.fold_in(jax.random.fold_in(rng, 6), dim), (parts,), jnp.float32, least / len(pieces), largest / len(pieces))
        return jnp.repeat(jnp.exp(draws), shape[dim] // parts).reshape((-1,) + (1,) * (len(shape) - dim - 1))

    gain = one(*pieces[0])
    for cut in pieces[1:]:
        gain = gain * one(*cut)
    return gain


def gaussian(stream_key, dims, deviation, bound, cuts=(), kind=jnp.bfloat16):
    loudness = level_of(stream_key, dims, cuts, -0.22, 0.18) if cuts else 1.0
    array = jax.random.normal(stream_key, dims, jnp.float32) * deviation * loudness
    return jnp.minimum(jnp.maximum(array, -bound), bound).astype(kind)


def gaussian_with(rng, dims, scale, limit, cuts, heavy, kind=jnp.bfloat16):
    values = scale * jax.random.normal(rng, dims, jnp.float32)
    if cuts:
        values = values * level_of(rng, dims, cuts, -0.22, 0.18)
    return jnp.clip(spiked(values, jax.random.fold_in(rng, 3), *heavy), -limit, limit).astype(kind)


def setup_inputs(seed: int = 0) -> dict:
    seeds = jax.random.split(jax.random.key(seed), 17)
    return {
        "patches": gaussian_with(seeds[0], (STRIPS, SEQ_LEN, D), 1.0, 6.0, ((0, 8), (1, 4)), (0, 2, 8, 2.0)),
        "segments": draw_segments(jax.random.fold_in(seeds[16], 71), 0),
        "first_gain": jnp.clip(1.0 + 0.18 * jax.random.normal(seeds[2], (D,), jnp.float32), 0.099609375, 1.8984375).astype(jnp.bfloat16),
        "first_bias": gaussian(seeds[3], (D,), 0.3, 1.75),
        "input_weight": gaussian(seeds[4], (D, 3 * D), (D // 2) ** -0.5, 0.3125),
        "query_bias": gaussian(seeds[5], (D,), 0.5, 3.0),
        "value_bias": gaussian(seeds[6], (D,), 0.5, 3.0),
        "output_weight": gaussian(seeds[7], (D, D), (D // 16) ** -0.5, 0.875),
        "output_bias": gaussian(seeds[8], (D,), 0.3, 1.75),
        "second_gain": jnp.clip(1.0 + 0.18 * jax.random.normal(seeds[9], (D,), jnp.float32), 0.099609375, 1.8984375).astype(jnp.bfloat16),
        "second_bias": gaussian(seeds[10], (D,), 0.3, 1.75),
        "up_weight": gaussian(seeds[11], (D, FF), D ** -0.5, 0.21875),
        "up_bias": gaussian(seeds[12], (FF,), 0.3, 1.75),
        "down_weight": gaussian(seeds[13], (FF, D), FF ** -0.5, 0.109375),
        "down_bias": gaussian(seeds[14], (D,), 0.3, 1.75),
        "cotangent": gaussian(seeds[15], (STRIPS, SEQ_LEN, D), 1.0, 6.0, ((0, 8), (1, 4))),
    }


EPSILON = 1e-06
NEGATIVE = -1e+30

@jax.custom_vjp
def low(v):
    return lax.optimization_barrier(v.astype(jnp.bfloat16)).astype(jnp.float32)

@jax.custom_vjp
def low_back(v):
    return v

def low_keep(v):
    return (low(v), None)

def low_pass(kept, grad):
    return (grad,)

def back_keep(v):
    return (v, None)

def back_low(kept, grad):
    return (low(grad),)
low.defvjp(low_keep, low_pass)
low_back.defvjp(back_keep, back_low)

def layer_norm(values, scales, offset):
    middle = lax.optimization_barrier(jnp.mean(values, axis=-1, keepdims=True))
    centered = values - middle
    spread = lax.optimization_barrier(jnp.mean(centered * centered, axis=-1, keepdims=True))
    return centered * lax.rsqrt(spread + EPSILON) * scales + offset

def dense(left, right):
    return jnp.dot(left, right, precision=lax.Precision.HIGHEST, preferred_element_type=jnp.float32)

def attend_strip(operands):
    queries, keys, values, segment_row = operands
    raw = jnp.einsum('qhd,khd->hqk', queries, keys, precision=lax.Precision.HIGHEST) * HEAD_DIM ** (-0.5)
    scores = low_back(raw)
    same = segment_row[:, None] == segment_row[None, :]
    scores = jnp.where(same[None], scores, NEGATIVE)
    highest = lax.optimization_barrier(jnp.max(scores, axis=-1, keepdims=True))
    exponent = jnp.exp(scores - highest)
    totals = lax.optimization_barrier(jnp.sum(exponent, axis=-1, keepdims=True))
    probs = low(exponent / totals)
    return jnp.einsum('hqk,khd->qhd', probs, values, precision=lax.Precision.HIGHEST)

def block_forward(block, segment_rows, params):
    first_gain, first_bias, input_weight, query_bias, value_bias, output_weight, output_bias, second_gain, second_bias, up_weight, up_bias, down_weight, down_bias = params
    strips = block.shape[0]
    rows = block.reshape(-1, D)
    normed_in = low(layer_norm(rows, first_gain, first_bias))
    bias_row = jnp.concatenate([query_bias, jnp.zeros_like(query_bias), value_bias])
    mixed = low(low_back(dense(normed_in, input_weight) + bias_row))
    mixed = mixed.reshape(strips, SEQ_LEN, 3, HEADS, HEAD_DIM)
    attended = lax.map(jax.checkpoint(attend_strip), (mixed[:, :, 0], mixed[:, :, 1], mixed[:, :, 2], segment_rows))
    attended = low(low_back(attended.reshape(-1, D)))
    residual = rows + low_back(dense(attended, output_weight) + output_bias)
    normed_mid = low(layer_norm(residual, second_gain, second_bias))
    upper = low_back(dense(normed_mid, up_weight) + up_bias)
    hidden = low(jax.nn.gelu(upper, approximate=False))
    return residual + low_back(dense(hidden, down_weight) + down_bias)

def reference(patches, segments, first_gain, first_bias, input_weight, query_bias, value_bias, output_weight, output_bias, second_gain, second_bias, up_weight, up_bias, down_weight, down_bias, cotangent):
    params = tuple((p.astype(jnp.float32) for p in (first_gain, first_bias, input_weight, query_bias, value_bias, output_weight, output_bias, second_gain, second_bias, up_weight, up_bias, down_weight, down_bias)))
    grouped = patches.astype(jnp.float32).reshape(N_DP, STRIPS_DEV, SEQ_LEN, D)
    grouped_ids = segments.reshape(N_DP, STRIPS_DEV, SEQ_LEN)
    grouped_back = cotangent.astype(jnp.float32).reshape(N_DP, STRIPS_DEV * SEQ_LEN, D)

    def one_group(totals, inputs):
        block, segment_rows, backward = inputs

        def forward(block_in, params_in):
            return block_forward(block_in, segment_rows, params_in)
        output, pullback = jax.vjp(forward, block, params)
        grad_block, grad_params = pullback(backward)
        totals = tuple((t + g for t, g in zip(totals, grad_params)))
        return (totals, (output.astype(jnp.bfloat16), grad_block))
    zeros = tuple((jnp.zeros_like(p) for p in params))
    totals, (outputs, grads) = lax.scan(one_group, zeros, (grouped, grouped_ids, grouped_back))
    block_output = outputs.reshape(STRIPS, SEQ_LEN, D)
    input_grad = grads.reshape(STRIPS, SEQ_LEN, D)
    return (block_output, input_grad, totals[0], totals[1], totals[2], totals[3], totals[4], totals[5], totals[6], totals[7], totals[8], totals[9], totals[10], totals[11], totals[12])
```

```python
import functools

import jax
import jax.numpy as jnp
from jax import lax
from jax.experimental import pallas as pl
from jax.experimental.pallas import tpu as pltpu
from jax.sharding import PartitionSpec as P

F32 = jnp.float32
BF = jnp.bfloat16
EPS = 1e-6
VL = 60 << 20
PART = 136

def nn(a,b): return lax.dot_general(a,b,(((1,),(0,)),((),())),preferred_element_type=F32)
def nt(a,b): return lax.dot_general(a,b,(((1,),(1,)),((),())),preferred_element_type=F32)
def tn(a,b): return lax.dot_general(a,b,(((0,),(0,)),((),())),preferred_element_type=F32)

def norm_parts(v):
    mid=jnp.mean(v,axis=-1,keepdims=True)
    c=v-mid
    r=lax.rsqrt(jnp.mean(c*c,axis=-1,keepdims=True)+EPS)
    return c*r,r

G1, B1, QB, VB, OB, G2, B2, DB = range(8)


def ka_kernel(x_ref, eq_ref, ek_ref, par_ref, wq_ref, wk_ref, wv_ref, qb_ref, vb_ref, wo_ref,
              q_out, k_out, v_out, att_out, lse_out, nmid_out, res_out, acc, nin_ref):
    i = pl.program_id(0)
    rows = x_ref.shape[0]

    @pl.when(i == 0)
    def _():
        xh, _r = norm_parts(x_ref[...].astype(F32))
        nin_ref[...] = (xh * par_ref[G1:G1 + 1] + par_ref[B1:B1 + 1]).astype(BF)
        acc[...] = jnp.zeros_like(acc)

    nin = nin_ref[...]
    q_out[...] = (nn(nin, wq_ref[...]) + qb_ref[QB:QB + 1]).astype(BF)
    k_out[...] = nn(nin, wk_ref[...]).astype(BF)
    v_out[...] = (nn(nin, wv_ref[...]) + vb_ref[VB:VB + 1]).astype(BF)
    lane = lax.broadcasted_iota(jnp.int32, (rows, 128), 1)
    eq = eq_ref[...]
    ek = ek_ref[...]
    for pair in range(2):
        cols = slice(128 * pair, 128 * pair + 128)
        qp = q_out[:, cols] * jnp.asarray(0.125, BF)
        kp = jnp.concatenate([k_out[:, cols], ek], axis=1)
        vp = v_out[:, cols]
        zero = jnp.zeros_like(qp)
        both = jnp.concatenate([jnp.concatenate([jnp.where(lane < 64, qp, zero), eq], axis=1),
                                jnp.concatenate([jnp.where(lane < 64, zero, qp), eq], axis=1)], axis=0)
        s = nt(both, kp)
        m = jnp.max(s, axis=-1, keepdims=True)
        e = jnp.exp(s - m)
        t = jnp.sum(e, axis=-1, keepdims=True)
        p = (e * (1.0 / t)).astype(BF)
        o = nn(p, vp)
        log = m + jnp.log(t)
        lse_out[:, 2 * pair:2 * pair + 1] = log[:rows]
        lse_out[:, 2 * pair + 1:2 * pair + 2] = log[rows:]
        att_out[:, cols] = jnp.where(lane < 64, o[:rows], o[rows:]).astype(BF)
    acc[...] += nn(att_out[...], wo_ref[...])

    @pl.when(i == pl.num_programs(0) - 1)
    def _():
        res = x_ref[...].astype(F32) + acc[...] + par_ref[OB:OB + 1]
        res_out[...] = res
        xh, _r = norm_parts(res)
        nmid_out[...] = (xh * par_ref[G2:G2 + 1] + par_ref[B2:B2 + 1]).astype(BF)


def ka(x, eq, ek, par, wi, wo):
    rows, D = x.shape
    full = lambda a: pl.BlockSpec(a.shape, lambda i: (0,) * a.ndim)
    n = 3
    blk = pl.BlockSpec((rows, 256), lambda i: (0, i))
    whole = pl.BlockSpec((rows, D), lambda i: (0, 0))
    S = jax.ShapeDtypeStruct
    wcol = lambda j: pl.BlockSpec((D, 256), lambda i: (0, n * j + i))
    pcol = pl.BlockSpec((8, 256), lambda i: (0, i))
    return pl.pallas_call(
        ka_kernel, grid=(n,),
        in_specs=[full(x), full(eq), full(ek), full(par), wcol(0), wcol(1), wcol(2), pcol, pcol,
                  pl.BlockSpec((256, D), lambda i: (i, 0))],
        out_specs=[blk, blk, blk, blk, pl.BlockSpec((rows, 128), lambda i: (0, i)), whole, whole],
        out_shape=[S((rows, D), BF)] * 4 + [S((rows, 384), F32), S((rows, D), BF), S((rows, D), F32)],
        scratch_shapes=[pltpu.VMEM((rows, D), F32), pltpu.VMEM((rows, D), BF)],
        name="attend_forward",
        compiler_params=pltpu.CompilerParams(vmem_limit_bytes=VL),
        cost_estimate=pl.CostEstimate(flops=17_000_000 * 1000, bytes_accessed=12_000_000, transcendentals=0),
    )(x, eq, ek, par, wi, wi, wi, par, par, wo)


def gelu_parts(u):
    a=jnp.abs(u)
    t=1.0/(a*(0.3275911*0.7071067811865476)+1.0)
    e=jnp.exp(u*u*-0.5)
    w=((((0.5*1.061405429*t-0.5*1.453152027)*t+0.5*1.421413741)*t-0.5*0.284496736)*t+0.5*0.254829592)*t*e
    phi=jnp.where(u>=0,1.0-w,w)
    return u*phi,phi+u*e*0.3989422804014327

def kb_kernel(sb,first,last,rel_ref,nmid_ref,cot_ref,*refs):
    nt_=2*sb
    wu_refs=refs[:nt_]; ub_refs=refs[nt_:2*nt_]; wd_refs=refs[2*nt_:3*nt_]
    down_in,dn_in,down_ref,dn_ref,keep_ref,send_ref,ubg_ref,nmt,cott,tmp=refs[3*nt_:3*nt_+10]
    down_acc=refs[-1] if last else down_ref
    i=pl.program_id(0)
    dp=rel_ref[0]; z=rel_ref[1]
    @pl.when(i==0)
    def _():
        nmt[...]=nmid_ref[...].T
        cott[...]=cot_ref[...].T
        down_acc[...]=down_in[...]
        if first:
            down_acc[...]+=dn_in[DB:DB+1]
            dn_ref[...]=jnp.zeros_like(dn_ref)
        else:
            dn_ref[...]=dn_in[...]
    nm=nmid_ref[...]; cot=cot_ref[...]
    wu=jnp.concatenate([r[...] for r in wu_refs],axis=1)
    wd=jnp.concatenate([r[...] for r in wd_refs],axis=0)
    ub=jnp.concatenate([r[...] for r in ub_refs],axis=1)
    u=nn(nm,wu)+ub
    act,der=gelu_parts(u)
    hid=act.astype(BF)
    gu=(nt(cot,wd)*der).astype(BF)
    down_acc[...]+=nn(hid,wd)
    dn_ref[...]+=nt(gu,wu)
    rows=nm.shape[0]
    ubg_ref[...]=jnp.sum(gu.astype(F32),axis=0,keepdims=True)
    tmp[...]=nn(nmt[...],gu).astype(BF)
    for r in range(8):
        out=(keep_ref,send_ref)[r&1]
        at=(r>>1&1)*2+(r>>2)
        rows_at=pl.ds(pl.multiple_of(lax.bitwise_xor(dp,r)*96,32),96)
        for k in range(sb):
            slot=lax.bitwise_xor(sb*i+k,z)
            for h in range(2):
                lanes=slice(256*k+128*h,256*k+128*h+128)
                out[0,at,slot,96*h:96*h+96,:]=tmp[rows_at,lanes]
    tmp[...]=nn(cott[...],hid).astype(BF)
    for k in range(sb):
        for p in range(2):
            out=(keep_ref,send_ref)[p]
            h=lax.bitwise_xor(dp&1,p)
            at=lax.bitwise_xor(2*(sb*i+k)+h,dp)>>1
            for s in range(4):
                out[1,at,lax.bitwise_xor(z,s)]=tmp[192*s:192*s+192,pl.ds(pl.multiple_of(256*k+128*h,128),128)]

    if last:
        @pl.when(i==pl.num_programs(0)-1)
        def _(): down_ref[...]=down_acc[...].astype(BF)

def kb(j,rel,nmid,cot,wu,ub,wd,down,dn,sb=4):
    first,last=j==0,j==2
    rows,D=nmid.shape
    cst=lambda shape: pl.BlockSpec(shape,lambda i,*_:(0,)*len(shape))
    S=jax.ShapeDtypeStruct
    offs=[6*k+3*h+j for k in range(sb) for h in range(2)]
    col=lambda o,n: pl.BlockSpec((n,128),lambda i,*_:(0,6*sb*i+o))
    row=lambda o: pl.BlockSpec((128,D),lambda i,*_:(6*sb*i+o,0))
    n=len(offs)
    return pl.pallas_call(functools.partial(kb_kernel,sb,first,last),
      grid_spec=pltpu.PrefetchScalarGridSpec(num_scalar_prefetch=1,grid=(4//sb,),
      in_specs=[cst((rows,D)),cst((rows,D))]+[col(o,D) for o in offs]+[col(o,1) for o in offs]+[row(o) for o in offs]+[cst((rows,D)),cst(dn.shape)],
      out_specs=[cst((rows,D)),cst((rows,D)),cst((2,4,4,192,128)),cst((2,4,4,192,128)),pl.BlockSpec((1,256*sb),lambda i,*_:(0,i))],
      scratch_shapes=[pltpu.VMEM((D,rows),BF)]*2+[pltpu.VMEM((D,256*sb),BF)]+([pltpu.VMEM((rows,D),F32)] if last else [])),
      out_shape=[S((rows,D),BF if last else F32),S((rows,D),F32)]+[S((2,4,4,192,128),BF)]*2+[S((1,1024),F32)],
      name="feed_forward",
      cost_estimate=pl.CostEstimate(flops=14_000_000*1000,bytes_accessed=16_000_000,transcendentals=0),
      compiler_params=pltpu.CompilerParams(vmem_limit_bytes=VL),
    )(rel,nmid,cot,*([wu]*n),*([ub]*n),*([wd]*n),down,dn)

def norm_back(dy,g,xh,r):
    dx=dy*g
    return r*(dx-jnp.mean(dx,axis=-1,keepdims=True)-xh*jnp.mean(dx*xh,axis=-1,keepdims=True))

def col(v): return jnp.sum(v,axis=0,keepdims=True)

def kc_kernel(rel_ref,x_ref,cot_ref,res_ref,dn_ref,att_ref,q_ref,k_ref,v_ref,lse_ref,eq_ref,ek_ref,wo_ref,wq_ref,wk_ref,wv_ref,par_ref,
              ing_ref,keep_ref,send_ref,vec_ref, gres,gproj,nint,acc,tmp,dm):
    i=pl.program_id(0)
    dp=rel_ref[0]
    rows=x_ref.shape[0]
    def scatter(c,order,val):
        tmp[...]=val
        for r in range(8):
            xb,yb=r>>1&1,r>>2
            at=jnp.where(order==0,2*xb+yb,2*yb+xb)
            (keep_ref,send_ref)[r&1][c,at]=tmp[pl.ds(pl.multiple_of(lax.bitwise_xor(dp,r)*96,32),96),:]
    @pl.when(i==0)
    def _():
        cot=cot_ref[...].astype(F32)
        dy=dn_ref[...]
        xh,r=norm_parts(res_ref[...])
        g=cot+norm_back(dy,par_ref[G2:G2+1],xh,r)
        gres[...]=g
        gb=g.astype(BF)
        gproj[...]=gb
        vec_ref[4:5]=col(gb.astype(F32))
        vec_ref[5:6]=col(dy*xh)
        vec_ref[6:7]=col(dy)
        vec_ref[7:8]=col(cot)
        scatter(3,0,tn(att_ref[...],gb).astype(BF))
        xh,r=norm_parts(x_ref[...].astype(F32))
        nint[...]=(xh*par_ref[G1:G1+1]+par_ref[B1:B1+1]).astype(BF).T
        acc[...]=jnp.zeros_like(acc)
    da=nt(gproj[...],wo_ref[...]).astype(BF)
    lane=lax.broadcasted_iota(jnp.int32,(rows,128),1)
    ek=ek_ref[...]
    for pair in range(2):
        cols=slice(128*pair,128*pair+128)
        qp=q_ref[:,cols]*jnp.asarray(0.125,BF); kp=k_ref[:,cols]
        zero=jnp.zeros_like(qp)
        qm=jnp.concatenate([jnp.where(lane<64,qp,zero),jnp.where(lane<64,zero,qp)],axis=0)
        ext=[]
        for h in range(2):
            l=lse_ref[:,2*pair+h:2*pair+h+1]
            hi=l.astype(BF); l=l-hi.astype(F32)
            mid=l.astype(BF); lo=(l-mid.astype(F32)).astype(BF)
            ext.append(jnp.where(lane==5,-hi,jnp.where(lane==6,-mid,jnp.where(lane==7,-lo,eq_ref[...]))))
        st=nt(jnp.concatenate([kp,ek],axis=1),jnp.concatenate([qm,jnp.concatenate(ext,axis=0)],axis=1))
        p=jnp.exp(st)
        dap=da[:,cols]
        dob=jnp.concatenate([jnp.where(lane<64,dap,zero),jnp.where(lane<64,zero,dap)],axis=0)
        dpt=nt(v_ref[:,cols],dob)
        dv=nn(p.astype(BF),dob)
        inner=jnp.sum(p*dpt,axis=0,keepdims=True)
        ds=(p*(dpt-inner)).astype(BF)
        dk=nn(ds,qm)
        dq=tn(ds,kp)*0.125
        dm[:,128*pair:128*pair+128]=jnp.where(lane<64,dq[:rows],dq[rows:]).astype(BF)
        dm[:,256+128*pair:256+128*pair+128]=dk.astype(BF)
        dm[:,512+128*pair:512+128*pair+128]=dv.astype(BF)
    w=jnp.concatenate([wq_ref[...],wk_ref[...],wv_ref[...]],axis=1)
    acc[...]+=nt(dm[...],w)
    at=pl.ds(pl.multiple_of(256*i,256),256)
    vec_ref[2:3,at]=col(dm[:,0:256].astype(F32))
    vec_ref[3:4,at]=col(dm[:,512:768].astype(F32))
    scatter(i,jnp.minimum(i,1),nn(nint[...],dm[...]).astype(BF))
    @pl.when(i==pl.num_programs(0)-1)
    def _():
        xh,r=norm_parts(x_ref[...].astype(F32))
        dy=acc[...]
        vec_ref[0:1]=col(dy*xh)
        vec_ref[1:2]=col(dy)
        ing_ref[...]=(gres[...]+norm_back(dy,par_ref[G1:G1+1],xh,r)).astype(BF)

def kc(rel,x,cot,res,dn,att,q,k,v,lse,eq,ek,wo,wi,par):
    rows,D=x.shape
    cst=lambda shape: pl.BlockSpec(shape,lambda i,*_:(0,)*len(shape))
    S=jax.ShapeDtypeStruct
    blk=pl.BlockSpec((rows,256),lambda i,*_:(0,i))
    wcol=lambda j: pl.BlockSpec((D,256),lambda i,*_:(0,3*j+i))
    return pl.pallas_call(kc_kernel,
      grid_spec=pltpu.PrefetchScalarGridSpec(num_scalar_prefetch=1,grid=(3,),
      in_specs=[cst((rows,D))]*5+[blk]*3+[pl.BlockSpec((rows,128),lambda i,*_:(0,i)),cst((rows,128)),cst((rows,128)),
        pl.BlockSpec((256,D),lambda i,*_:(i,0)),wcol(0),wcol(1),wcol(2),cst((8,D))],
      out_specs=[cst((rows,D)),cst((4,4,96,D)),cst((4,4,96,D)),cst((8,D))],
      scratch_shapes=[pltpu.VMEM((rows,D),F32),pltpu.VMEM((rows,D),BF),pltpu.VMEM((D,rows),BF),pltpu.VMEM((rows,D),F32),pltpu.VMEM((D,D),BF),pltpu.VMEM((rows,D),BF)]),
      out_shape=[S((rows,D),BF),S((4,4,96,D),BF),S((4,4,96,D),BF),S((8,D),F32)],
      name="attend_backward",
      cost_estimate=pl.CostEstimate(flops=30_000_000*1000,bytes_accessed=16_000_000,transcendentals=0),
      compiler_params=pltpu.CompilerParams(vmem_limit_bytes=VL),
    )(rel,x,cot,res,dn,att,q,k,v,lse,eq,ek,wo,wi,wi,wi,par)


def on_device(n_dp, n_seq, patches, segments, first_gain, first_bias, input_weight, query_bias, value_bias, output_weight,
              output_bias, second_gain, second_bias, up_weight, up_bias, down_weight, down_bias, cotangent):
    strips, length, D = patches.shape
    dp, z = lax.axis_index("dp"), lax.axis_index("seq")
    core = dp % 2
    stride = n_dp // 8
    both = ("dp", "seq")

    def owned(at_z, at_core):
        k = at_z - at_core
        return k, (0 <= k) & (k < strips)

    def outward(d):
        pairs = []
        for g in range(n_dp):
            for a in range(n_seq):
                b = (a + d) % n_seq
                if owned(b, g % 2)[1]:
                    pairs.append((g * n_seq + a, g * n_seq + b))
        return pairs

    def homeward(d):
        return [(b, a) for a, b in outward(d)]

    def pick(array, d):
        k, fine = owned((z + d) % n_seq, core)
        part = lax.dynamic_index_in_dim(array, jnp.clip(k, 0, strips - 1), 0, keepdims=False)
        return jnp.where(fine, part, jnp.zeros_like(part)) if d == 0 else part

    def gather(array):
        return [pick(array, 0)] + [lax.ppermute(pick(array, d), both, outward(d)) for d in range(1, n_seq)]

    def home(array):
        parts = array.reshape(n_seq, PART, D)
        got = [parts[0]] + [lax.ppermute(parts[d], both, homeward(d)) for d in range(1, n_seq)]
        rows = []
        for k in range(strips):
            at = (k + core - z) % n_seq
            row = got[0]
            for d in range(1, n_seq):
                row = jnp.where(at == d, got[d], row)
            rows.append(row[:length])
        return jnp.stack(rows)

    pad = lambda a: jnp.pad(a, ((0, 0), (0, PART - length), (0, 0)))
    ids = jnp.pad(segments, ((0, 0), (0, PART - length)), constant_values=4).astype(BF)
    ids = jnp.broadcast_to(ids[:, :, None], (strips, PART, 128))
    ids = jnp.concatenate(gather(ids), axis=0)
    lane = lax.broadcasted_iota(jnp.int32, ids.shape, 1)
    same = ids == lane.astype(BF)
    eq = jnp.where(same | (lane >= 5), 0.0, -1e30).astype(BF)
    ek = jnp.where((same & (lane < 5)) | ((lane >= 5) & (lane < 8)), 1.0, 0.0).astype(BF)
    par = jnp.stack([first_gain, first_bias, query_bias, value_bias, output_bias, second_gain, second_bias, down_bias]).astype(F32)
    ub = up_bias.astype(F32).reshape(1, -1)
    x = jnp.concatenate(gather(pad(patches)), axis=0)
    later, _ = lax.optimization_barrier((cotangent, x))
    cot = jnp.concatenate(gather(pad(later)), axis=0)
    rel = jnp.stack([dp // stride, z]).astype(jnp.int32)

    q, k, v, att, lse, nmid, res = ka(x, eq, ek, par, input_weight, output_weight)

    def swap(value, bit):
        return lax.ppermute(value, "dp", [(i, i ^ (stride << bit)) for i in range(n_dp)])

    def add(a, b):
        return (a.astype(F32) + b.astype(F32)).astype(BF)

    def halve(keep, got, bits):
        for n, bit in zip((2, 1), bits):
            sent = add(keep[n:], got[n:])
            kept = add(keep[:n], got[:n])
            keep, got = kept, swap(sent, bit)
        return keep[0].astype(F32) + got[0].astype(F32)

    downs, grads_back = res, par
    ub_grads, ups_parts, downs_parts = [], [], []

    def over_seq(value):
        value_bf = value.astype(BF)
        total = value[0]
        for s in range(1, n_seq):
            total += lax.ppermute(value_bf[s], "seq", [(i, i ^ s) for i in range(n_seq)]).astype(F32)
        return total

    for j in range(3):
        downs, grads_back, keep, send, ubg = kb(j, rel, nmid, cot, up_weight, ub, down_weight, downs, grads_back)
        got = swap(send, 0)
        ups_parts.append(over_seq(halve(keep[0], got[0], (1, 2))))
        downs_parts.append(over_seq(halve(keep[1], got[1], (2, 1))))
        ub_grads.append(ubg)
    block_output = home(downs)
    up_grad = jnp.stack([u.reshape(2, 96, 128) for u in ups_parts])
    up_grad = up_grad.transpose(2, 1, 0, 3).reshape(96, 768)
    down_grad = jnp.stack(downs_parts)
    down_grad = down_grad.transpose(0, 2, 1).reshape(384, 192)
    ub_grad = jnp.stack(ub_grads).reshape(3, 8, 128).transpose(1, 0, 2).reshape(4, D)

    ing, keep, send, vec = kc(rel, x, cot, res, grads_back, att, q, k, v, lse, eq, ek, output_weight, input_weight, par)
    input_grad = home(ing).astype(F32)
    got = swap(send, 0)
    chunk = [halve(keep[c], got[c], (1, 2) if c in (0, 3) else (2, 1)).astype(BF) for c in range(4)]
    in_rows = jnp.concatenate([chunk[i][:, 256 * j:256 * j + 256] for j in range(3) for i in range(3)], axis=1)

    def columns_over_seq(rows):
        width = rows.shape[1] // n_seq
        cut = lambda s: lax.dynamic_slice_in_dim(rows, (z ^ s) * width, width, 1)
        total = cut(0).astype(F32)
        for s in range(1, n_seq):
            total += lax.ppermute(cut(s), "seq", [(i, i ^ s) for i in range(n_seq)]).astype(F32)
        return total

    in_grad = columns_over_seq(in_rows)
    out_grad = columns_over_seq(chunk[3])

    vec = jnp.concatenate([vec, ub_grad], axis=0)
    bit = 1
    while bit < n_dp:
        vec += lax.ppermute(vec, "dp", [(i, i ^ bit) for i in range(n_dp)])
        bit *= 2
    bit = 1
    while bit < n_seq:
        vec += lax.ppermute(vec, "seq", [(i, i ^ bit) for i in range(n_seq)])
        bit *= 2

    weights = [in_grad, out_grad, up_grad, down_grad]
    if stride > 1:
        groups = [[g * stride + t for t in range(stride)] for g in range(8)]
        weights = [lax.psum_scatter(w, "dp", scatter_dimension=0, axis_index_groups=groups, tiled=True) for w in weights]
    in_grad, out_grad, up_grad, down_grad = weights
    return (block_output, input_grad, vec[0], vec[1], in_grad, vec[2], vec[3], out_grad, vec[4], vec[5], vec[6], up_grad,
            vec[8:12].reshape(-1), down_grad, vec[7])


def solution(mesh):
    rep = P()
    rows = P("dp", "seq", None)
    cut = P("dp", "seq")
    return jax.shard_map(
        functools.partial(on_device, mesh.shape["dp"], mesh.shape["seq"]),
        mesh=mesh,
        in_specs=(rows, cut) + (rep,) * 13 + (rows,),
        out_specs=(rows, rows, rep, rep, cut, rep, rep, cut, rep, rep, rep, cut, rep, cut, rep),
        check_vma=False,
    )
```

```python
import functools

import jax
import jax.numpy as jnp
from jax import lax
from jax.experimental import pallas as pl
from jax.experimental.pallas import tpu as pltpu
from jax.sharding import PartitionSpec as P

F32 = jnp.float32
BF = jnp.bfloat16
EPS = 1e-6
VL = 60 << 20
PART = 136
SENT = 144
MESH = pl.DeviceIdType.MESH

def nn(a,b): return lax.dot_general(a,b,(((1,),(0,)),((),())),preferred_element_type=F32)
def nt(a,b): return lax.dot_general(a,b,(((1,),(1,)),((),())),preferred_element_type=F32)
def tn(a,b): return lax.dot_general(a,b,(((0,),(0,)),((),())),preferred_element_type=F32)

def norm_parts(v):
    mid=jnp.mean(v,axis=-1,keepdims=True)
    c=v-mid
    r=lax.rsqrt(jnp.mean(c*c,axis=-1,keepdims=True)+EPS)
    return c*r,r

G1, B1, QB, VB, OB, G2, B2, DB = range(8)


def ka_kernel(x_ref, eq_ref, ek_ref, par_ref, wq_ref, wk_ref, wv_ref, qb_ref, vb_ref, wo_ref,
              q_out, k_out, v_out, att_out, lse_out, nmid_out, res_out, acc, nin_ref):
    i = pl.program_id(0)
    rows = x_ref.shape[0]

    @pl.when(i == 0)
    def _():
        xh, _r = norm_parts(x_ref[...].astype(F32))
        nin_ref[...] = (xh * par_ref[G1:G1 + 1] + par_ref[B1:B1 + 1]).astype(BF)
        acc[...] = jnp.zeros_like(acc)

    nin = nin_ref[...]
    q_out[...] = (nn(nin, wq_ref[...]) + qb_ref[QB:QB + 1]).astype(BF)
    k_out[...] = nn(nin, wk_ref[...]).astype(BF)
    v_out[...] = (nn(nin, wv_ref[...]) + vb_ref[VB:VB + 1]).astype(BF)
    lane = lax.broadcasted_iota(jnp.int32, (rows, 128), 1)
    eq = eq_ref[...]
    ek = ek_ref[...]
    for pair in range(2):
        cols = slice(128 * pair, 128 * pair + 128)
        qp = q_out[:, cols] * jnp.asarray(0.125, BF)
        kp = jnp.concatenate([k_out[:, cols], ek], axis=1)
        vp = v_out[:, cols]
        zero = jnp.zeros_like(qp)
        both = jnp.concatenate([jnp.concatenate([jnp.where(lane < 64, qp, zero), eq], axis=1),
                                jnp.concatenate([jnp.where(lane < 64, zero, qp), eq], axis=1)], axis=0)
        s = nt(both, kp)
        m = jnp.max(s, axis=-1, keepdims=True)
        e = jnp.exp(s - m)
        t = jnp.sum(e, axis=-1, keepdims=True)
        p = (e * (1.0 / t)).astype(BF)
        o = nn(p, vp)
        log = m + jnp.log(t)
        lse_out[:, 2 * pair:2 * pair + 1] = log[:rows]
        lse_out[:, 2 * pair + 1:2 * pair + 2] = log[rows:]
        att_out[:, cols] = jnp.where(lane < 64, o[:rows], o[rows:]).astype(BF)
    acc[...] += nn(att_out[...], wo_ref[...])

    @pl.when(i == pl.num_programs(0) - 1)
    def _():
        res = x_ref[...].astype(F32) + acc[...] + par_ref[OB:OB + 1]
        res_out[...] = res
        xh, _r = norm_parts(res)
        nmid_out[...] = (xh * par_ref[G2:G2 + 1] + par_ref[B2:B2 + 1]).astype(BF)


def ka(x, eq, ek, par, wi, wo):
    rows, D = x.shape
    full = lambda a: pl.BlockSpec(a.shape, lambda i: (0,) * a.ndim)
    n = 3
    blk = pl.BlockSpec((rows, 256), lambda i: (0, i))
    whole = pl.BlockSpec((rows, D), lambda i: (0, 0))
    S = jax.ShapeDtypeStruct
    wcol = lambda j: pl.BlockSpec((D, 256), lambda i: (0, n * j + i))
    pcol = pl.BlockSpec((8, 256), lambda i: (0, i))
    return pl.pallas_call(
        ka_kernel, grid=(n,),
        in_specs=[full(x), full(eq), full(ek), full(par), wcol(0), wcol(1), wcol(2), pcol, pcol,
                  pl.BlockSpec((256, D), lambda i: (i, 0))],
        out_specs=[blk, blk, blk, blk, pl.BlockSpec((rows, 128), lambda i: (0, i)), whole, whole],
        out_shape=[S((rows, D), BF)] * 4 + [S((rows, 384), F32), S((rows, D), BF), S((rows, D), F32)],
        scratch_shapes=[pltpu.VMEM((rows, D), F32), pltpu.VMEM((rows, D), BF)],
        name="attend_forward",
        compiler_params=pltpu.CompilerParams(vmem_limit_bytes=VL),
        cost_estimate=pl.CostEstimate(flops=17_000_000 * 1000, bytes_accessed=12_000_000, transcendentals=0),
    )(x, eq, ek, par, wi, wi, wi, par, par, wo)


def gelu_parts(u):
    a=jnp.abs(u)
    t=1.0/(a*(0.3275911*0.7071067811865476)+1.0)
    e=jnp.exp(u*u*-0.5)
    w=((((0.5*1.061405429*t-0.5*1.453152027)*t+0.5*1.421413741)*t-0.5*0.284496736)*t+0.5*0.254829592)*t*e
    phi=jnp.where(u>=0,1.0-w,w)
    return u*phi,phi+u*e*0.3989422804014327

def kb_kernel(sb,first,last,rel_ref,nmid_ref,cot_ref,*refs):
    nt_=2*sb
    wu_refs=refs[:nt_]; ub_refs=refs[nt_:2*nt_]; wd_refs=refs[2*nt_:3*nt_]
    down_in,dn_in,down_ref,dn_ref,keep_ref,send_ref,ubg_ref,nmt,cott,tmp=refs[3*nt_:3*nt_+10]
    down_acc=refs[-1] if last else down_ref
    i=pl.program_id(0)
    dp=rel_ref[0]; z=rel_ref[1]
    @pl.when(i==0)
    def _():
        nmt[...]=nmid_ref[...].T
        cott[...]=cot_ref[...].T
        down_acc[...]=down_in[...]
        if first:
            down_acc[...]+=dn_in[DB:DB+1]
            dn_ref[...]=jnp.zeros_like(dn_ref)
        else:
            dn_ref[...]=dn_in[...]
    nm=nmid_ref[...]; cot=cot_ref[...]
    wu=jnp.concatenate([r[...] for r in wu_refs],axis=1)
    wd=jnp.concatenate([r[...] for r in wd_refs],axis=0)
    ub=jnp.concatenate([r[...] for r in ub_refs],axis=1)
    u=nn(nm,wu)+ub
    act,der=gelu_parts(u)
    hid=act.astype(BF)
    gu=(nt(cot,wd)*der).astype(BF)
    down_acc[...]+=nn(hid,wd)
    dn_ref[...]+=nt(gu,wu)
    rows=nm.shape[0]
    ubg_ref[...]=jnp.sum(gu.astype(F32),axis=0,keepdims=True)
    tmp[...]=nn(nmt[...],gu).astype(BF)
    for r in range(8):
        out=(keep_ref,send_ref)[r&1]
        at=(r>>1&1)*2+(r>>2)
        rows_at=pl.ds(pl.multiple_of(lax.bitwise_xor(dp,r)*96,32),96)
        for k in range(sb):
            slot=lax.bitwise_xor(sb*i+k,z)*192
            for h in range(2):
                lanes=slice(256*k+128*h,256*k+128*h+128)
                out[0,at,pl.ds(pl.multiple_of(slot+96*h,32),96),:]=tmp[rows_at,lanes]
    tmp[...]=nn(cott[...],hid).astype(BF)
    for k in range(sb):
        for p in range(2):
            out=(keep_ref,send_ref)[p]
            h=lax.bitwise_xor(dp&1,p)
            at=lax.bitwise_xor(2*(sb*i+k)+h,dp)>>1
            for s in range(4):
                out[1,at,pl.ds(pl.multiple_of(lax.bitwise_xor(z,s)*192,64),192),:]=tmp[192*s:192*s+192,pl.ds(pl.multiple_of(256*k+128*h,128),128)]

    if last:
        @pl.when(i==pl.num_programs(0)-1)
        def _():
            for d in range(4): down_ref[d,0:PART]=down_acc[PART*d:PART*d+PART].astype(BF)

def kb(j,rel,nmid,cot,wu,ub,wd,down,dn,sb=4):
    first,last=j==0,j==2
    rows,D=nmid.shape
    cst=lambda shape: pl.BlockSpec(shape,lambda i,*_:(0,)*len(shape))
    S=jax.ShapeDtypeStruct
    offs=[6*k+3*h+j for k in range(sb) for h in range(2)]
    col=lambda o,n: pl.BlockSpec((n,128),lambda i,*_:(0,6*sb*i+o))
    row=lambda o: pl.BlockSpec((128,D),lambda i,*_:(6*sb*i+o,0))
    n=len(offs)
    return pl.pallas_call(functools.partial(kb_kernel,sb,first,last),
      grid_spec=pltpu.PrefetchScalarGridSpec(num_scalar_prefetch=1,grid=(4//sb,),
      in_specs=[cst((rows,D)),cst((rows,D))]+[col(o,D) for o in offs]+[col(o,1) for o in offs]+[row(o) for o in offs]+[cst((rows,D)),cst(dn.shape)],
      out_specs=[cst((4,SENT,D)) if last else cst((rows,D)),cst((rows,D)),cst((2,4,768,128)),cst((2,4,768,128)),pl.BlockSpec((1,256*sb),lambda i,*_:(0,i))],
      scratch_shapes=[pltpu.VMEM((D,rows),BF)]*2+[pltpu.VMEM((D,256*sb),BF)]+([pltpu.VMEM((rows,D),F32)] if last else [])),
      out_shape=[S((4,SENT,D),BF) if last else S((rows,D),F32),S((rows,D),F32)]+[S((2,4,768,128),BF)]*2+[S((1,1024),F32)],
      name="feed_forward",
      cost_estimate=pl.CostEstimate(flops=14_000_000*1000,bytes_accessed=16_000_000,transcendentals=0),
      compiler_params=pltpu.CompilerParams(vmem_limit_bytes=VL),
    )(rel,nmid,cot,*([wu]*n),*([ub]*n),*([wd]*n),down,dn)

def norm_back(dy,g,xh,r):
    dx=dy*g
    return r*(dx-jnp.mean(dx,axis=-1,keepdims=True)-xh*jnp.mean(dx*xh,axis=-1,keepdims=True))

def col(v): return jnp.sum(v,axis=0,keepdims=True)


def xor(a, b):
    return lax.bitwise_xor(a, b)


def kc_kernel(stride,
              x_hbm, cot_hbm, res_hbm, dn_hbm, att_hbm, q_hbm, k_hbm, v_hbm, lse_hbm, eq_hbm, ek_hbm, wo_hbm, wi_hbm, par_ref,
              ub0, ub1, ub2, bo_hbm, kept0, kept1, kept2, sent0, sent1, sent2,
              bo_home, ing_home, mlp_out, io_out, vec_out,
              x_ref, cot_ref, gres, acc, att_ref, q_ref, k_ref, v_ref, lse_ref, eq_ref, ek_ref, wo_ref, wi_ref,
              gproj, nint, dm, tmp, ing,
              mk, mc, m1, m2, mz, ik, isnd, ic, i1, i2, izs, iz, vs, vr,
              load_sem, core_s, core_r, a_s, a_r, b_s, b_r, z_s, z_r, v_s, v_r, h_s, h_r):
    dp, z = lax.axis_index("dp"), lax.axis_index("seq")
    inner = dp // stride
    core = lax.rem(dp, 2)
    mine = z - core
    owner = (mine >= 0) & (mine < 3)
    slot = jnp.clip(mine, 0, 2)
    peers = [{"dp": xor(dp, stride << b)} for b in range(3)]
    along = [{"seq": xor(z, s)} for s in range(4)]

    barrier = pltpu.get_barrier_semaphore()
    for peer in peers + along[1:]:
        pl.semaphore_signal(barrier, inc=1, device_id=peer, device_id_type=MESH)
    pl.semaphore_wait(barrier, 6)

    def remote(src, dst, ssem, rsem, device):
        return pltpu.make_async_remote_copy(src_ref=src, dst_ref=dst, send_sem=ssem, recv_sem=rsem,
                                            device_id=device, device_id_type=MESH)

    loads = {}

    def load(name, src, dst):
        c = pltpu.make_async_copy(src, dst, load_sem.at[len(loads)])
        c.start()
        loads[name] = c

    sends = []

    def start(c):
        c.start()
        sends.append(c)
        return c

    pairs = [dict(keep=mk.at[j], got=mc.at[j], one=m1.at[j], two=m2.at[j], n=j) for j in range(3)]
    pairs += [dict(keep=ik.at[c], got=ic.at[c], one=i1.at[c], two=i2.at[c], n=3 + c) for c in range(4)]

    def add(dst, src, n):
        @pl.loop(0, 2 * n)
        def _(t):
            u, a = t // n, lax.rem(t, n)
            dst[u, a] = (dst[u, a].astype(F32) + src[u, a].astype(F32)).astype(BF)

    def core_start(p, src):
        p["c"] = start(remote(src, p["got"], core_s.at[p["n"]], core_r.at[p["n"]], peers[0]))

    def core_done(p):
        p["c"].wait_recv()
        add(p["keep"], p["got"], 4)
        n = p["n"]
        p["a"] = [start(remote(p["keep"].at[u, pl.ds(2, 2)], p["one"].at[u], a_s.at[2 * n + u], a_r.at[2 * n + u], peers[1 + u]))
                  for u in range(2)]

    def one_done(p):
        for c in p["a"]:
            c.wait_recv()
        add(p["keep"], p["one"], 2)
        n = p["n"]
        p["b"] = [start(remote(p["keep"].at[u, pl.ds(1, 1)], p["two"].at[u], b_s.at[2 * n + u], b_r.at[2 * n + u], peers[2 - u]))
                  for u in range(2)]

    def two_done(p):
        for c in p["b"]:
            c.wait_recv()
        add(p["keep"], p["two"], 1)

    def mlp_z(j):
        p = pairs[j]
        two_done(p)
        p["z"] = [start(remote(mk.at[j, :, 0, pl.ds(192 * s, 192)], mz.at[j, s - 1], z_s.at[3 * j + s - 1], z_r.at[3 * j + s - 1],
                               along[s])) for s in range(1, 4)]

    def mlp_end(j):
        p = pairs[j]
        for c in p["z"]:
            c.wait_recv()
        for u in range(2):
            total = mk[j, u, 0, 0:192].astype(F32)
            for s in range(3):
                total += mz[j, s, u].astype(F32)
            mlp_out[j, u] = total

    load("dn", dn_hbm, acc)
    load("res", res_hbm, gres)
    load("cot", cot_hbm, cot_ref)
    load("att", att_hbm, att_ref)
    load("wo", wo_hbm, wo_ref)
    load("x", x_hbm, x_ref)
    core_start(pairs[0], sent0)
    load("q", q_hbm, q_ref)
    load("k", k_hbm, k_ref)
    load("v", v_hbm, v_ref)
    load("lse", lse_hbm, lse_ref)
    load("eq", eq_hbm, eq_ref)
    load("ek", ek_hbm, ek_ref)
    load("keep0", kept0, mk.at[0])
    core_start(pairs[1], sent1)
    load("wi", wi_hbm, wi_ref)
    load("keep1", kept1, mk.at[1])
    core_start(pairs[2], sent2)
    load("keep2", kept2, mk.at[2])

    def homeward(which, src, dst):
        def parts(d):
            at = lax.rem(z - d + 4, 4)
            return remote(src.at[d], dst.at[slot], h_s.at[4 * which + d], h_r.at[3 * which + slot], {"seq": at})

        own = pltpu.make_async_copy(src.at[0], dst.at[slot], h_s.at[4 * which])

        @pl.when(owner)
        def _():
            for d in range(1, 4):
                parts(d).start()
            own.start()

        def finish():
            @pl.when(owner)
            def _():
                for d in range(1, 4):
                    parts(d).wait_send()
                own.wait()

            for k in range(3):
                @pl.when(k + core != z)
                def _():
                    remote(src.at[0], dst.at[k], h_s.at[4 * which], h_r.at[3 * which + k], {"seq": xor(z, 1)}).wait_recv()
        return finish

    bo_end = homeward(0, bo_hbm, bo_home)

    def scatter(c, val):
        tmp[...] = val
        for r in range(8):
            xb, yb = r >> 1 & 1, r >> 2
            rows_at = pl.ds(pl.multiple_of(xor(inner, r) * 96, 32), 96)
            out = (ik, isnd)[r & 1]
            out[c, 0, 2 * xb + yb] = tmp[rows_at, 0:384]
            out[c, 1, 2 * yb + xb] = tmp[rows_at, 384:768]
        core_start(pairs[3 + c], isnd.at[c])

    for name in ("dn", "res", "cot"):
        loads[name].wait()
    cot = cot_ref[...].astype(F32)
    dy = acc[...]
    xh, r = norm_parts(gres[...])
    g = cot + norm_back(dy, par_ref[G2:G2 + 1], xh, r)
    gres[...] = g
    gb = g.astype(BF)
    gproj[...] = gb
    vec = vs.at[0]
    vec[12:16] = jnp.zeros((4, 768), F32)
    vec[4:5] = col(gb.astype(F32))
    vec[5:6] = col(dy * xh)
    vec[6:7] = col(dy)
    vec[7:8] = col(cot)
    for j, ub in enumerate((ub0, ub1, ub2)):
        for b in range(8):
            t = 3 * b + j
            vec[8 + t // 6:9 + t // 6, 128 * (t % 6):128 * (t % 6) + 128] = ub[0:1, 128 * b:128 * b + 128]
    for name in ("att", "wo", "x"):
        loads[name].wait()
    scatter(3, tn(att_ref[...], gproj[...]).astype(BF))
    xh, r = norm_parts(x_ref[...].astype(F32))
    nint[...] = (xh * par_ref[G1:G1 + 1] + par_ref[B1:B1 + 1]).astype(BF).T
    for name in ("q", "k", "v", "lse", "eq", "ek", "keep0"):
        loads[name].wait()
    core_done(pairs[0])
    rows = x_ref.shape[0]
    lane = lax.broadcasted_iota(jnp.int32, (rows, 128), 1)

    def pair_back(i, pair, da):
        cols = slice(256 * i + 128 * pair, 256 * i + 128 * pair + 128)
        qp = q_ref[:, cols] * jnp.asarray(0.125, BF)
        kp = k_ref[:, cols]
        zero = jnp.zeros_like(qp)
        qm = jnp.concatenate([jnp.where(lane < 64, qp, zero), jnp.where(lane < 64, zero, qp)], axis=0)
        ext = []
        for h in range(2):
            at = 128 * i + 2 * pair + h
            l = lse_ref[:, at:at + 1]
            hi = l.astype(BF)
            l = l - hi.astype(F32)
            mid = l.astype(BF)
            lo = (l - mid.astype(F32)).astype(BF)
            ext.append(jnp.where(lane == 5, -hi, jnp.where(lane == 6, -mid, jnp.where(lane == 7, -lo, eq_ref[...]))))
        st = nt(jnp.concatenate([kp, ek_ref[...]], axis=1), jnp.concatenate([qm, jnp.concatenate(ext, axis=0)], axis=1))
        p = jnp.exp(st)
        dap = da[:, 128 * pair:128 * pair + 128]
        dob = jnp.concatenate([jnp.where(lane < 64, dap, zero), jnp.where(lane < 64, zero, dap)], axis=0)
        dpt = nt(v_ref[:, cols], dob)
        dv = nn(p.astype(BF), dob)
        inside = jnp.sum(p * dpt, axis=0, keepdims=True)
        ds = (p * (dpt - inside)).astype(BF)
        dk = nn(ds, qm)
        dq = tn(ds, kp) * 0.125
        at = 128 * pair
        dm[:, at:at + 128] = jnp.where(lane < 64, dq[:rows], dq[rows:]).astype(BF)
        dm[:, 256 + at:256 + at + 128] = dk.astype(BF)
        dm[:, 512 + at:512 + at + 128] = dv.astype(BF)

    polls = {(0, 0): lambda: (loads["keep1"].wait(), loads["keep2"].wait(), core_done(pairs[1])),
             (0, 1): lambda: (core_done(pairs[2]), core_done(pairs[6])),
             (1, 0): lambda: (one_done(pairs[0]),),
             (1, 1): lambda: (core_done(pairs[3]), one_done(pairs[1])),
             (2, 0): lambda: (mlp_z(0), one_done(pairs[6])),
             (2, 1): lambda: (core_done(pairs[4]), one_done(pairs[2]), mlp_z(1))}
    for i in range(3):
        da = nt(gproj[...], wo_ref[256 * i:256 * i + 256]).astype(BF)
        for pair in range(2):
            pair_back(i, pair, da)
            polls[i, pair]()
        if i == 0:
            loads["wi"].wait()
        w = jnp.concatenate([wi_ref[:, 768 * j + 256 * i:768 * j + 256 * i + 256] for j in range(3)], axis=1)
        part = nt(dm[...], w)
        acc[...] = part if i == 0 else acc[...] + part
        vec[2:3, 256 * i:256 * i + 256] = col(dm[:, 0:256].astype(F32))
        vec[3:4, 256 * i:256 * i + 256] = col(dm[:, 512:768].astype(F32))
        scatter(i, nn(nint[...], dm[...]).astype(BF))

    xh, r = norm_parts(x_ref[...].astype(F32))
    dy = acc[...]
    vec[0:1] = col(dy * xh)
    vec[1:2] = col(dy)
    vcopies = []

    def vsend(stage):
        if stage < 3:
            c = start(remote(vs.at[stage], vr.at[stage], v_s.at[stage], v_r.at[stage], peers[stage]))
            vcopies.append([c])
        else:
            vcopies.append([start(remote(vs.at[3], vr.at[2 + s], v_s.at[2 + s], v_r.at[2 + s], along[s])) for s in range(1, 4)])

    def vadd(stage):
        for c in vcopies[stage]:
            c.wait_recv()
        if stage < 3:
            vs[stage + 1] = vs[stage] + vr[stage]
            vsend(stage + 1)
        else:
            vec_out[...] = (vs[3] + vr[3]) + (vr[4] + vr[5])

    vsend(0)
    gi = gres[...] + norm_back(dy, par_ref[G1:G1 + 1], xh, r)
    for d in range(4):
        ing[d, 0:PART] = gi[PART * d:PART * d + PART].astype(BF)
    ing_end = homeward(1, ing, ing_home)

    vadd(0)
    core_done(pairs[5])
    one_done(pairs[3])
    mlp_z(2)
    vadd(1)
    two_done(pairs[6])
    one_done(pairs[4])
    two_done(pairs[3])
    mlp_end(0)
    vadd(2)
    one_done(pairs[5])
    two_done(pairs[4])
    mlp_end(1)
    two_done(pairs[5])

    whole = lambda c: jnp.concatenate([ik[c, 0, 0], ik[c, 1, 0]], axis=1).astype(F32)
    w3 = [whole(c) for c in range(3)]
    full = jnp.concatenate([w3[i][:, 256 * j:256 * j + 256] for j in range(3) for i in range(3)], axis=1)
    wo = whole(3)
    half = lax.broadcasted_iota(jnp.int32, (96, 128), 1) < 64
    for b in range(4):
        if b % 2:
            win = pltpu.roll(full[:, 576 * b - 64:576 * b + 576], 640 - 64, 1)
            w = wo[:, 192 * b - 64:192 * b + 192]
        else:
            win = full[:, 576 * b:576 * b + 640]
            w = pltpu.roll(wo[:, 192 * b:192 * b + 256], 64, 1)
        block = jnp.concatenate([win[:, :512], jnp.where(half, win[:, 512:], w[:, :128]), w[:, 128:]], axis=1)
        izs[xor(z, b)] = block.astype(BF)
    last = [start(remote(izs.at[s], iz.at[s - 1], z_s.at[9 + s - 1], z_r.at[9 + s - 1], along[s])) for s in range(1, 4)]
    mlp_end(2)
    vadd(3)
    for c in last:
        c.wait_recv()
    io_out[...] = (izs[0].astype(F32) + iz[0].astype(F32)) + (iz[1].astype(F32) + iz[2].astype(F32))
    ing_end()
    bo_end()
    for c in sends:
        c.wait_send()


def kc(stride, x, cot, res, dn, att, q, k, v, lse, eq, ek, wo, wi, par, ubs, bo, kepts, sents):
    rows, D = x.shape
    S = jax.ShapeDtypeStruct
    V = pltpu.VMEM
    hbm = pl.BlockSpec(memory_space=pl.ANY)
    vm = pl.BlockSpec(memory_space=pltpu.VMEM)
    wide = lambda t=BF: V((rows, D), t)
    dma = pltpu.SemaphoreType.DMA
    return pl.pallas_call(
        functools.partial(kc_kernel, stride),
        in_specs=[hbm] * 13 + [vm] * 4 + [hbm] * 7,
        out_specs=[hbm, hbm, vm, vm, vm],
        out_shape=[S((3, SENT, D), BF), S((3, SENT, D), BF), S((3, 2, 192, 128), F32), S((96, D), F32), S((16, D), F32)],
        scratch_shapes=[wide(), wide(), wide(F32), wide(F32), wide(), wide(), wide(), wide(), V((rows, 384), F32), V((rows, 128), BF),
                        V((rows, 128), BF), V((D, D), BF), V((D, 3 * D), BF),
                        wide(), V((D, rows), BF), wide(), V((D, D), BF), V((4, SENT, D), BF),
                        V((3, 2, 4, 768, 128), BF), V((3, 2, 4, 768, 128), BF), V((3, 2, 2, 768, 128), BF), V((3, 2, 1, 768, 128), BF),
                        V((3, 3, 2, 192, 128), BF),
                        V((4, 2, 4, 96, 384), BF), V((4, 2, 4, 96, 384), BF), V((4, 2, 4, 96, 384), BF), V((4, 2, 2, 96, 384), BF),
                        V((4, 2, 1, 96, 384), BF), V((4, 96, D), BF), V((3, 96, D), BF),
                        V((4, 16, D), F32), V((6, 16, D), F32),
                        dma((16,)), dma((7,)), dma((7,)), dma((14,)), dma((14,)), dma((14,)), dma((14,)), dma((12,)), dma((12,)),
                        dma((6,)), dma((6,)), dma((8,)), dma((6,))],
        name="attend_backward",
        compiler_params=pltpu.CompilerParams(vmem_limit_bytes=VL, collective_id=0, has_side_effects=True),
        cost_estimate=pl.CostEstimate(flops=30_000_000 * 1000, bytes_accessed=16_000_000, transcendentals=0),
    )(x, cot, res, dn, att, q, k, v, lse, eq, ek, wo, wi, par, *ubs, bo, *kepts, *sents)


def on_device(n_dp, n_seq, patches, segments, first_gain, first_bias, input_weight, query_bias, value_bias, output_weight,
              output_bias, second_gain, second_bias, up_weight, up_bias, down_weight, down_bias, cotangent):
    strips, length, D = patches.shape
    dp, z = lax.axis_index("dp"), lax.axis_index("seq")
    core = dp % 2
    stride = n_dp // 8
    both = ("dp", "seq")

    def owned(at_z, at_core):
        k = at_z - at_core
        return k, (0 <= k) & (k < strips)

    def outward(d):
        pairs = []
        for g in range(n_dp):
            for a in range(n_seq):
                b = (a + d) % n_seq
                if owned(b, g % 2)[1]:
                    pairs.append((g * n_seq + a, g * n_seq + b))
        return pairs

    def pick(array, d):
        k, fine = owned((z + d) % n_seq, core)
        part = lax.dynamic_index_in_dim(array, jnp.clip(k, 0, strips - 1), 0, keepdims=False)
        return jnp.where(fine, part, jnp.zeros_like(part)) if d == 0 else part

    def gather(array):
        return [pick(array, 0)] + [lax.ppermute(pick(array, d), both, outward(d)) for d in range(1, n_seq)]

    pad = lambda a: jnp.pad(a, ((0, 0), (0, PART - length), (0, 0)))
    ids = jnp.pad(segments, ((0, 0), (0, PART - length)), constant_values=4).astype(BF)
    ids = jnp.broadcast_to(ids[:, :, None], (strips, PART, 128))
    ids = jnp.concatenate(gather(ids), axis=0)
    lane = lax.broadcasted_iota(jnp.int32, ids.shape, 1)
    same = ids == lane.astype(BF)
    eq = jnp.where(same | (lane >= 5), 0.0, -1e30).astype(BF)
    ek = jnp.where((same & (lane < 5)) | ((lane >= 5) & (lane < 8)), 1.0, 0.0).astype(BF)
    par = jnp.stack([first_gain, first_bias, query_bias, value_bias, output_bias, second_gain, second_bias, down_bias]).astype(F32)
    ub = up_bias.astype(F32).reshape(1, -1)
    x = jnp.concatenate(gather(pad(patches)), axis=0)
    later, _ = lax.optimization_barrier((cotangent, x))
    cot = jnp.concatenate(gather(pad(later)), axis=0)
    rel = jnp.stack([dp // stride, z]).astype(jnp.int32)

    q, k, v, att, lse, nmid, res = ka(x, eq, ek, par, input_weight, output_weight)

    downs, grads_back = res, par
    ubs, kepts, sents = [], [], []
    for j in range(3):
        downs, grads_back, keep, send, ubg = kb(j, rel, nmid, cot, up_weight, ub, down_weight, downs, grads_back)
        ubs.append(ubg)
        kepts.append(keep)
        sents.append(send)
    bo, ing, mlp, io, vec = kc(stride, x, cot, res, grads_back, att, q, k, v, lse, eq, ek, output_weight, input_weight, par,
                               ubs, downs, kepts, sents)
    block_output = bo[:, :length]
    input_grad = ing[:, :length].astype(F32)
    up_grad = mlp[:, 0].reshape(3, 2, 96, 128).transpose(2, 1, 0, 3).reshape(96, 768)
    down_grad = mlp[:, 1].transpose(0, 2, 1).reshape(384, 192)
    in_grad = io[:, :576]
    out_grad = io[:, 576:]
    weights = [in_grad, out_grad, up_grad, down_grad]
    if stride > 1:
        groups = [[g * stride + t for t in range(stride)] for g in range(8)]
        weights = [lax.psum_scatter(w, "dp", scatter_dimension=0, axis_index_groups=groups, tiled=True) for w in weights]
        vec = lax.psum(vec, "dp", axis_index_groups=groups)
    in_grad, out_grad, up_grad, down_grad = weights
    return (block_output, input_grad, vec[0], vec[1], in_grad, vec[2], vec[3], out_grad, vec[4], vec[5], vec[6], up_grad,
            vec[8:12].reshape(-1), down_grad, vec[7])


def solution(mesh):
    rep = P()
    rows = P("dp", "seq", None)
    cut = P("dp", "seq")
    return jax.shard_map(
        functools.partial(on_device, mesh.shape["dp"], mesh.shape["seq"]),
        mesh=mesh,
        in_specs=(rows, cut) + (rep,) * 13 + (rows,),
        out_specs=(rows, rows, rep, rep, cut, rep, rep, cut, rep, rep, rep, cut, rep, cut, rep),
        check_vma=False,
    )
```

```python
import functools

import jax
import jax.numpy as jnp
from jax import lax
from jax.experimental import pallas as pl
from jax.experimental.pallas import tpu as pltpu
from jax.sharding import PartitionSpec as P

F32 = jnp.float32
BF = jnp.bfloat16
EPS = 1e-6
VL = 62 << 20
PART = 136
SENT = 144
MESH = pl.DeviceIdType.MESH
G1, B1, QB, VB, OB, G2, B2, DB = range(8)


def nn(a, b):
    return lax.dot_general(a, b, (((1,), (0,)), ((), ())), preferred_element_type=F32)


def nt(a, b):
    return lax.dot_general(a, b, (((1,), (1,)), ((), ())), preferred_element_type=F32)


def tn(a, b):
    return lax.dot_general(a, b, (((0,), (0,)), ((), ())), preferred_element_type=F32)


def xor(a, b):
    return lax.bitwise_xor(a, b)


def col(v):
    return jnp.sum(v, axis=0, keepdims=True)


def norm_parts(v):
    c = v - jnp.mean(v, axis=-1, keepdims=True)
    r = lax.rsqrt(jnp.mean(c * c, axis=-1, keepdims=True) + EPS)
    return c * r, r


def norm_back(dy, g, xh, r):
    dx = dy * g
    return r * (dx - jnp.mean(dx, axis=-1, keepdims=True) - xh * jnp.mean(dx * xh, axis=-1, keepdims=True))


def gelu_parts(u):
    a = jnp.abs(u)
    t = 1.0 / (a * (0.3275911 * 0.7071067811865476) + 1.0)
    e = jnp.exp(u * u * -0.5)
    w = ((((0.5 * 1.061405429 * t - 0.5 * 1.453152027) * t + 0.5 * 1.421413741) * t - 0.5 * 0.284496736) * t
         + 0.5 * 0.254829592) * t * e
    phi = jnp.where(u >= 0, 1.0 - w, w)
    return u * phi, phi + u * e * 0.3989422804014327


def layer_kernel(stride, xp_hbm, cotp_hbm, wi_hbm, wo_hbm, wu_hbm, wd_hbm, par_ref,
                 bo_home, ing_home, mlp_out, io_out, vec_out,
                 xparts, cotparts, cot_ref, cott, q_ref, k_ref, v_ref, att_ref, lse_ref, eq_ref, ek_ref, res_ref, dn_ref, down_ref,
                 nmid_ref, nmt, tmp, bo, wi_ref, wo_ref, wu_ref, wd_ref,
                 mk, ms, mc, m1, m2, m3, m4, ik, isnd, ic, i1, i2, izs, iz, vs, vr,
                 load_sem, core_s, core_r, a_s, a_r, b_s, b_r, z_s, z_r, v_s, v_r, h_s, h_r, g_s, g_r):
    dp, z = lax.axis_index("dp"), lax.axis_index("seq")
    inner = dp // stride
    core = lax.rem(dp, 2)
    mine = z - core
    owner = (mine >= 0) & (mine < 3)
    slot = jnp.clip(mine, 0, 2)
    peers = [{"dp": xor(dp, stride << b)} for b in range(3)]
    along = [{"seq": xor(z, s)} for s in range(4)]
    rows, D = cot_ref.shape

    barrier = pltpu.get_barrier_semaphore()
    for peer in peers + along[1:]:
        pl.semaphore_signal(barrier, inc=1, device_id=peer, device_id_type=MESH)

    def remote(src, dst, ssem, rsem, device):
        return pltpu.make_async_remote_copy(src_ref=src, dst_ref=dst, send_sem=ssem, recv_sem=rsem,
                                            device_id=device, device_id_type=MESH)

    n_loads = [0]

    def load(src, dst):
        c = pltpu.make_async_copy(src, dst, load_sem.at[n_loads[0]])
        n_loads[0] += 1
        c.start()
        return c

    def load_mlp(j):
        s = j % 2
        return [load(wd_hbm.at[:, j], wd_ref.at[s])] + [
            load(wu_hbm.at[:, pl.ds(128 * (3 * b + j), 128)], wu_ref.at[s, :, pl.ds(128 * b, 128)]) for b in range(8)]

    wi_load, wo_load = load(wi_hbm, wi_ref), load(wo_hbm, wo_ref)
    mlp_loads = [load_mlp(0), load_mlp(1)]

    def outward(which, src, dst):
        def each(fn):
            for d in range(1, 4):
                at = lax.rem(z + d, 4)
                k = at - core

                @pl.when((k >= 0) & (k < 3))
                def _():
                    fn(remote(src.at[jnp.clip(k, 0, 2)], dst.at[d], g_s.at[4 * which + d], g_r.at[4 * which + d], {"seq": at}))

        def own():
            return pltpu.make_async_copy(src.at[slot], dst.at[0], g_s.at[4 * which])

        def arrived():
            @pl.when(owner)
            def _():
                own().wait()
                for d in range(1, 4):
                    remote(src.at[0], dst.at[d], g_s.at[4 * which + d], g_r.at[4 * which + d], {"seq": xor(z, 1)}).wait_recv()

        def begin():
            @pl.when(owner)
            def _():
                own().start()
            each(lambda c: c.start())

        return begin, arrived, lambda: each(lambda c: c.wait_send())

    @pl.when(jnp.logical_not(owner))
    def _():
        xparts[...] = jnp.zeros_like(xparts)
        cotparts[...] = jnp.zeros_like(cotparts)

    pl.semaphore_wait(barrier, 6)
    x_begin, x_arrived, x_sent = outward(0, xp_hbm, xparts)
    c_begin, c_arrived, c_sent = outward(1, cotp_hbm, cotparts)
    x_begin()
    x_sent()
    c_begin()
    x_arrived()

    def joined(parts):
        return jnp.concatenate([parts[d].astype(F32)[:PART] for d in range(4)], axis=0)

    row = lax.broadcasted_iota(jnp.int32, (PART, 128), 0)
    spot = lax.broadcasted_iota(jnp.int32, (PART, 128), 1)
    eqs, eks = [], []
    for d in range(4):
        ids = xparts[d, 128:144, 0:256].astype(F32).T[:PART, 5:6]
        ids = jnp.where(row >= 133, 4.0, ids)
        same = ids == spot.astype(F32)
        eqs.append(jnp.where(same | (spot >= 5), 0.0, -1e30))
        eks.append(jnp.where((same & (spot < 5)) | ((spot >= 5) & (spot < 8)), 1.0, 0.0))
    eq_ref[...] = jnp.concatenate(eqs, axis=0).astype(BF)
    ek_ref[...] = jnp.concatenate(eks, axis=0).astype(BF)

    lane = lax.broadcasted_iota(jnp.int32, (rows, 128), 1)
    x = joined(xparts)
    xh, _r = norm_parts(x)
    nmid_ref[...] = (xh * par_ref[G1:G1 + 1] + par_ref[B1:B1 + 1]).astype(BF)
    res_ref[...] = x + par_ref[OB:OB + 1]
    wi_load.wait()
    wo_load.wait()

    @pl.loop(0, 3)
    def _(i):
        cut = lambda j: pl.ds(pl.multiple_of(768 * j + 256 * i, 256), 256)
        at = cut(0)
        nin = nmid_ref[...]
        q_ref[:, at] = (nn(nin, wi_ref[:, cut(0)]) + par_ref[QB:QB + 1, at]).astype(BF)
        k_ref[:, at] = nn(nin, wi_ref[:, cut(1)]).astype(BF)
        v_ref[:, at] = (nn(nin, wi_ref[:, cut(2)]) + par_ref[VB:VB + 1, at]).astype(BF)
        eq, ek = eq_ref[...], ek_ref[...]
        for pair in range(2):
            cols = pl.ds(pl.multiple_of(256 * i + 128 * pair, 128), 128)
            qp = q_ref[:, cols] * jnp.asarray(0.125, BF)
            kp = jnp.concatenate([k_ref[:, cols], ek], axis=1)
            zero = jnp.zeros_like(qp)
            both = jnp.concatenate([jnp.concatenate([jnp.where(lane < 64, qp, zero), eq], axis=1),
                                    jnp.concatenate([jnp.where(lane < 64, zero, qp), eq], axis=1)], axis=0)
            s = nt(both, kp)
            m = jnp.max(s, axis=-1, keepdims=True)
            e = jnp.exp(s - m)
            t = jnp.sum(e, axis=-1, keepdims=True)
            p = (e * (1.0 / t)).astype(BF)
            o = nn(p, v_ref[:, cols])
            log = m + jnp.log(t)
            lse_ref[i, :, 2 * pair:2 * pair + 1] = log[:rows]
            lse_ref[i, :, 2 * pair + 1:2 * pair + 2] = log[rows:]
            att_ref[:, cols] = jnp.where(lane < 64, o[:rows], o[rows:]).astype(BF)
        res_ref[...] += nn(att_ref[:, at], wo_ref[at, :])

    res = res_ref[...]
    xh, _r = norm_parts(res)
    nmid = (xh * par_ref[G2:G2 + 1] + par_ref[B2:B2 + 1]).astype(BF)
    nmid_ref[...] = nmid
    nmt[...] = nmid.T
    down_ref[...] = res + par_ref[DB:DB + 1]
    c_arrived()
    cot = joined(cotparts).astype(BF)
    cot_ref[...] = cot
    cott[...] = cot.T

    pairs = [dict(keep=mk.at[j], got=mc.at[j], one=m1.at[j], two=m2.at[j], n=j) for j in range(3)]
    pairs += [dict(keep=ik.at[c], got=ic.at[c], one=i1.at[c], two=i2.at[c], n=3 + c) for c in range(4)]
    sends = []

    def start(c):
        c.start()
        sends.append(c)
        return c

    def add(dst, src, n):
        @pl.loop(0, 2 * n)
        def _(t):
            u, a = t // n, lax.rem(t, n)
            dst[u, a] = (dst[u, a].astype(F32) + src[u, a].astype(F32)).astype(BF)

    def core_start(p, src):
        p["c"] = remote(src, p["got"], core_s.at[p["n"]], core_r.at[p["n"]], peers[0])
        p["c"].start()

    def core_done(p):
        p["c"].wait_recv()
        add(p["keep"], p["got"], 4)
        n = p["n"]
        p["a"] = [start(remote(p["keep"].at[u, pl.ds(2, 2)], p["one"].at[u], a_s.at[2 * n + u], a_r.at[2 * n + u], peers[1 + u]))
                  for u in range(2)]

    def one_done(p):
        for c in p["a"]:
            c.wait_recv()
        add(p["keep"], p["one"], 2)
        n = p["n"]
        p["b"] = [start(remote(p["keep"].at[u, pl.ds(1, 1)], p["two"].at[u], b_s.at[2 * n + u], b_r.at[2 * n + u], peers[2 - u]))
                  for u in range(2)]

    def two_done(p):
        for c in p["b"]:
            c.wait_recv()
        add(p["keep"], p["two"], 1)

    def mlp_z1(j):
        p = pairs[j]
        two_done(p)
        p["z"] = start(remote(mk.at[j, :, 0, pl.ds(384, 384)], m3.at[j], z_s.at[2 * j], z_r.at[2 * j], along[1]))

    def mlp_z2(j):
        p = pairs[j]
        p["z"].wait_recv()
        for u in range(2):
            mk[j, u, 0, 0:384] = (mk[j, u, 0, 0:384].astype(F32) + m3[j, u].astype(F32)).astype(BF)
        p["z"] = start(remote(mk.at[j, :, 0, pl.ds(192, 192)], m4.at[j], z_s.at[2 * j + 1], z_r.at[2 * j + 1], along[2]))

    def mlp_end(j):
        pairs[j]["z"].wait_recv()
        for u in range(2):
            mlp_out[j, u] = mk[j, u, 0, 0:192].astype(F32) + m4[j, u].astype(F32)

    def place(s):
        return (s & 1) * 2 + (s >> 1)

    vec = vs.at[0]
    vec[12:16] = jnp.zeros((4, D), F32)

    def hidden_bias(t):
        return par_ref[8 + t // 6:9 + t // 6, 128 * (t % 6):128 * (t % 6) + 128]

    def mlp_step(j, i):
        s = j % 2
        wu = wu_ref[s, :, 512 * i:512 * i + 512]
        wd = wd_ref[s, 4 * i:4 * i + 4].reshape(512, D)
        ub = jnp.concatenate([hidden_bias(3 * b + j) for b in range(4 * i, 4 * i + 4)], axis=1)
        act, der = gelu_parts(nn(nmid_ref[...], wu) + ub)
        hid = act.astype(BF)
        gu = (nt(cot_ref[...], wd) * der).astype(BF)
        down_ref[...] += nn(hid, wd)
        part = nt(gu, wu)
        dn_ref[...] = part if j == 0 and i == 0 else dn_ref[...] + part
        sums = col(gu.astype(F32))
        for b in range(4):
            t = 3 * (4 * i + b) + j
            vec[8 + t // 6:9 + t // 6, 128 * (t % 6):128 * (t % 6) + 128] = sums[:, 128 * b:128 * b + 128]
        if i == 0 and j > 0:
            pairs[j - 1]["c"].wait_send()
        tmp[...] = nn(nmt[...], gu).astype(BF)
        for r in range(8):
            out = mk.at[j] if r % 2 == 0 else ms
            at = (r >> 1 & 1) * 2 + (r >> 2)
            rows_at = pl.ds(pl.multiple_of(xor(inner, r) * 96, 32), 96)
            for k in range(2):
                to = place(xor(2 * i + k, z)) * 192
                for h in range(2):
                    out[0, at, pl.ds(pl.multiple_of(to + 96 * h, 32), 96), :] = tmp[rows_at, 256 * k + 128 * h:256 * k + 128 * h + 128]
        tmp[...] = nn(cott[...], hid).astype(BF)
        for k in range(2):
            for p in range(2):
                out = (mk.at[j], ms)[p]
                h = xor(inner & 1, p)
                at = xor(2 * (2 * i + k) + h, inner) >> 1
                for b in range(4):
                    to = pl.ds(pl.multiple_of(place(xor(b, z)) * 192, 64), 192)
                    out[1, at, to, :] = tmp[192 * b:192 * b + 192, pl.ds(pl.multiple_of(256 * k + 128 * h, 128), 128)]

    for j in range(3):
        for c in mlp_loads[j]:
            c.wait()
        mlp_step(j, 0)
        if j == 1:
            core_done(pairs[0])
        if j == 2:
            core_done(pairs[1])
        mlp_step(j, 1)
        core_start(pairs[j], ms)
        if j == 0:
            mlp_loads.append(load_mlp(2))
        if j == 2:
            one_done(pairs[0])

    def homeward(which, src, dst):
        def parts(d):
            return remote(src.at[d], dst.at[slot], h_s.at[4 * which + d], h_r.at[3 * which + slot], {"seq": lax.rem(z - d + 4, 4)})

        own = pltpu.make_async_copy(src.at[0], dst.at[slot], h_s.at[4 * which])

        @pl.when(owner)
        def _():
            for d in range(1, 4):
                parts(d).start()
            own.start()

        def finish():
            @pl.when(owner)
            def _():
                for d in range(1, 4):
                    parts(d).wait_send()
                own.wait()

            for k in range(3):
                @pl.when(k + core != z)
                def _():
                    remote(src.at[0], dst.at[k], h_s.at[4 * which], h_r.at[3 * which + k], {"seq": xor(z, 1)}).wait_recv()
        return finish

    down = down_ref[...]
    for d in range(4):
        bo[d, 0:PART] = down[PART * d:PART * d + PART].astype(BF)
    bo_end = homeward(0, bo, bo_home)

    def scatter(c, val):
        pairs[{3: 2, 0: 6, 1: 3, 2: 4}[c]]["c"].wait_send()
        tmp[:, 0:384] = val[:, 0:384].astype(BF)
        tmp2 = val[:, 384:768].astype(BF)
        for half in range(2):
            if half:
                tmp[:, 0:384] = tmp2
            for r in range(8):
                xb, yb = r >> 1 & 1, r >> 2
                rows_at = pl.ds(pl.multiple_of(xor(inner, r) * 96, 32), 96)
                at = 2 * yb + xb if half else 2 * xb + yb
                if r % 2:
                    isnd[half, at] = tmp[rows_at, 0:384]
                else:
                    ik[c, half, at] = tmp[rows_at, 0:384]
        core_start(pairs[3 + c], isnd)

    cot = cot_ref[...].astype(F32)
    dy = dn_ref[...]
    xh, r = norm_parts(res_ref[...])
    g = cot + norm_back(dy, par_ref[G2:G2 + 1], xh, r)
    res_ref[...] = g
    gb = g.astype(BF)
    gproj = nmid_ref
    gproj[...] = gb
    vec[4:5] = col(gb.astype(F32))
    vec[5:6] = col(dy * xh)
    vec[6:7] = col(dy)
    vec[7:8] = col(cot)
    scatter(3, tn(att_ref[...], gb))
    xh, r = norm_parts(joined(xparts))
    nint = nmt
    nint[...] = (xh * par_ref[G1:G1 + 1] + par_ref[B1:B1 + 1]).astype(BF).T
    core_done(pairs[2])
    dm = cot_ref
    acc = dn_ref

    def pair_back(i, pair, da):
        cols = slice(256 * i + 128 * pair, 256 * i + 128 * pair + 128)
        qp = q_ref[:, cols] * jnp.asarray(0.125, BF)
        kp = k_ref[:, cols]
        zero = jnp.zeros_like(qp)
        qm = jnp.concatenate([jnp.where(lane < 64, qp, zero), jnp.where(lane < 64, zero, qp)], axis=0)
        ext = []
        for h in range(2):
            at = 2 * pair + h
            l = lse_ref[i, :, at:at + 1]
            hi = l.astype(BF)
            l = l - hi.astype(F32)
            mid = l.astype(BF)
            lo = (l - mid.astype(F32)).astype(BF)
            ext.append(jnp.where(lane == 5, -hi, jnp.where(lane == 6, -mid, jnp.where(lane == 7, -lo, eq_ref[...]))))
        st = nt(jnp.concatenate([kp, ek_ref[...]], axis=1), jnp.concatenate([qm, jnp.concatenate(ext, axis=0)], axis=1))
        p = jnp.exp(st)
        dap = da[:, 128 * pair:128 * pair + 128]
        dob = jnp.concatenate([jnp.where(lane < 64, dap, zero), jnp.where(lane < 64, zero, dap)], axis=0)
        dpt = nt(v_ref[:, cols], dob)
        dv = nn(p.astype(BF), dob)
        inside = jnp.sum(p * dpt, axis=0, keepdims=True)
        ds = (p * (dpt - inside)).astype(BF)
        dk = nn(ds, qm)
        dq = tn(ds, kp) * 0.125
        at = 128 * pair
        dm[:, at:at + 128] = jnp.where(lane < 64, dq[:rows], dq[rows:]).astype(BF)
        dm[:, 256 + at:256 + at + 128] = dk.astype(BF)
        dm[:, 512 + at:512 + at + 128] = dv.astype(BF)

    polls = {(0, 0): lambda: (one_done(pairs[1]), mlp_z1(0)),
             (0, 1): lambda: (core_done(pairs[6]),),
             (1, 0): lambda: (one_done(pairs[2]), mlp_z1(1), mlp_z2(0)),
             (1, 1): lambda: (core_done(pairs[3]), one_done(pairs[6])),
             (2, 0): lambda: (mlp_z1(2), mlp_z2(1), mlp_end(0)),
             (2, 1): lambda: (core_done(pairs[4]), one_done(pairs[3]), two_done(pairs[6]), mlp_end(1), mlp_z2(2))}
    for i in range(3):
        da = nt(gproj[...], wo_ref[256 * i:256 * i + 256]).astype(BF)
        for pair in range(2):
            pair_back(i, pair, da)
            polls[i, pair]()
        w = jnp.concatenate([wi_ref[:, 768 * j + 256 * i:768 * j + 256 * i + 256] for j in range(3)], axis=1)
        part = nt(dm[...], w)
        acc[...] = part if i == 0 else acc[...] + part
        vec[2:3, 256 * i:256 * i + 256] = col(dm[:, 0:256].astype(F32))
        vec[3:4, 256 * i:256 * i + 256] = col(dm[:, 512:768].astype(F32))
        scatter(i, nn(nint[...], dm[...]))

    xh, r = norm_parts(joined(xparts))
    dy = acc[...]
    vec[0:1] = col(dy * xh)
    vec[1:2] = col(dy)
    vcopies = []

    def vsend(stage):
        if stage < 3:
            vcopies.append([start(remote(vs.at[stage], vr.at[stage], v_s.at[stage], v_r.at[stage], peers[stage]))])
        else:
            vcopies.append([start(remote(vs.at[3], vr.at[2 + s], v_s.at[2 + s], v_r.at[2 + s], along[s])) for s in range(1, 4)])

    def vadd(stage):
        for c in vcopies[stage]:
            c.wait_recv()
        if stage < 3:
            vs[stage + 1] = vs[stage] + vr[stage]
            vsend(stage + 1)
        else:
            vec_out[...] = (vs[3] + vr[3]) + (vr[4] + vr[5])

    vsend(0)
    gi = res_ref[...] + norm_back(dy, par_ref[G1:G1 + 1], xh, r)
    ing = cotparts
    for d in range(4):
        ing[d, 0:PART] = gi[PART * d:PART * d + PART].astype(BF)
    ing_end = homeward(1, ing, ing_home)

    vadd(0)
    core_done(pairs[5])
    one_done(pairs[4])
    two_done(pairs[3])
    vadd(1)
    one_done(pairs[5])
    two_done(pairs[4])
    vadd(2)
    mlp_end(2)
    two_done(pairs[5])

    whole = lambda c: jnp.concatenate([ik[c, 0, 0], ik[c, 1, 0]], axis=1).astype(F32)
    w3 = [whole(c) for c in range(3)]
    full = jnp.concatenate([w3[i][:, 256 * j:256 * j + 256] for j in range(3) for i in range(3)], axis=1)
    wo = whole(3)
    half = lax.broadcasted_iota(jnp.int32, (96, 128), 1) < 64
    for b in range(4):
        if b % 2:
            win = pltpu.roll(full[:, 576 * b - 64:576 * b + 576], 640 - 64, 1)
            w = wo[:, 192 * b - 64:192 * b + 192]
        else:
            win = full[:, 576 * b:576 * b + 640]
            w = pltpu.roll(wo[:, 192 * b:192 * b + 256], 64, 1)
        block = jnp.concatenate([win[:, :512], jnp.where(half, win[:, 512:], w[:, :128]), w[:, 128:]], axis=1)
        izs[xor(z, b)] = block.astype(BF)
    last = [start(remote(izs.at[s], iz.at[s - 1], z_s.at[6 + s - 1], z_r.at[6 + s - 1], along[s])) for s in range(1, 4)]
    vadd(3)
    for c in last:
        c.wait_recv()
    io_out[...] = (izs[0].astype(F32) + iz[0].astype(F32)) + (iz[1].astype(F32) + iz[2].astype(F32))
    ing_end()
    bo_end()
    c_sent()
    for c in sends + [pairs[5]["c"]]:
        c.wait_send()


def inputs_kernel(patches, segments, cotangent, *refs):
    vectors, (xp, cotp, par, wide) = refs[:9], refs[9:]
    strips, length, D = patches.shape
    wide[...] = jnp.zeros_like(wide)
    for k in range(strips):
        wide[0:length] = cotangent[k].astype(F32)
        cotp[k] = wide[...].astype(BF)
    for k in range(strips):
        wide[0:length] = patches[k].astype(F32)
        wide[length:length + 1, 0:length] = segments[k:k + 1].astype(F32)
        xp[k] = wide[...].astype(BF)
    for i in range(8):
        par[i:i + 1] = vectors[i][...].astype(F32).reshape(1, D)
    up = vectors[8][...].astype(F32).reshape(1, 4 * D)
    for i in range(4):
        par[8 + i:9 + i] = up[:, D * i:D * i + D]
    par[12:16] = jnp.zeros((4, D), F32)


def inputs(patches, segments, cotangent, *vectors):
    strips, length, D = patches.shape
    S = jax.ShapeDtypeStruct
    vm = pl.BlockSpec(memory_space=pltpu.VMEM)
    return pl.pallas_call(inputs_kernel, in_specs=[vm] * 12, out_specs=[vm] * 3, name="inputs",
                          out_shape=[S((strips, SENT, D), BF)] * 2 + [S((16, D), F32)],
                          scratch_shapes=[pltpu.VMEM((SENT, D), F32)],
                          compiler_params=pltpu.CompilerParams(vmem_limit_bytes=VL))(patches, segments, cotangent, *vectors)


def layer(stride, xp, cotp, wi, wo, wu, wd, par):
    D = xp.shape[2]
    rows = 4 * PART
    S = jax.ShapeDtypeStruct
    V = pltpu.VMEM
    hbm = pl.BlockSpec(memory_space=pl.ANY)
    vm = pl.BlockSpec(memory_space=pltpu.VMEM)
    wide = lambda t=BF: V((rows, D), t)
    dma = lambda n: pltpu.SemaphoreType.DMA((n,))
    return pl.pallas_call(
        functools.partial(layer_kernel, stride),
        in_specs=[hbm] * 6 + [vm],
        out_specs=[hbm, hbm, vm, vm, vm],
        out_shape=[S((3, SENT, D), BF), S((3, SENT, D), BF), S((3, 2, 192, 128), F32), S((96, D), F32), S((16, D), F32)],
        scratch_shapes=[V((4, SENT, D), BF), V((4, SENT, D), BF), wide(), V((D, rows), BF), wide(), wide(), wide(), wide(),
                        V((3, rows, 128), F32), V((rows, 128), BF), V((rows, 128), BF), wide(F32), wide(F32), wide(F32),
                        wide(), V((D, rows), BF), V((D, 512), BF), V((4, SENT, D), BF),
                        V((D, 3 * D), BF), V((D, D), BF), V((2, D, 1024), BF), V((2, 8, 128, D), BF),
                        V((3, 2, 4, 768, 128), BF), V((2, 4, 768, 128), BF), V((3, 2, 4, 768, 128), BF), V((3, 2, 2, 768, 128), BF),
                        V((3, 2, 1, 768, 128), BF), V((3, 2, 384, 128), BF), V((3, 2, 192, 128), BF),
                        V((4, 2, 4, 96, 384), BF), V((2, 4, 96, 384), BF), V((4, 2, 4, 96, 384), BF), V((4, 2, 2, 96, 384), BF),
                        V((4, 2, 1, 96, 384), BF), V((4, 96, D), BF), V((3, 96, D), BF),
                        V((4, 16, D), F32), V((6, 16, D), F32),
                        dma(29), dma(7), dma(7), dma(14), dma(14), dma(14), dma(14), dma(9), dma(9),
                        dma(6), dma(6), dma(8), dma(6), dma(8), dma(8)],
        name="layer",
        compiler_params=pltpu.CompilerParams(vmem_limit_bytes=VL, collective_id=0, has_side_effects=True),
        cost_estimate=pl.CostEstimate(flops=30_000_000 * 1000, bytes_accessed=16_000_000, transcendentals=0),
    )(xp, cotp, wi, wo, wu, wd, par)


def outputs_kernel(bo, ing, mlp, io, vec, bo_out, ing_out, wi_out, wo_out, wu_out, wd_out, *vec_outs):
    length = bo_out.shape[1]
    for k in range(3):
        bo_out[k] = bo[k].astype(F32)[:length].astype(BF)
        ing_out[k] = ing[k].astype(F32)[:length]
    wi_out[...] = io[:, :576]
    wo_out[...] = io[:, 576:]
    for j in range(3):
        for h in range(2):
            wu_out[:, 384 * h + 128 * j:384 * h + 128 * j + 128] = mlp[j, 0, 96 * h:96 * h + 96]
        wd_out[128 * j:128 * j + 128, :] = mlp[j, 1].T
    for i, out in enumerate(vec_outs[:8]):
        out[...] = vec[i:i + 1].reshape(out.shape)
    vec_outs[8][...] = jnp.concatenate([vec[8 + i:9 + i] for i in range(4)], axis=1).reshape(vec_outs[8].shape)


def outputs(length, bo, ing, mlp, io, vec):
    D = bo.shape[2]
    S = jax.ShapeDtypeStruct
    vm = pl.BlockSpec(memory_space=pltpu.VMEM)
    shapes = [S((3, length, D), BF), S((3, length, D), F32), S((96, 576), F32), S((96, 192), F32), S((96, D), F32), S((384, 192), F32)]
    shapes += [S((D,), F32)] * 8 + [S((4 * D,), F32)]
    return pl.pallas_call(outputs_kernel, in_specs=[vm] * 5, out_specs=[vm] * len(shapes), out_shape=shapes, name="outputs",
                          compiler_params=pltpu.CompilerParams(vmem_limit_bytes=VL))(bo, ing, mlp, io, vec)


def on_device(n_dp, patches, segments, first_gain, first_bias, input_weight, query_bias, value_bias, output_weight,
              output_bias, second_gain, second_bias, up_weight, up_bias, down_weight, down_bias, cotangent):
    strips, length, D = patches.shape
    stride = n_dp // 8
    xp, cotp, par = inputs(patches, segments, cotangent, first_gain, first_bias, query_bias, value_bias, output_bias, second_gain,
                           second_bias, down_bias, up_bias)
    bo, ing, mlp, io, vec = layer(stride, xp, cotp, input_weight, output_weight, up_weight, down_weight.reshape(8, 3, 128, D), par)
    (block_output, input_grad, in_grad, out_grad, up_grad, down_grad, *vecs) = outputs(length, bo, ing, mlp, io, vec)
    weights = [in_grad, out_grad, up_grad, down_grad]
    if stride > 1:
        groups = [[g * stride + t for t in range(stride)] for g in range(8)]
        weights = [lax.psum_scatter(w, "dp", scatter_dimension=0, axis_index_groups=groups, tiled=True) for w in weights]
        vecs = lax.psum(vecs, "dp", axis_index_groups=groups)
    in_grad, out_grad, up_grad, down_grad = weights
    return (block_output, input_grad, vecs[0], vecs[1], in_grad, vecs[2], vecs[3], out_grad, vecs[4], vecs[5], vecs[6], up_grad,
            vecs[8], down_grad, vecs[7])


def solution(mesh):
    rep = P()
    rows = P("dp", "seq", None)
    cut = P("dp", "seq")
    return jax.shard_map(
        functools.partial(on_device, mesh.shape["dp"]),
        mesh=mesh,
        in_specs=(rows, cut) + (rep,) * 13 + (rows,),
        out_specs=(rows, rows, rep, rep, cut, rep, rep, cut, rep, rep, rep, cut, rep, cut, rep),
        check_vma=False,
    )
```

```python
import functools

import jax
import jax.numpy as jnp
from jax import lax
from jax.experimental import pallas as pl
from jax.experimental.pallas import tpu as pltpu
from jax.sharding import PartitionSpec as P

F32 = jnp.float32
BF = jnp.bfloat16
EPS = 1e-6
VL = 62 << 20
PART = 136
SENT = 144
MESH = pl.DeviceIdType.MESH
G1, B1, QB, VB, OB, G2, B2, DB = range(8)
PLAN = (
    "F", "F", "D0", "B", "B", "F", "cD0", "F", "D1", "cU0", "B", "B", "F", "cD1",
    "aD0", "F", "bo", "cU1", "D2", "aU0", "B", "B", "aD1", "M", "cD2", "bD0", "G", "cU2",
    "P", "cI3", "aU1", "P", "bU0", "N", "bD1", "W0", "dD0", "G", "P", "aD2", "dU0", "P",
    "cI0", "dD1", "N", "aU2", "W1", "G", "P", "aI3", "bU1", "P", "cI1", "bD2", "N", "W2",
    "aI0", "dU1", "L", "bU2", "dD2", "eD0", "eU0", "eD1", "v0", "bI3", "cI2", "eU1", "aI1", "v1",
    "bI0", "aI2", "bI1", "bI2", "v2", "dU2", "eD2", "dI3", "dI0", "dI1", "dI2", "eU2", "eI3", "eI0",
    "eI1", "eI2", "v3",
)
AFTER = {4: 0, 5: 1, 7: 9, 8: 6}
TILES = (((0, 1), (2, 3), (4, 5), (5, 5)), ((0, 1), (2, 2), (3, 3), (4, 5)), ((0, 0), (0, 1), (2, 3), (4, 5)),
         ((0, 1), (1, 2), (3, 4), (4, 5)))


def nn(a, b):
    return lax.dot_general(a, b, (((1,), (0,)), ((), ())), preferred_element_type=F32)


def nt(a, b):
    return lax.dot_general(a, b, (((1,), (1,)), ((), ())), preferred_element_type=F32)


def tn(a, b):
    return lax.dot_general(a, b, (((0,), (0,)), ((), ())), preferred_element_type=F32)


def xor(a, b):
    return lax.bitwise_xor(a, b)


def col(v):
    return jnp.sum(v, axis=0, keepdims=True)


def norm_parts(v):
    c = v - jnp.mean(v, axis=-1, keepdims=True)
    r = lax.rsqrt(jnp.mean(c * c, axis=-1, keepdims=True) + EPS)
    return c * r, r


def norm_back(dy, g, xh, r):
    dx = dy * g
    return r * (dx - jnp.mean(dx, axis=-1, keepdims=True) - xh * jnp.mean(dx * xh, axis=-1, keepdims=True))


def gelu_parts(u):
    a = jnp.abs(u)
    t = 1.0 / (a * (0.3275911 * 0.7071067811865476) + 1.0)
    e = jnp.exp(u * u * -0.5)
    w = ((((0.5 * 1.061405429 * t - 0.5 * 1.453152027) * t + 0.5 * 1.421413741) * t - 0.5 * 0.284496736) * t
         + 0.5 * 0.254829592) * t * e
    phi = jnp.where(u >= 0, 1.0 - w, w)
    return u * phi, phi + u * e * 0.3989422804014327


def layer_kernel(stride, patches, segments, cotangent, vec0, vec1, vec2, vec3, vec4, vec5, vec6, vec7, vec8, wi_hbm, wo_hbm, wu_hbm, wd_hbm,
                 bo_home, ing_home, mlp_out, io_out, vec_out,
                 par_ref, xparts, cotparts, cot_ref, cott, q_ref, k_ref, v_ref, att_ref, lse_ref, eq_ref, ek_ref, res_ref, dn_ref, down_ref,
                 nmid_ref, nmt, tmp, bo, wi_ref, wo_ref, wu_ref, wd_ref,
                 hid_ref, der_ref, mk, ms, mc, m1, m2, m3, m4, ik, isnd, ic, i1, i2, izs, iz1, iz2, vs, vr,
                 load_sem, core_s, core_r, a_s, a_r, b_s, b_r, z_s, z_r, v_s, v_r, h_s, h_r, g_s, g_r, credit, go):
    dp, z = lax.axis_index("dp"), lax.axis_index("seq")
    inner = dp // stride
    core = lax.rem(dp, 2)
    mine = z - core
    owner = (mine >= 0) & (mine < 3)
    slot = jnp.clip(mine, 0, 2)
    peers = [{"dp": xor(dp, stride << b)} for b in range(3)]
    along = [{"seq": xor(z, s)} for s in range(4)]
    rows, D = cot_ref.shape

    barrier = pltpu.get_barrier_semaphore()
    for peer in peers + along[1:]:
        pl.semaphore_signal(barrier, inc=1, device_id=peer, device_id_type=MESH)

    def remote(src, dst, ssem, rsem, device):
        return pltpu.make_async_remote_copy(src_ref=src, dst_ref=dst, send_sem=ssem, recv_sem=rsem,
                                            device_id=device, device_id_type=MESH)

    n_loads = [0]

    def load(src, dst):
        c = pltpu.make_async_copy(src, dst, load_sem.at[n_loads[0]])
        n_loads[0] += 1
        c.start()
        return c

    def load_mlp(j):
        s = j % 2
        return [load(wd_hbm.at[:, j], wd_ref.at[s])] + [
            load(wu_hbm.at[:, pl.ds(128 * (3 * b + j), 128)], wu_ref.at[s, :, pl.ds(128 * b, 128)]) for b in range(8)]

    wi_load, wo_load = load(wi_hbm, wi_ref), load(wo_hbm, wo_ref)
    mlp_loads = [load_mlp(0), load_mlp(1)]

    def outward(which, src, dst):
        def each(fn):
            for d in range(1, 4):
                at = lax.rem(z + d, 4)
                k = at - core

                @pl.when((k >= 0) & (k < 3))
                def _():
                    fn(remote(src(jnp.clip(k, 0, 2)), dst.at[d], g_s.at[4 * which + d], g_r.at[4 * which + d], {"seq": at}))

        def own():
            return pltpu.make_async_copy(src(slot), dst.at[0], g_s.at[4 * which])

        def arrived():
            @pl.when(owner)
            def _():
                own().wait()
                for d in range(1, 4):
                    remote(src(0), dst.at[d], g_s.at[4 * which + d], g_r.at[4 * which + d], {"seq": xor(z, 1)}).wait_recv()

        def begin():
            @pl.when(owner)
            def _():
                own().start()
            each(lambda c: c.start())

        return begin, arrived, lambda: each(lambda c: c.wait_send())

    length = patches.shape[1]
    wide = down_ref.at[0:SENT]
    wide[...] = jnp.zeros((SENT, D), F32)
    for k in range(3):
        wide[0:length] = patches[k].astype(F32)
        wide[length:length + 1, 0:length] = segments[k:k + 1].astype(F32)
        bo[k] = wide[...].astype(BF)

    @pl.when(jnp.logical_not(owner))
    def _():
        xparts[...] = jnp.zeros_like(xparts)
        cotparts[...] = jnp.zeros_like(cotparts)

    pl.semaphore_wait(barrier, 6)
    x_begin, x_arrived, x_sent = outward(0, lambda k: bo.at[k], xparts)
    c_begin, c_arrived, c_sent = outward(1, lambda k: cot_ref.at[pl.ds(pl.multiple_of(SENT * k, 16), SENT)], cotparts)
    x_begin()
    wide[length:length + 1] = jnp.zeros((1, D), F32)
    for k in range(3):
        wide[0:length] = cotangent[k].astype(F32)
        cot_ref[SENT * k:SENT * k + SENT] = wide[...].astype(BF)
    for i, v in enumerate((vec0, vec1, vec2, vec3, vec4, vec5, vec6, vec7)):
        par_ref[i:i + 1] = v[...].astype(F32).reshape(1, D)
    up = vec8[...].astype(F32).reshape(1, 4 * D)
    for i in range(4):
        par_ref[8 + i:9 + i] = up[:, D * i:D * i + D]
    x_sent()
    x_arrived()
    for peer in along[1:]:
        pl.semaphore_signal(go, inc=1, device_id=peer, device_id_type=MESH)

    def joined(parts):
        return jnp.concatenate([parts[d].astype(F32)[:PART] for d in range(4)], axis=0)

    row = lax.broadcasted_iota(jnp.int32, (PART, 128), 0)
    spot = lax.broadcasted_iota(jnp.int32, (PART, 128), 1)
    eqs, eks = [], []
    for d in range(4):
        ids = xparts[d, 128:144, 0:256].astype(F32).T[:PART, 5:6]
        ids = jnp.where(row >= length, 4.0, ids)
        same = ids == spot.astype(F32)
        eqs.append(jnp.where(same | (spot >= 5), 0.0, -1e30))
        eks.append(jnp.where((same & (spot < 5)) | ((spot >= 5) & (spot < 8)), 1.0, 0.0))
    eq_ref[...] = jnp.concatenate(eqs, axis=0).astype(BF)
    ek_ref[...] = jnp.concatenate(eks, axis=0).astype(BF)

    lane = lax.broadcasted_iota(jnp.int32, (rows, 128), 1)
    x = joined(xparts)
    xh, _r = norm_parts(x)
    nmid_ref[...] = (xh * par_ref[G1:G1 + 1] + par_ref[B1:B1 + 1]).astype(BF)
    res_ref[...] = x + par_ref[OB:OB + 1]
    lse_ref[...] = jnp.zeros_like(lse_ref)
    pl.semaphore_wait(go, 3)
    c_begin()
    wi_load.wait()
    wo_load.wait()

    @pl.loop(0, 3)
    def _(i):
        cut = lambda j: pl.ds(pl.multiple_of(768 * j + 256 * i, 256), 256)
        at = cut(0)
        nin = nmid_ref[...]
        q_ref[:, at] = (nn(nin, wi_ref[:, cut(0)]) + par_ref[QB:QB + 1, at]).astype(BF)
        k_ref[:, at] = nn(nin, wi_ref[:, cut(1)]).astype(BF)
        v_ref[:, at] = (nn(nin, wi_ref[:, cut(2)]) + par_ref[VB:VB + 1, at]).astype(BF)
        eq, ek = eq_ref[...], ek_ref[...]
        for pair in range(2):
            cols = pl.ds(pl.multiple_of(256 * i + 128 * pair, 128), 128)
            qp = q_ref[:, cols] * jnp.asarray(0.125, BF)
            kp = jnp.concatenate([k_ref[:, cols], ek], axis=1)
            zero = jnp.zeros_like(qp)
            both = jnp.concatenate([jnp.concatenate([jnp.where(lane < 64, qp, zero), eq], axis=1),
                                    jnp.concatenate([jnp.where(lane < 64, zero, qp), eq], axis=1)], axis=0)
            s = nt(both, kp)
            m = jnp.max(s, axis=-1, keepdims=True)
            e = jnp.exp(s - m)
            t = jnp.sum(e, axis=-1, keepdims=True)
            p = (e * (1.0 / t)).astype(BF)
            o = nn(p, v_ref[:, cols])
            log = m + jnp.log(t)
            head = 4 * i + 2 * pair
            lse_ref[...] = jnp.where(lane == head, log[:rows], jnp.where(lane == head + 1, log[rows:], lse_ref[...]))
            att_ref[:, cols] = jnp.where(lane < 64, o[:rows], o[rows:]).astype(BF)
        res_ref[...] += nn(att_ref[:, at], wo_ref[at, :])

    res = res_ref[...]
    xh, _r = norm_parts(res)
    nmid = (xh * par_ref[G2:G2 + 1] + par_ref[B2:B2 + 1]).astype(BF)
    nmid_ref[...] = nmid
    nmt[...] = nmid.T
    down_ref[...] = res + par_ref[DB:DB + 1]

    def cot_in():
        c_arrived()
        c_sent()
        cot = joined(cotparts).astype(BF)
        cot_ref[...] = cot
        cott[...] = cot.T

    def unit(n, wide, keep, got, one, two, **more):
        if wide:
            lo, hi = pl.ds(0, 384), pl.ds(384, 384)
            p = dict(a_send=[keep.at[1, :, lo], keep.at[:, 1, hi]], b_send=[keep.at[0, 1, lo], keep.at[1, 0, hi]],
                     a_keep=[[keep.at[0, k, lo] for k in range(2)], [keep.at[k, 0, hi] for k in range(2)]],
                     b_keep=[keep.at[0, 0, lo], keep.at[0, 0, hi]])
        else:
            p = dict(a_send=[keep.at[0, 1], keep.at[1, :, 1]], b_send=[keep.at[0, 0, 1], keep.at[1, 1, 0]],
                     a_keep=[[keep.at[0, 0, k] for k in range(2)], [keep.at[1, k, 0] for k in range(2)]],
                     b_keep=[keep.at[0, 0, 0], keep.at[1, 0, 0]])
        return dict(p, n=n, keep=keep, got=got, one=one, two=two, **more)

    mlp = [[unit(2 * j + u, True, mk.at[j, u], mc.at[j % 2, u], m1.at[j, u], m2.at[j, u], j=j, u=u) for u in range(2)]
           for j in range(3)]
    io = [unit(6 + c, False, ik.at[c], ic.at[(c + 1) % 2], i1.at[c], i2.at[c]) for c in range(4)]
    sends = []

    def start(c):
        c.start()
        sends.append(c)
        return c

    def place(s):
        return (s & 1) * 2 + (s >> 1)

    def core_start(p, src):
        if p["n"] in AFTER:
            pl.semaphore_wait(credit.at[AFTER[p["n"]]], 1)
        p["c"] = remote(src, p["got"], core_s.at[p["n"]], core_r.at[p["n"]], peers[0])
        p["c"].start()
        p["open"] = True

    def core_sent(p):
        if p.pop("open", False):
            p["c"].wait_send()

    def core_done(p):
        n = p["n"]
        p["c"].wait_recv()
        keep, got = p["keep"], p["got"]
        for a in range(2):
            for b in range(2):
                if "j" in p:
                    keep[a, b] += got[a, b]
                else:
                    keep[:, a, b] += got[:, a, b]
        if n in AFTER.values():
            pl.semaphore_signal(credit.at[n], inc=1, device_id=peers[0], device_id_type=MESH)
        p["a"] = [start(remote(p["a_send"][h], p["one"].at[h], a_s.at[2 * n + h], a_r.at[2 * n + h], peers[1 + h])) for h in range(2)]

    def one_done(p):
        n = p["n"]
        for h in range(2):
            p["a"][h].wait_recv()
            for k in range(2):
                p["a_keep"][h][k][...] += p["one"][h, k]
        p["b"] = [start(remote(p["b_send"][h], p["two"].at[h], b_s.at[2 * n + h], b_r.at[2 * n + h], peers[2 - h])) for h in range(2)]

    def two_done(p):
        n = p["n"]
        for h in range(2):
            p["b"][h].wait_recv()
            p["b_keep"][h][...] += p["two"][h]
        if "j" in p:
            src, dst = mk.at[p["j"], p["u"], 0, 0, pl.ds(384, 384)], m3.at[p["j"], p["u"]]
        else:
            c = n - 6
            for b in range(4):
                for t, tile in enumerate(TILES[c][b]):
                    izs[c, place(xor(b, z)), t] = ik[c, tile // 3, 0, 0, :, 128 * (tile % 3):128 * (tile % 3) + 128]
            src, dst = izs.at[c, pl.ds(2, 2)], iz1.at[c]
        p["z"] = start(remote(src, dst, z_s.at[2 * n], z_r.at[2 * n], along[1]))

    def near_done(p):
        n = p["n"]
        p["z"].wait_recv()
        if "j" in p:
            j, u = p["j"], p["u"]
            mk[j, u, 0, 0, 0:384] += m3[j, u]
            src, dst = mk.at[j, u, 0, 0, pl.ds(192, 192)], m4.at[j, u]
        else:
            c = n - 6
            for k in range(2):
                izs[c, k] += iz1[c, k]
            src, dst = izs.at[c, 1], iz2.at[c]
        p["z"] = start(remote(src, dst, z_s.at[2 * n + 1], z_r.at[2 * n + 1], along[2]))

    def far_done(p):
        p["z"].wait_recv()
        if "j" in p:
            j, u = p["j"], p["u"]
            mlp_out[j, u] = mk[j, u, 0, 0, 0:192].astype(F32) + m4[j, u].astype(F32)
        else:
            c = p["n"] - 6
            io_out[c] = izs[c, 0].astype(F32) + iz2[c].astype(F32)

    vec = vs.at[0]
    vec[12:16] = jnp.zeros((4, D), F32)

    def hidden_bias(t):
        return par_ref[8 + t // 6:9 + t // 6, 128 * (t % 6):128 * (t % 6) + 128]

    def mlp_forward(j, i):
        s = j % 2
        wu = wu_ref[s, :, 512 * i:512 * i + 512]
        wd = wd_ref[s, 4 * i:4 * i + 4].reshape(512, D)
        ub = jnp.concatenate([hidden_bias(3 * b + j) for b in range(4 * i, 4 * i + 4)], axis=1)
        act, der = gelu_parts(nn(nmid_ref[...], wu) + ub)
        hid = act.astype(BF)
        hid_ref[:, 512 * i:512 * i + 512] = hid
        der_ref[:, 512 * i:512 * i + 512] = der
        down_ref[...] += nn(hid, wd)

    def mlp_down_grad(j):
        if j:
            core_sent(mlp[j - 1][1])
        else:
            cot_in()
        for i in range(2):
            tmp[...] = nn(cott[...], hid_ref[:, 512 * i:512 * i + 512]).astype(BF)
            for k in range(2):
                for p in range(2):
                    out = (mk.at[j], ms)[p]
                    h = xor(inner & 1, p)
                    rel = xor(2 * (2 * i + k) + h, inner)
                    xb, yb = (rel >> 1) & 1, rel >> 2
                    for b in range(4):
                        to = pl.ds(pl.multiple_of(place(xor(b, z)) * 192, 64), 192)
                        out[1, xb, yb, to, :] = tmp[192 * b:192 * b + 192, pl.ds(pl.multiple_of(256 * k + 128 * h, 128), 128)]
        core_start(mlp[j][1], ms.at[1])

    def mlp_backward(j, i):
        s = j % 2
        wu = wu_ref[s, :, 512 * i:512 * i + 512]
        wd = wd_ref[s, 4 * i:4 * i + 4].reshape(512, D)
        gu = (nt(cot_ref[...], wd) * der_ref[:, 512 * i:512 * i + 512]).astype(BF)
        part = nt(gu, wu)
        dn_ref[...] = part if j == 0 and i == 0 else dn_ref[...] + part
        sums = col(gu.astype(F32))
        for b in range(4):
            t = 3 * (4 * i + b) + j
            vec[8 + t // 6:9 + t // 6, 128 * (t % 6):128 * (t % 6) + 128] = sums[:, 128 * b:128 * b + 128]
        if i == 0 and j:
            core_sent(mlp[j - 1][0])
        tmp[...] = nn(nmt[...], gu).astype(BF)
        for r in range(8):
            out = mk.at[j] if r % 2 == 0 else ms
            xb, yb = r >> 1 & 1, r >> 2
            rows_at = pl.ds(pl.multiple_of(xor(inner, r) * 96, 32), 96)
            for k in range(2):
                to = place(xor(2 * i + k, z)) * 192
                for h in range(2):
                    out[0, xb, yb, pl.ds(pl.multiple_of(to + 96 * h, 32), 96), :] = tmp[rows_at, 256 * k + 128 * h:256 * k + 128 * h + 128]

    def forward(j, i):
        if i == 0:
            for c in mlp_loads[j]:
                c.wait()
        mlp_forward(j, i)

    def backward(j, i):
        mlp_backward(j, i)
        if i == 1:
            core_start(mlp[j][0], ms.at[0])
            if j == 0:
                mlp_loads.append(load_mlp(2))

    def homeward(which, src, dst):
        def parts(d):
            return remote(src.at[d], dst.at[slot], h_s.at[4 * which + d], h_r.at[3 * which + slot], {"seq": lax.rem(z - d + 4, 4)})

        own = pltpu.make_async_copy(src.at[0], dst.at[slot], h_s.at[4 * which])

        @pl.when(owner)
        def _():
            for d in range(1, 4):
                parts(d).start()
            own.start()

        def finish():
            @pl.when(owner)
            def _():
                for d in range(1, 4):
                    parts(d).wait_send()
                own.wait()

            for k in range(3):
                @pl.when(k + core != z)
                def _():
                    remote(src.at[0], dst.at[k], h_s.at[4 * which], h_r.at[3 * which + k], {"seq": xor(z, 1)}).wait_recv()
        return finish

    ends = []

    def block_home():
        down = down_ref[...]
        for d in range(4):
            bo[d, 0:PART] = down[PART * d:PART * d + PART].astype(BF)
        ends.append(homeward(0, bo, bo_home))


    def scatter(c, val):
        for before in {3: mlp[2], 0: [io[3]], 1: [io[0]], 2: [io[1]]}[c]:
            core_sent(before)
        for half in range(2):
            tmp[:, 0:384] = val[:, 384 * half:384 * half + 384].astype(BF)
            for r in range(8):
                xb, yb = r >> 1 & 1, r >> 2
                rows_at = pl.ds(pl.multiple_of(xor(inner, r) * 96, 32), 96)
                if r % 2:
                    isnd[half, xb, yb] = tmp[rows_at, 0:384]
                else:
                    ik[c, half, xb, yb] = tmp[rows_at, 0:384]
        core_start(io[c], isnd)

    gproj, nint, dm, acc = nmid_ref, nmt, cot_ref, dn_ref

    def middle():
        cot = cot_ref[...].astype(F32)
        dy = dn_ref[...]
        xh, r = norm_parts(res_ref[...])
        g = cot + norm_back(dy, par_ref[G2:G2 + 1], xh, r)
        res_ref[...] = g
        gb = g.astype(BF)
        gproj[...] = gb
        vec[4:5] = col(gb.astype(F32))
        vec[5:6] = col(dy * xh)
        vec[6:7] = col(dy)
        vec[7:8] = col(cot)
        scatter(3, tn(att_ref[...], gb))
        xh, r = norm_parts(joined(xparts))
        nint[...] = (xh * par_ref[G1:G1 + 1] + par_ref[B1:B1 + 1]).astype(BF).T

    def pair_back(i, pair, da):
        cols = slice(256 * i + 128 * pair, 256 * i + 128 * pair + 128)
        qp = q_ref[:, cols] * jnp.asarray(0.125, BF)
        kp = k_ref[:, cols]
        zero = jnp.zeros_like(qp)
        qm = jnp.concatenate([jnp.where(lane < 64, qp, zero), jnp.where(lane < 64, zero, qp)], axis=0)
        ext = []
        for h in range(2):
            at = 4 * i + 2 * pair + h
            l = lse_ref[:, at:at + 1]
            hi = l.astype(BF)
            l = l - hi.astype(F32)
            mid = l.astype(BF)
            lo = (l - mid.astype(F32)).astype(BF)
            ext.append(jnp.where(lane == 5, -hi, jnp.where(lane == 6, -mid, jnp.where(lane == 7, -lo, eq_ref[...]))))
        st = nt(jnp.concatenate([kp, ek_ref[...]], axis=1), jnp.concatenate([qm, jnp.concatenate(ext, axis=0)], axis=1))
        p = jnp.exp(st)
        dap = da[:, 128 * pair:128 * pair + 128]
        dob = jnp.concatenate([jnp.where(lane < 64, dap, zero), jnp.where(lane < 64, zero, dap)], axis=0)
        dpt = nt(v_ref[:, cols], dob)
        dv = nn(p.astype(BF), dob)
        inside = jnp.sum(p * dpt, axis=0, keepdims=True)
        ds = (p * (dpt - inside)).astype(BF)
        dk = nn(ds, qm)
        dq = tn(ds, kp) * 0.125
        at = 128 * pair
        dm[:, at:at + 128] = jnp.where(lane < 64, dq[:rows], dq[rows:]).astype(BF)
        dm[:, 256 + at:256 + at + 128] = dk.astype(BF)
        dm[:, 512 + at:512 + at + 128] = dv.astype(BF)

    grad_att = {}

    def head_group(i):
        grad_att[i] = nt(gproj[...], wo_ref[256 * i:256 * i + 256]).astype(BF)

    def group_input(i):
        w = jnp.concatenate([wi_ref[:, 768 * j + 256 * i:768 * j + 256 * i + 256] for j in range(3)], axis=1)
        part = nt(dm[...], w)
        acc[...] = part if i == 0 else acc[...] + part
        vec[2:3, 256 * i:256 * i + 256] = col(dm[:, 0:256].astype(F32))
        vec[3:4, 256 * i:256 * i + 256] = col(dm[:, 512:768].astype(F32))

    def group_weight(i):
        scatter(i, nn(nint[...], dm[...]))

    vcopies = []

    def vsend(stage):
        if stage < 3:
            vcopies.append([start(remote(vs.at[stage], vr.at[stage], v_s.at[stage], v_r.at[stage], peers[stage]))])
        else:
            vcopies.append([start(remote(vs.at[3], vr.at[2 + s], v_s.at[2 + s], v_r.at[2 + s], along[s])) for s in range(1, 4)])

    def vadd(stage):
        for c in vcopies[stage]:
            c.wait_recv()
        if stage < 3:
            vs[stage + 1] = vs[stage] + vr[stage]
            vsend(stage + 1)
        else:
            vec_out[...] = (vs[3] + vr[3]) + (vr[4] + vr[5])

    def last():
        xh, r = norm_parts(joined(xparts))
        dy = acc[...]
        vec[0:1] = col(dy * xh)
        vec[1:2] = col(dy)
        vsend(0)
        gi = res_ref[...] + norm_back(dy, par_ref[G1:G1 + 1], xh, r)
        ing = cotparts
        for d in range(4):
            ing[d, 0:PART] = gi[PART * d:PART * d + PART].astype(BF)
        ends.append(homeward(1, ing, ing_home))

    number = {"F": [(j, i) for j in range(3) for i in range(2)], "B": [(j, i) for j in range(3) for i in range(2)],
              "P": [(i, pair) for i in range(3) for pair in range(2)], "G": range(3), "N": range(3)}
    number = {k: iter(v) for k, v in number.items()}

    simple = {"bo": block_home, "M": middle, "L": last}
    indexed = {"D": mlp_down_grad, "W": group_weight, "v": vadd}
    staged = {"c": core_done, "a": one_done, "b": two_done, "d": near_done, "e": far_done}
    units = {"I%d" % c: io[c] for c in range(4)}
    units.update({"UD"[u] + "%d" % j: mlp[j][u] for j in range(3) for u in range(2)})
    for step in PLAN:
        if step in simple:
            simple[step]()
        elif step == "F":
            forward(*next(number["F"]))
        elif step == "B":
            backward(*next(number["B"]))
        elif step == "G":
            head_group(next(number["G"]))
        elif step == "P":
            i, pair = next(number["P"])
            pair_back(i, pair, grad_att[i])
        elif step == "N":
            group_input(next(number["N"]))
        elif len(step) == 3:
            staged[step[0]](units[step[1:]])
        else:
            indexed[step[0]](int(step[1]))
    for end in ends:
        end()
    for p in units.values():
        core_sent(p)
    for c in sends:
        c.wait_send()


def layer(stride, patches, segments, cotangent, vectors, wi, wo, wu, wd):
    D = patches.shape[2]
    rows = 4 * PART
    S = jax.ShapeDtypeStruct
    V = pltpu.VMEM
    hbm = pl.BlockSpec(memory_space=pl.ANY)
    vm = pl.BlockSpec(memory_space=pltpu.VMEM)
    wide = lambda t=BF: V((rows, D), t)
    dma = lambda n: pltpu.SemaphoreType.DMA((n,))
    return pl.pallas_call(
        functools.partial(layer_kernel, stride),
        in_specs=[vm] * 12 + [hbm] * 4,
        out_specs=[hbm, hbm, vm, vm, vm],
        out_shape=[S((3, SENT, D), BF), S((3, SENT, D), BF), S((3, 2, 192, 128), F32), S((4, 2, 96, 128), F32), S((16, D), F32)],
        scratch_shapes=[V((16, D), F32), V((4, SENT, D), BF), V((4, SENT, D), BF), wide(), V((D, rows), BF), wide(), wide(), wide(), wide(),
                        V((rows, 128), F32), V((rows, 128), BF), V((rows, 128), BF), wide(F32), wide(F32), wide(F32),
                        wide(), V((D, rows), BF), V((D, 512), BF), V((4, SENT, D), BF),
                        V((D, 3 * D), BF), V((D, D), BF), V((2, D, 1024), BF), V((2, 8, 128, D), BF),
                        V((rows, 1024), BF), V((rows, 1024), F32),
                        V((3, 2, 2, 2, 768, 128), BF), V((2, 2, 2, 768, 128), BF), V((2, 2, 2, 2, 768, 128), BF),
                        V((3, 2, 2, 2, 384, 128), BF), V((3, 2, 2, 384, 128), BF), V((3, 2, 384, 128), BF), V((3, 2, 192, 128), BF),
                        V((4, 2, 2, 2, 96, 384), BF), V((2, 2, 2, 96, 384), BF), V((2, 2, 2, 2, 96, 384), BF),
                        V((4, 2, 2, 96, 384), BF), V((4, 2, 96, 384), BF),
                        V((4, 4, 2, 96, 128), BF), V((4, 2, 2, 96, 128), BF), V((4, 2, 96, 128), BF),
                        V((4, 16, D), F32), V((6, 16, D), F32),
                        dma(29), dma(10), dma(10), dma(20), dma(20), dma(20), dma(20), dma(20), dma(20),
                        dma(6), dma(6), dma(8), dma(6), dma(8), dma(8), pltpu.SemaphoreType.REGULAR((10,)), pltpu.SemaphoreType.REGULAR],
        name="layer",
        compiler_params=pltpu.CompilerParams(vmem_limit_bytes=VL, collective_id=0, has_side_effects=True),
        cost_estimate=pl.CostEstimate(flops=30_000_000 * 1000, bytes_accessed=16_000_000, transcendentals=0),
    )(patches, segments, cotangent, *vectors, wi, wo, wu, wd)


def outputs_kernel(bo_hbm, ing_hbm, mlp_hbm, io_hbm, vec_hbm, *refs):
    results, vec_outs, refs = refs[:6], refs[6:15], refs[15:]
    (bo, ing, mlp, io, vec), (bo_out, ing_out, wi_out, wo_out, wu_out, wd_out), arrive, leave = refs[:5], refs[5:11], refs[11], refs[12]
    length = bo_out.shape[1]
    ins = [pltpu.make_async_copy(ing_hbm.at[k], ing.at[k], arrive.at[k]) for k in range(3)]
    ins += [pltpu.make_async_copy(bo_hbm.at[k], bo.at[k], arrive.at[3 + k]) for k in range(3)]
    ins += [pltpu.make_async_copy(a, b, arrive.at[6 + k]) for k, (a, b) in enumerate(((mlp_hbm, mlp), (io_hbm, io), (vec_hbm, vec)))]
    for c in ins:
        c.start()
    outs = []

    def write(src, dst):
        c = pltpu.make_async_copy(src, dst, leave.at[len(outs)])
        c.start()
        outs.append(c)

    for k in range(3):
        ins[k].wait()
        ing_out[k] = ing[k].astype(F32)[:length]
        write(ing_out.at[k], results[1].at[k])
    for k in range(3):
        ins[3 + k].wait()
        bo_out[k] = bo[k].astype(F32)[:length].astype(BF)
        write(bo_out.at[k], results[0].at[k])
    ins[6].wait()
    for j in range(3):
        for h in range(2):
            wu_out[:, 384 * h + 128 * j:384 * h + 128 * j + 128] = mlp[j, 0, 96 * h:96 * h + 96]
        wd_out[:, 128 * j:128 * j + 128] = mlp[j, 1]
    write(wu_out, results[4])
    write(wd_out, results[5])
    ins[7].wait()
    z = lax.axis_index("seq")
    order = (((0, 0), (0, 1), (1, 0), (1, 1), (2, 0)), ((2, 0), (2, 1), (0, 0), (0, 1), (1, 0)),
             ((1, 0), (2, 0), (2, 1), (0, 0), (0, 1)), ((0, 0), (1, 0), (1, 1), (2, 0), (2, 1)))
    for b in range(4):
        @pl.when(z == b)
        def _():
            wi = jnp.concatenate([io[c, t] for c, t in order[b]], axis=1)
            wo = jnp.concatenate([io[3, 0], io[3, 1]], axis=1)
            if b % 2:
                wi, wo = pltpu.roll(wi, 640 - 64, 1), pltpu.roll(wo, 256 - 64, 1)
            wi_out[...] = wi[:, :576]
            wo_out[...] = wo[:, :192]

    write(wi_out, results[2])
    write(wo_out, results[3])
    ins[8].wait()
    for i, out in enumerate(vec_outs[:8]):
        out[...] = vec[i:i + 1].reshape(out.shape)
    vec_outs[8][...] = jnp.concatenate([vec[8 + i:9 + i] for i in range(4)], axis=1).reshape(vec_outs[8].shape)
    for c in outs:
        c.wait()


def outputs(length, bo, ing, mlp, io, vec):
    D = bo.shape[2]
    S = jax.ShapeDtypeStruct
    vm = pl.BlockSpec(memory_space=pltpu.VMEM)
    hbm = pl.BlockSpec(memory_space=pl.ANY)
    big = [S((3, length, D), BF), S((3, length, D), F32), S((96, 576), F32), S((96, 192), F32), S((96, D), F32), S((192, 384), F32)]
    held = [pltpu.VMEM(a.shape, a.dtype) for a in (bo, ing, mlp, io, vec, *big)]
    return pl.pallas_call(outputs_kernel, in_specs=[hbm] * 5, out_specs=[hbm] * 6 + [vm] * 9,
                          out_shape=big + [S((D,), F32)] * 8 + [S((4 * D,), F32)], name="outputs",
                          scratch_shapes=held + [pltpu.SemaphoreType.DMA((9,)), pltpu.SemaphoreType.DMA((10,))],
                          compiler_params=pltpu.CompilerParams(vmem_limit_bytes=VL))(bo, ing, mlp, io, vec)


def on_device(n_dp, patches, segments, first_gain, first_bias, input_weight, query_bias, value_bias, output_weight,
              output_bias, second_gain, second_bias, up_weight, up_bias, down_weight, down_bias, cotangent):
    strips, length, D = patches.shape
    stride = n_dp // 8
    vectors = (first_gain, first_bias, query_bias, value_bias, output_bias, second_gain, second_bias, down_bias, up_bias)
    bo, ing, mlp, io, vec = layer(stride, patches, segments, cotangent, vectors, input_weight, output_weight, up_weight,
                                  down_weight.reshape(8, 3, 128, D))
    (block_output, input_grad, in_grad, out_grad, up_grad, down_grad, *vecs) = outputs(length, bo, ing, mlp, io, vec)
    weights = [in_grad, out_grad, up_grad, down_grad.T]
    if stride > 1:
        groups = [[g * stride + t for t in range(stride)] for g in range(8)]
        weights = [lax.psum_scatter(w, "dp", scatter_dimension=0, axis_index_groups=groups, tiled=True) for w in weights]
        vecs = lax.psum(vecs, "dp", axis_index_groups=groups)
    in_grad, out_grad, up_grad, down_grad = weights
    return (block_output, input_grad, vecs[0], vecs[1], in_grad, vecs[2], vecs[3], out_grad, vecs[4], vecs[5], vecs[6], up_grad,
            vecs[8], down_grad, vecs[7])


def solution(mesh):
    rep = P()
    rows = P("dp", "seq", None)
    cut = P("dp", "seq")
    return jax.shard_map(
        functools.partial(on_device, mesh.shape["dp"]),
        mesh=mesh,
        in_specs=(rows, cut) + (rep,) * 13 + (rows,),
        out_specs=(rows, rows, rep, rep, cut, rep, rep, cut, rep, rep, rep, cut, rep, cut, rep),
        check_vma=False,
    )
```

```python
import functools

import jax
import jax.numpy as jnp
from jax import lax
from jax.experimental import pallas as pl
from jax.experimental.pallas import tpu as pltpu
from jax.sharding import PartitionSpec as P

F32 = jnp.float32
BF = jnp.bfloat16
EPS = 1e-6
VL = 62 << 20
PART = 136
SENT = 144
MESH = pl.DeviceIdType.MESH
G1, B1, QB, VB, OB, G2, B2, DB = range(8)
PLAN = (
    "F", "F", "D0", "B", "B", "cD0", "sD0", "F", "F", "cU0", "sU0", "D1", "aD0", "B",
    "B", "cD1", "aU0", "sD1", "F", "bD0", "F", "cU1", "sU1", "bU0", "bo", "D2", "dD0", "B",
    "aD1", "dU0", "B", "cD2", "aU1", "sD2", "M", "cU2", "sU2", "bD1", "G", "bU1", "P", "cI3",
    "sI3", "P", "aD2", "N", "W0", "aU2", "dD1", "G", "P", "aI3", "dU1", "P", "cI0", "sI0",
    "bD2", "N", "bU2", "W1", "bI3", "G", "P", "aI0", "dD2", "P", "cI1", "sI1", "dU2", "dI3",
    "N", "L", "bI0", "W2", "aI1", "eD0", "v0", "eU0", "eD1", "eU1", "eD2", "v1", "eU2", "eI3",
    "cI2", "v2", "sI2", "bI1", "aI2", "bI2", "dI0", "dI1", "dI2", "eI0", "eI1", "eI2", "v3",
)
AFTER = {4: 0, 5: 1, 7: 9, 8: 6}
TILES = (((0, 1), (2, 3), (4, 5), (5, 5)), ((0, 1), (2, 2), (3, 3), (4, 5)), ((0, 0), (0, 1), (2, 3), (4, 5)),
         ((0, 1), (1, 2), (3, 4), (4, 5)))


def nn(a, b):
    return lax.dot_general(a, b, (((1,), (0,)), ((), ())), preferred_element_type=F32)


def nt(a, b):
    return lax.dot_general(a, b, (((1,), (1,)), ((), ())), preferred_element_type=F32)


def tn(a, b):
    return lax.dot_general(a, b, (((0,), (0,)), ((), ())), preferred_element_type=F32)


def xor(a, b):
    return lax.bitwise_xor(a, b)


def col(v):
    return jnp.sum(v, axis=0, keepdims=True)


def norm_parts(v):
    c = v - jnp.mean(v, axis=-1, keepdims=True)
    r = lax.rsqrt(jnp.mean(c * c, axis=-1, keepdims=True) + EPS)
    return c * r, r


def norm_back(dy, g, xh, r):
    dx = dy * g
    return r * (dx - jnp.mean(dx, axis=-1, keepdims=True) - xh * jnp.mean(dx * xh, axis=-1, keepdims=True))


def gelu_parts(u):
    a = jnp.abs(u)
    t = 1.0 / (a * (0.3275911 * 0.7071067811865476) + 1.0)
    e = jnp.exp(u * u * -0.5)
    w = ((((0.5 * 1.061405429 * t - 0.5 * 1.453152027) * t + 0.5 * 1.421413741) * t - 0.5 * 0.284496736) * t
         + 0.5 * 0.254829592) * t * e
    phi = jnp.where(u >= 0, 1.0 - w, w)
    return u * phi, phi + u * e * 0.3989422804014327


def layer_kernel(stride, patches, segments, cotangent, vec0, vec1, vec2, vec3, vec4, vec5, vec6, vec7, vec8, wi_hbm, wo_hbm, wu_hbm, wd_hbm,
                 bo_home, ing_home, mlp_out, io_out, vec_out,
                 par_ref, xparts, cotparts, cot_ref, cott, q_ref, k_ref, v_ref, att_ref, lse_ref, eq_ref, ek_ref, res_ref, dn_ref, down_ref,
                 nmid_ref, nmt, tmp, bo, wi_ref, wo_ref, wu_ref, wd_ref,
                 hid_ref, der_ref, mk, ms, mc, m1, m2, m3, m4, ik, isnd, ic, i1, i2, izs, iz1, iz2, vs, vr,
                 load_sem, core_s, core_r, a_s, a_r, b_s, b_r, z_s, z_r, v_s, v_r, h_s, h_r, g_s, g_r, credit, go):
    dp, z = lax.axis_index("dp"), lax.axis_index("seq")
    inner = dp // stride
    core = lax.rem(dp, 2)
    mine = z - core
    owner = (mine >= 0) & (mine < 3)
    slot = jnp.clip(mine, 0, 2)
    peers = [{"dp": xor(dp, stride << b)} for b in range(3)]
    along = [{"seq": xor(z, s)} for s in range(4)]
    rows, D = cot_ref.shape

    barrier = pltpu.get_barrier_semaphore()
    for peer in peers + along[1:]:
        pl.semaphore_signal(barrier, inc=1, device_id=peer, device_id_type=MESH)

    def remote(src, dst, ssem, rsem, device):
        return pltpu.make_async_remote_copy(src_ref=src, dst_ref=dst, send_sem=ssem, recv_sem=rsem,
                                            device_id=device, device_id_type=MESH)

    n_loads = [0]

    def load(src, dst):
        c = pltpu.make_async_copy(src, dst, load_sem.at[n_loads[0]])
        n_loads[0] += 1
        c.start()
        return c

    def load_mlp(j):
        s = j % 2
        return [load(wd_hbm.at[:, j], wd_ref.at[s])] + [
            load(wu_hbm.at[:, pl.ds(128 * (3 * b + j), 128)], wu_ref.at[s, :, pl.ds(128 * b, 128)]) for b in range(8)]

    wi_load, wo_load = load(wi_hbm, wi_ref), load(wo_hbm, wo_ref)
    mlp_loads = [load_mlp(0), load_mlp(1)]

    def outward(which, src, dst):
        def each(fn):
            for d in range(1, 4):
                at = lax.rem(z + d, 4)
                k = at - core

                @pl.when((k >= 0) & (k < 3))
                def _():
                    fn(remote(src(jnp.clip(k, 0, 2)), dst.at[d], g_s.at[4 * which + d], g_r.at[4 * which + d], {"seq": at}))

        def own():
            return pltpu.make_async_copy(src(slot), dst.at[0], g_s.at[4 * which])

        def arrived():
            @pl.when(owner)
            def _():
                own().wait()
                for d in range(1, 4):
                    remote(src(0), dst.at[d], g_s.at[4 * which + d], g_r.at[4 * which + d], {"seq": xor(z, 1)}).wait_recv()

        def begin():
            @pl.when(owner)
            def _():
                own().start()
            each(lambda c: c.start())

        return begin, arrived, lambda: each(lambda c: c.wait_send())

    length = patches.shape[1]
    wide = down_ref.at[0:SENT]
    wide[...] = jnp.zeros((SENT, D), F32)
    for k in range(3):
        wide[0:length] = patches[k].astype(F32)
        wide[length:length + 1, 0:length] = segments[k:k + 1].astype(F32)
        bo[k] = wide[...].astype(BF)

    @pl.when(jnp.logical_not(owner))
    def _():
        xparts[...] = jnp.zeros_like(xparts)
        cotparts[...] = jnp.zeros_like(cotparts)

    pl.semaphore_wait(barrier, 6)
    x_begin, x_arrived, x_sent = outward(0, lambda k: bo.at[k], xparts)
    c_begin, c_arrived, c_sent = outward(1, lambda k: cot_ref.at[pl.ds(pl.multiple_of(SENT * k, 16), SENT)], cotparts)
    x_begin()
    wide[length:length + 1] = jnp.zeros((1, D), F32)
    for k in range(3):
        wide[0:length] = cotangent[k].astype(F32)
        cot_ref[SENT * k:SENT * k + SENT] = wide[...].astype(BF)
    for i, v in enumerate((vec0, vec1, vec2, vec3, vec4, vec5, vec6, vec7)):
        par_ref[i:i + 1] = v[...].astype(F32).reshape(1, D)
    up = vec8[...].astype(F32).reshape(1, 4 * D)
    for i in range(4):
        par_ref[8 + i:9 + i] = up[:, D * i:D * i + D]
    x_sent()
    x_arrived()
    for peer in along[1:]:
        pl.semaphore_signal(go, inc=1, device_id=peer, device_id_type=MESH)

    def joined(parts):
        return jnp.concatenate([parts[d].astype(F32)[:PART] for d in range(4)], axis=0)

    row = lax.broadcasted_iota(jnp.int32, (PART, 128), 0)
    spot = lax.broadcasted_iota(jnp.int32, (PART, 128), 1)
    eqs, eks = [], []
    for d in range(4):
        ids = xparts[d, 128:144, 0:256].astype(F32).T[:PART, 5:6]
        ids = jnp.where(row >= length, 4.0, ids)
        same = ids == spot.astype(F32)
        eqs.append(jnp.where(same | (spot >= 5), 0.0, -1e30))
        eks.append(jnp.where((same & (spot < 5)) | ((spot >= 5) & (spot < 8)), 1.0, 0.0))
    eq_ref[...] = jnp.concatenate(eqs, axis=0).astype(BF)
    ek_ref[...] = jnp.concatenate(eks, axis=0).astype(BF)

    lane = lax.broadcasted_iota(jnp.int32, (rows, 128), 1)
    x = joined(xparts)
    xh, _r = norm_parts(x)
    nmid_ref[...] = (xh * par_ref[G1:G1 + 1] + par_ref[B1:B1 + 1]).astype(BF)
    res_ref[...] = x + par_ref[OB:OB + 1]
    lse_ref[...] = jnp.zeros_like(lse_ref)
    pl.semaphore_wait(go, 3)
    c_begin()
    wi_load.wait()
    wo_load.wait()

    @pl.loop(0, 3)
    def _(i):
        cut = lambda j: pl.ds(pl.multiple_of(768 * j + 256 * i, 256), 256)
        at = cut(0)
        nin = nmid_ref[...]
        q_ref[:, at] = (nn(nin, wi_ref[:, cut(0)]) + par_ref[QB:QB + 1, at]).astype(BF)
        k_ref[:, at] = nn(nin, wi_ref[:, cut(1)]).astype(BF)
        v_ref[:, at] = (nn(nin, wi_ref[:, cut(2)]) + par_ref[VB:VB + 1, at]).astype(BF)
        eq, ek = eq_ref[...], ek_ref[...]
        for pair in range(2):
            cols = pl.ds(pl.multiple_of(256 * i + 128 * pair, 128), 128)
            qp = q_ref[:, cols] * jnp.asarray(0.125, BF)
            kp = jnp.concatenate([k_ref[:, cols], ek], axis=1)
            zero = jnp.zeros_like(qp)
            both = jnp.concatenate([jnp.concatenate([jnp.where(lane < 64, qp, zero), eq], axis=1),
                                    jnp.concatenate([jnp.where(lane < 64, zero, qp), eq], axis=1)], axis=0)
            s = nt(both, kp)
            m = jnp.max(s, axis=-1, keepdims=True)
            e = jnp.exp(s - m)
            t = jnp.sum(e, axis=-1, keepdims=True)
            p = (e * (1.0 / t)).astype(BF)
            o = nn(p, v_ref[:, cols])
            log = m + jnp.log(t)
            head = 4 * i + 2 * pair
            lse_ref[...] = jnp.where(lane == head, log[:rows], jnp.where(lane == head + 1, log[rows:], lse_ref[...]))
            att_ref[:, cols] = jnp.where(lane < 64, o[:rows], o[rows:]).astype(BF)
        res_ref[...] += nn(att_ref[:, at], wo_ref[at, :])

    res = res_ref[...]
    xh, _r = norm_parts(res)
    nmid = (xh * par_ref[G2:G2 + 1] + par_ref[B2:B2 + 1]).astype(BF)
    nmid_ref[...] = nmid
    nmt[...] = nmid.T
    down_ref[...] = res + par_ref[DB:DB + 1]

    def cot_in():
        c_arrived()
        c_sent()
        cot = joined(cotparts).astype(BF)
        cot_ref[...] = cot
        cott[...] = cot.T

    def unit(n, wide, keep, got, one, two, **more):
        if wide:
            lo, hi = pl.ds(0, 384), pl.ds(384, 384)
            p = dict(a_send=[keep.at[1, :, lo], keep.at[:, 1, hi]], b_send=[keep.at[0, 1, lo], keep.at[1, 0, hi]],
                     a_keep=[[keep.at[0, k, lo] for k in range(2)], [keep.at[k, 0, hi] for k in range(2)]],
                     b_keep=[keep.at[0, 0, lo], keep.at[0, 0, hi]])
        else:
            p = dict(a_send=[keep.at[0, 1], keep.at[1, :, 1]], b_send=[keep.at[0, 0, 1], keep.at[1, 1, 0]],
                     a_keep=[[keep.at[0, 0, k] for k in range(2)], [keep.at[1, k, 0] for k in range(2)]],
                     b_keep=[keep.at[0, 0, 0], keep.at[1, 0, 0]])
        return dict(p, n=n, keep=keep, got=got, one=one, two=two, **more)

    mlp = [[unit(2 * j + u, True, mk.at[j, u], mc.at[j % 2, u], m1.at[j, u], m2.at[j, u], j=j, u=u) for u in range(2)]
           for j in range(3)]
    io = [unit(6 + c, False, ik.at[c], ic.at[(c + 1) % 2], i1.at[c], i2.at[c]) for c in range(4)]
    sends = []

    def start(c):
        c.start()
        sends.append(c)
        return c

    def place(s):
        return (s & 1) * 2 + (s >> 1)

    def core_start(p, src):
        if p["n"] in AFTER:
            pl.semaphore_wait(credit.at[AFTER[p["n"]]], 1)
        p["c"] = remote(src, p["got"], core_s.at[p["n"]], core_r.at[p["n"]], peers[0])
        p["c"].start()
        p["open"] = True

    def core_sent(p):
        if p.pop("open", False):
            p["c"].wait_send()

    def core_done(p):
        n = p["n"]
        p["c"].wait_recv()
        keep, got = p["keep"], p["got"]
        for a in range(2):
            for b in range(2):
                if "j" in p:
                    keep[a, b] += got[a, b]
                else:
                    keep[:, a, b] += got[:, a, b]
        if n in AFTER.values():
            pl.semaphore_signal(credit.at[n], inc=1, device_id=peers[0], device_id_type=MESH)

    def one_start(p):
        n = p["n"]
        p["a"] = [start(remote(p["a_send"][h], p["one"].at[h], a_s.at[2 * n + h], a_r.at[2 * n + h], peers[1 + h])) for h in range(2)]

    def one_done(p):
        n = p["n"]
        for h in range(2):
            p["a"][h].wait_recv()
            for k in range(2):
                p["a_keep"][h][k][...] += p["one"][h, k]
        p["b"] = [start(remote(p["b_send"][h], p["two"].at[h], b_s.at[2 * n + h], b_r.at[2 * n + h], peers[2 - h])) for h in range(2)]

    def two_done(p):
        n = p["n"]
        for h in range(2):
            p["b"][h].wait_recv()
            p["b_keep"][h][...] += p["two"][h]
        if "j" in p:
            src, dst = mk.at[p["j"], p["u"], 0, 0, pl.ds(384, 384)], m3.at[p["j"], p["u"]]
        else:
            c = n - 6
            for b in range(4):
                for t, tile in enumerate(TILES[c][b]):
                    izs[c, place(xor(b, z)), t] = ik[c, tile // 3, 0, 0, :, 128 * (tile % 3):128 * (tile % 3) + 128]
            src, dst = izs.at[c, pl.ds(2, 2)], iz1.at[c]
        p["z"] = start(remote(src, dst, z_s.at[2 * n], z_r.at[2 * n], along[1]))

    def near_done(p):
        n = p["n"]
        p["z"].wait_recv()
        if "j" in p:
            j, u = p["j"], p["u"]
            mk[j, u, 0, 0, 0:384] += m3[j, u]
            src, dst = mk.at[j, u, 0, 0, pl.ds(192, 192)], m4.at[j, u]
        else:
            c = n - 6
            for k in range(2):
                izs[c, k] += iz1[c, k]
            src, dst = izs.at[c, 1], iz2.at[c]
        p["z"] = start(remote(src, dst, z_s.at[2 * n + 1], z_r.at[2 * n + 1], along[2]))

    def far_done(p):
        p["z"].wait_recv()
        if "j" in p:
            j, u = p["j"], p["u"]
            mlp_out[j, u] = mk[j, u, 0, 0, 0:192].astype(F32) + m4[j, u].astype(F32)
        else:
            c = p["n"] - 6
            io_out[c] = izs[c, 0].astype(F32) + iz2[c].astype(F32)

    vec = vs.at[0]
    vec[12:16] = jnp.zeros((4, D), F32)

    def hidden_bias(t):
        return par_ref[8 + t // 6:9 + t // 6, 128 * (t % 6):128 * (t % 6) + 128]

    def mlp_forward(j, i):
        s = j % 2
        wu = wu_ref[s, :, 512 * i:512 * i + 512]
        wd = wd_ref[s, 4 * i:4 * i + 4].reshape(512, D)
        ub = jnp.concatenate([hidden_bias(3 * b + j) for b in range(4 * i, 4 * i + 4)], axis=1)
        act, der = gelu_parts(nn(nmid_ref[...], wu) + ub)
        hid = act.astype(BF)
        hid_ref[:, 512 * i:512 * i + 512] = hid
        der_ref[:, 512 * i:512 * i + 512] = der
        down_ref[...] += nn(hid, wd)

    def mlp_down_grad(j):
        if j:
            core_sent(mlp[j - 1][1])
        else:
            cot_in()
        for i in range(2):
            tmp[...] = nn(cott[...], hid_ref[:, 512 * i:512 * i + 512]).astype(BF)
            for k in range(2):
                for p in range(2):
                    out = (mk.at[j], ms)[p]
                    h = xor(inner & 1, p)
                    rel = xor(2 * (2 * i + k) + h, inner)
                    xb, yb = (rel >> 1) & 1, rel >> 2
                    for b in range(4):
                        to = pl.ds(pl.multiple_of(place(xor(b, z)) * 192, 64), 192)
                        out[1, xb, yb, to, :] = tmp[192 * b:192 * b + 192, pl.ds(pl.multiple_of(256 * k + 128 * h, 128), 128)]
        core_start(mlp[j][1], ms.at[1])

    def mlp_backward(j, i):
        s = j % 2
        wu = wu_ref[s, :, 512 * i:512 * i + 512]
        wd = wd_ref[s, 4 * i:4 * i + 4].reshape(512, D)
        gu = (nt(cot_ref[...], wd) * der_ref[:, 512 * i:512 * i + 512]).astype(BF)
        part = nt(gu, wu)
        dn_ref[...] = part if j == 0 and i == 0 else dn_ref[...] + part
        sums = col(gu.astype(F32))
        for b in range(4):
            t = 3 * (4 * i + b) + j
            vec[8 + t // 6:9 + t // 6, 128 * (t % 6):128 * (t % 6) + 128] = sums[:, 128 * b:128 * b + 128]
        if i == 0 and j:
            core_sent(mlp[j - 1][0])
        tmp[...] = nn(nmt[...], gu).astype(BF)
        for r in range(8):
            out = mk.at[j] if r % 2 == 0 else ms
            xb, yb = r >> 1 & 1, r >> 2
            rows_at = pl.ds(pl.multiple_of(xor(inner, r) * 96, 32), 96)
            for k in range(2):
                to = place(xor(2 * i + k, z)) * 192
                for h in range(2):
                    out[0, xb, yb, pl.ds(pl.multiple_of(to + 96 * h, 32), 96), :] = tmp[rows_at, 256 * k + 128 * h:256 * k + 128 * h + 128]

    def forward(j, i):
        if i == 0:
            for c in mlp_loads[j]:
                c.wait()
        mlp_forward(j, i)

    def backward(j, i):
        mlp_backward(j, i)
        if i == 1:
            core_start(mlp[j][0], ms.at[0])
            if j == 0:
                mlp_loads.append(load_mlp(2))

    def homeward(which, src, dst):
        def parts(d):
            return remote(src.at[d], dst.at[slot], h_s.at[4 * which + d], h_r.at[3 * which + slot], {"seq": lax.rem(z - d + 4, 4)})

        own = pltpu.make_async_copy(src.at[0], dst.at[slot], h_s.at[4 * which])

        @pl.when(owner)
        def _():
            for d in range(1, 4):
                parts(d).start()
            own.start()

        def finish():
            @pl.when(owner)
            def _():
                for d in range(1, 4):
                    parts(d).wait_send()
                own.wait()

            for k in range(3):
                @pl.when(k + core != z)
                def _():
                    remote(src.at[0], dst.at[k], h_s.at[4 * which], h_r.at[3 * which + k], {"seq": xor(z, 1)}).wait_recv()
        return finish

    ends = []

    def block_home():
        down = down_ref[...]
        for d in range(4):
            bo[d, 0:PART] = down[PART * d:PART * d + PART].astype(BF)
        ends.append(homeward(0, bo, bo_home))


    def scatter(c, val):
        for before in {3: mlp[2], 0: [io[3]], 1: [io[0]], 2: [io[1]]}[c]:
            core_sent(before)
        for half in range(2):
            tmp[:, 0:384] = val[:, 384 * half:384 * half + 384].astype(BF)
            for r in range(8):
                xb, yb = r >> 1 & 1, r >> 2
                rows_at = pl.ds(pl.multiple_of(xor(inner, r) * 96, 32), 96)
                if r % 2:
                    isnd[half, xb, yb] = tmp[rows_at, 0:384]
                else:
                    ik[c, half, xb, yb] = tmp[rows_at, 0:384]
        core_start(io[c], isnd)

    gproj, nint, dm, acc = nmid_ref, nmt, cot_ref, dn_ref

    def middle():
        cot = cot_ref[...].astype(F32)
        dy = dn_ref[...]
        xh, r = norm_parts(res_ref[...])
        g = cot + norm_back(dy, par_ref[G2:G2 + 1], xh, r)
        res_ref[...] = g
        gb = g.astype(BF)
        gproj[...] = gb
        vec[4:5] = col(gb.astype(F32))
        vec[5:6] = col(dy * xh)
        vec[6:7] = col(dy)
        vec[7:8] = col(cot)
        scatter(3, tn(att_ref[...], gb))
        xh, r = norm_parts(joined(xparts))
        nint[...] = (xh * par_ref[G1:G1 + 1] + par_ref[B1:B1 + 1]).astype(BF).T

    def pair_back(i, pair, da):
        cols = slice(256 * i + 128 * pair, 256 * i + 128 * pair + 128)
        qp = q_ref[:, cols] * jnp.asarray(0.125, BF)
        kp = k_ref[:, cols]
        zero = jnp.zeros_like(qp)
        qm = jnp.concatenate([jnp.where(lane < 64, qp, zero), jnp.where(lane < 64, zero, qp)], axis=0)
        ext = []
        for h in range(2):
            at = 4 * i + 2 * pair + h
            l = lse_ref[:, at:at + 1]
            hi = l.astype(BF)
            l = l - hi.astype(F32)
            mid = l.astype(BF)
            lo = (l - mid.astype(F32)).astype(BF)
            ext.append(jnp.where(lane == 5, -hi, jnp.where(lane == 6, -mid, jnp.where(lane == 7, -lo, eq_ref[...]))))
        st = nt(jnp.concatenate([kp, ek_ref[...]], axis=1), jnp.concatenate([qm, jnp.concatenate(ext, axis=0)], axis=1))
        p = jnp.exp(st)
        dap = da[:, 128 * pair:128 * pair + 128]
        dob = jnp.concatenate([jnp.where(lane < 64, dap, zero), jnp.where(lane < 64, zero, dap)], axis=0)
        dpt = nt(v_ref[:, cols], dob)
        dv = nn(p.astype(BF), dob)
        inside = jnp.sum(p * dpt, axis=0, keepdims=True)
        ds = (p * (dpt - inside)).astype(BF)
        dk = nn(ds, qm)
        dq = tn(ds, kp) * 0.125
        at = 128 * pair
        dm[:, at:at + 128] = jnp.where(lane < 64, dq[:rows], dq[rows:]).astype(BF)
        dm[:, 256 + at:256 + at + 128] = dk.astype(BF)
        dm[:, 512 + at:512 + at + 128] = dv.astype(BF)

    grad_att = {}

    def head_group(i):
        grad_att[i] = nt(gproj[...], wo_ref[256 * i:256 * i + 256]).astype(BF)

    def group_input(i):
        w = jnp.concatenate([wi_ref[:, 768 * j + 256 * i:768 * j + 256 * i + 256] for j in range(3)], axis=1)
        part = nt(dm[...], w)
        acc[...] = part if i == 0 else acc[...] + part
        vec[2:3, 256 * i:256 * i + 256] = col(dm[:, 0:256].astype(F32))
        vec[3:4, 256 * i:256 * i + 256] = col(dm[:, 512:768].astype(F32))

    def group_weight(i):
        scatter(i, nn(nint[...], dm[...]))

    vcopies = []

    def vsend(stage):
        if stage < 3:
            vcopies.append([start(remote(vs.at[stage], vr.at[stage], v_s.at[stage], v_r.at[stage], peers[stage]))])
        else:
            vcopies.append([start(remote(vs.at[3], vr.at[2 + s], v_s.at[2 + s], v_r.at[2 + s], along[s])) for s in range(1, 4)])

    def vadd(stage):
        for c in vcopies[stage]:
            c.wait_recv()
        if stage < 3:
            vs[stage + 1] = vs[stage] + vr[stage]
            vsend(stage + 1)
        else:
            vec_out[...] = (vs[3] + vr[3]) + (vr[4] + vr[5])

    def last():
        xh, r = norm_parts(joined(xparts))
        dy = acc[...]
        vec[0:1] = col(dy * xh)
        vec[1:2] = col(dy)
        vsend(0)
        gi = res_ref[...] + norm_back(dy, par_ref[G1:G1 + 1], xh, r)
        ing = cotparts
        for d in range(4):
            ing[d, 0:PART] = gi[PART * d:PART * d + PART].astype(BF)
        ends.append(homeward(1, ing, ing_home))

    number = {"F": [(j, i) for j in range(3) for i in range(2)], "B": [(j, i) for j in range(3) for i in range(2)],
              "P": [(i, pair) for i in range(3) for pair in range(2)], "G": range(3), "N": range(3)}
    number = {k: iter(v) for k, v in number.items()}

    simple = {"bo": block_home, "M": middle, "L": last}
    indexed = {"D": mlp_down_grad, "W": group_weight, "v": vadd}
    staged = {"c": core_done, "s": one_start, "a": one_done, "b": two_done, "d": near_done, "e": far_done}
    units = {"I%d" % c: io[c] for c in range(4)}
    units.update({"UD"[u] + "%d" % j: mlp[j][u] for j in range(3) for u in range(2)})
    for step in PLAN:
        if step in simple:
            simple[step]()
        elif step == "F":
            forward(*next(number["F"]))
        elif step == "B":
            backward(*next(number["B"]))
        elif step == "G":
            head_group(next(number["G"]))
        elif step == "P":
            i, pair = next(number["P"])
            pair_back(i, pair, grad_att[i])
        elif step == "N":
            group_input(next(number["N"]))
        elif len(step) == 3:
            staged[step[0]](units[step[1:]])
        else:
            indexed[step[0]](int(step[1]))
    for end in ends:
        end()
    for p in units.values():
        core_sent(p)
    for c in sends:
        c.wait_send()


def layer(stride, patches, segments, cotangent, vectors, wi, wo, wu, wd):
    D = patches.shape[2]
    rows = 4 * PART
    S = jax.ShapeDtypeStruct
    V = pltpu.VMEM
    hbm = pl.BlockSpec(memory_space=pl.ANY)
    vm = pl.BlockSpec(memory_space=pltpu.VMEM)
    wide = lambda t=BF: V((rows, D), t)
    dma = lambda n: pltpu.SemaphoreType.DMA((n,))
    return pl.pallas_call(
        functools.partial(layer_kernel, stride),
        in_specs=[vm] * 12 + [hbm] * 4,
        out_specs=[hbm, hbm, vm, vm, vm],
        out_shape=[S((3, SENT, D), BF), S((3, SENT, D), BF), S((3, 2, 192, 128), F32), S((4, 2, 96, 128), F32), S((16, D), F32)],
        scratch_shapes=[V((16, D), F32), V((4, SENT, D), BF), V((4, SENT, D), BF), wide(), V((D, rows), BF), wide(), wide(), wide(), wide(),
                        V((rows, 128), F32), V((rows, 128), BF), V((rows, 128), BF), wide(F32), wide(F32), wide(F32),
                        wide(), V((D, rows), BF), V((D, 512), BF), V((4, SENT, D), BF),
                        V((D, 3 * D), BF), V((D, D), BF), V((2, D, 1024), BF), V((2, 8, 128, D), BF),
                        V((rows, 1024), BF), V((rows, 1024), F32),
                        V((3, 2, 2, 2, 768, 128), BF), V((2, 2, 2, 768, 128), BF), V((2, 2, 2, 2, 768, 128), BF),
                        V((3, 2, 2, 2, 384, 128), BF), V((3, 2, 2, 384, 128), BF), V((3, 2, 384, 128), BF), V((3, 2, 192, 128), BF),
                        V((4, 2, 2, 2, 96, 384), BF), V((2, 2, 2, 96, 384), BF), V((2, 2, 2, 2, 96, 384), BF),
                        V((4, 2, 2, 96, 384), BF), V((4, 2, 96, 384), BF),
                        V((4, 4, 2, 96, 128), BF), V((4, 2, 2, 96, 128), BF), V((4, 2, 96, 128), BF),
                        V((4, 16, D), F32), V((6, 16, D), F32),
                        dma(29), dma(10), dma(10), dma(20), dma(20), dma(20), dma(20), dma(20), dma(20),
                        dma(6), dma(6), dma(8), dma(6), dma(8), dma(8), pltpu.SemaphoreType.REGULAR((10,)), pltpu.SemaphoreType.REGULAR],
        name="layer",
        compiler_params=pltpu.CompilerParams(vmem_limit_bytes=VL, collective_id=0, has_side_effects=True),
        cost_estimate=pl.CostEstimate(flops=30_000_000 * 1000, bytes_accessed=16_000_000, transcendentals=0),
    )(patches, segments, cotangent, *vectors, wi, wo, wu, wd)


def outputs_kernel(bo_hbm, ing_hbm, mlp_hbm, io_hbm, vec_hbm, *refs):
    results, vec_outs, refs = refs[:6], refs[6:15], refs[15:]
    (bo, ing, mlp, io, vec), (bo_out, ing_out, wi_out, wo_out, wu_out, wd_out), arrive, leave = refs[:5], refs[5:11], refs[11], refs[12]
    length = bo_out.shape[1]
    ins = [pltpu.make_async_copy(ing_hbm.at[k], ing.at[k], arrive.at[k]) for k in range(3)]
    ins += [pltpu.make_async_copy(bo_hbm.at[k], bo.at[k], arrive.at[3 + k]) for k in range(3)]
    ins += [pltpu.make_async_copy(a, b, arrive.at[6 + k]) for k, (a, b) in enumerate(((mlp_hbm, mlp), (io_hbm, io), (vec_hbm, vec)))]
    for c in ins:
        c.start()
    outs = []

    def write(src, dst):
        c = pltpu.make_async_copy(src, dst, leave.at[len(outs)])
        c.start()
        outs.append(c)

    for k in range(3):
        ins[k].wait()
        ing_out[k] = ing[k].astype(F32)[:length]
        write(ing_out.at[k], results[1].at[k])
    for k in range(3):
        ins[3 + k].wait()
        bo_out[k] = bo[k].astype(F32)[:length].astype(BF)
        write(bo_out.at[k], results[0].at[k])
    ins[6].wait()
    for j in range(3):
        for h in range(2):
            wu_out[:, 384 * h + 128 * j:384 * h + 128 * j + 128] = mlp[j, 0, 96 * h:96 * h + 96]
        wd_out[:, 128 * j:128 * j + 128] = mlp[j, 1]
    write(wu_out, results[4])
    write(wd_out, results[5])
    ins[7].wait()
    z = lax.axis_index("seq")
    order = (((0, 0), (0, 1), (1, 0), (1, 1), (2, 0)), ((2, 0), (2, 1), (0, 0), (0, 1), (1, 0)),
             ((1, 0), (2, 0), (2, 1), (0, 0), (0, 1)), ((0, 0), (1, 0), (1, 1), (2, 0), (2, 1)))
    for b in range(4):
        @pl.when(z == b)
        def _():
            wi = jnp.concatenate([io[c, t] for c, t in order[b]], axis=1)
            wo = jnp.concatenate([io[3, 0], io[3, 1]], axis=1)
            if b % 2:
                wi, wo = pltpu.roll(wi, 640 - 64, 1), pltpu.roll(wo, 256 - 64, 1)
            wi_out[...] = wi[:, :576]
            wo_out[...] = wo[:, :192]

    write(wi_out, results[2])
    write(wo_out, results[3])
    ins[8].wait()
    for i, out in enumerate(vec_outs[:8]):
        out[...] = vec[i:i + 1].reshape(out.shape)
    vec_outs[8][...] = jnp.concatenate([vec[8 + i:9 + i] for i in range(4)], axis=1).reshape(vec_outs[8].shape)
    for c in outs:
        c.wait()


def outputs(length, bo, ing, mlp, io, vec):
    D = bo.shape[2]
    S = jax.ShapeDtypeStruct
    vm = pl.BlockSpec(memory_space=pltpu.VMEM)
    hbm = pl.BlockSpec(memory_space=pl.ANY)
    big = [S((3, length, D), BF), S((3, length, D), F32), S((96, 576), F32), S((96, 192), F32), S((96, D), F32), S((192, 384), F32)]
    held = [pltpu.VMEM(a.shape, a.dtype) for a in (bo, ing, mlp, io, vec, *big)]
    return pl.pallas_call(outputs_kernel, in_specs=[hbm] * 5, out_specs=[hbm] * 6 + [vm] * 9,
                          out_shape=big + [S((D,), F32)] * 8 + [S((4 * D,), F32)], name="outputs",
                          scratch_shapes=held + [pltpu.SemaphoreType.DMA((9,)), pltpu.SemaphoreType.DMA((10,))],
                          compiler_params=pltpu.CompilerParams(vmem_limit_bytes=VL))(bo, ing, mlp, io, vec)


def on_device(n_dp, patches, segments, first_gain, first_bias, input_weight, query_bias, value_bias, output_weight,
              output_bias, second_gain, second_bias, up_weight, up_bias, down_weight, down_bias, cotangent):
    strips, length, D = patches.shape
    stride = n_dp // 8
    vectors = (first_gain, first_bias, query_bias, value_bias, output_bias, second_gain, second_bias, down_bias, up_bias)
    bo, ing, mlp, io, vec = layer(stride, patches, segments, cotangent, vectors, input_weight, output_weight, up_weight,
                                  down_weight.reshape(8, 3, 128, D))
    (block_output, input_grad, in_grad, out_grad, up_grad, down_grad, *vecs) = outputs(length, bo, ing, mlp, io, vec)
    weights = [in_grad, out_grad, up_grad, down_grad.T]
    if stride > 1:
        groups = [[g * stride + t for t in range(stride)] for g in range(8)]
        weights = [lax.psum_scatter(w, "dp", scatter_dimension=0, axis_index_groups=groups, tiled=True) for w in weights]
        vecs = lax.psum(vecs, "dp", axis_index_groups=groups)
    in_grad, out_grad, up_grad, down_grad = weights
    return (block_output, input_grad, vecs[0], vecs[1], in_grad, vecs[2], vecs[3], out_grad, vecs[4], vecs[5], vecs[6], up_grad,
            vecs[8], down_grad, vecs[7])


def solution(mesh):
    rep = P()
    rows = P("dp", "seq", None)
    cut = P("dp", "seq")
    return jax.shard_map(
        functools.partial(on_device, mesh.shape["dp"]),
        mesh=mesh,
        in_specs=(rows, cut) + (rep,) * 13 + (rows,),
        out_specs=(rows, rows, rep, rep, cut, rep, rep, cut, rep, rep, rep, cut, rep, cut, rep),
        check_vma=False,
    )
```

```python
import functools

import jax
import jax.numpy as jnp
from jax import lax
from jax.experimental import pallas as pl
from jax.experimental.pallas import tpu as pltpu
from jax.sharding import PartitionSpec as P

F32 = jnp.float32
BF = jnp.bfloat16
EPS = 1e-6
VL = 62 << 20
PART = 136
SENT = 144
MESH = pl.DeviceIdType.MESH
G1, B1, QB, VB, OB, G2, B2, DB = range(8)
PLAN = (
    "F", "F", "D0", "B", "B", "cD0", "sD0", "F", "F", "cU0", "sU0", "D1", "aD0", "B",
    "B", "cD1", "aU0", "sD1", "F", "bD0", "F", "cU1", "sU1", "bU0", "bo", "D2", "dD0", "B",
    "aD1", "dU0", "B", "cD2", "aU1", "sD2", "M", "cU2", "sU2", "bD1", "G", "bU1", "P", "cI3",
    "sI3", "P", "aD2", "N", "W0", "aU2", "dD1", "G", "P", "aI3", "dU1", "P", "cI0", "sI0",
    "bD2", "N", "bU2", "W1", "bI3", "G", "P", "aI0", "dD2", "P", "cI1", "sI1", "dU2", "dI3",
    "N", "L", "bI0", "W2", "aI1", "cI2", "sI2", "v0", "bI1", "aI2", "v1", "bI2", "v2", "dI0",
    "dI1", "dI2", "eD0", "eU0", "eD1", "eU1", "eD2", "eU2", "eI3", "eI0", "eI1", "eI2", "v3",
)
AFTER = {4: 0, 5: 1, 7: 9, 8: 6}
TILES = (((0, 1), (2, 3), (4, 5), (5, 5)), ((0, 1), (2, 2), (3, 3), (4, 5)), ((0, 0), (0, 1), (2, 3), (4, 5)),
         ((0, 1), (1, 2), (3, 4), (4, 5)))


def nn(a, b):
    return lax.dot_general(a, b, (((1,), (0,)), ((), ())), preferred_element_type=F32)


def nt(a, b):
    return lax.dot_general(a, b, (((1,), (1,)), ((), ())), preferred_element_type=F32)


def tn(a, b):
    return lax.dot_general(a, b, (((0,), (0,)), ((), ())), preferred_element_type=F32)


def xor(a, b):
    return lax.bitwise_xor(a, b)


def col(v):
    return jnp.sum(v, axis=0, keepdims=True)


def norm_parts(v):
    c = v - jnp.mean(v, axis=-1, keepdims=True)
    r = lax.rsqrt(jnp.mean(c * c, axis=-1, keepdims=True) + EPS)
    return c * r, r


def norm_back(dy, g, xh, r):
    dx = dy * g
    return r * (dx - jnp.mean(dx, axis=-1, keepdims=True) - xh * jnp.mean(dx * xh, axis=-1, keepdims=True))


def gelu_parts(u):
    a = jnp.abs(u)
    t = 1.0 / (a * (0.3275911 * 0.7071067811865476) + 1.0)
    e = jnp.exp(u * u * -0.5)
    w = ((((0.5 * 1.061405429 * t - 0.5 * 1.453152027) * t + 0.5 * 1.421413741) * t - 0.5 * 0.284496736) * t
         + 0.5 * 0.254829592) * t * e
    phi = jnp.where(u >= 0, 1.0 - w, w)
    return u * phi, phi + u * e * 0.3989422804014327


def layer_kernel(stride, patches, segments, cotangent, vec0, vec1, vec2, vec3, vec4, vec5, vec6, vec7, vec8, wi_hbm, wo_hbm, wu_hbm, wd_hbm,
                 bo_home, ing_home, mlp_out, io_out, vec_out,
                 par_ref, xparts, cotparts, cot_ref, cott, q_ref, k_ref, v_ref, att_ref, lse_ref, eq_ref, ek_ref, res_ref, dn_ref, down_ref,
                 nmid_ref, nmt, tmp, bo, wi_ref, wo_ref, wu_ref, wd_ref,
                 hid_ref, der_ref, mk, ms, mc, m1, m2, m3, m4, ik, isnd, ic, i1, i2, izs, iz1, iz2, vs, vr,
                 load_sem, core_s, core_r, a_s, a_r, b_s, b_r, z_s, z_r, v_s, v_r, h_s, h_r, g_s, g_r, credit, go):
    dp, z = lax.axis_index("dp"), lax.axis_index("seq")
    inner = dp // stride
    core = lax.rem(dp, 2)
    mine = z - core
    owner = (mine >= 0) & (mine < 3)
    slot = jnp.clip(mine, 0, 2)
    peers = [{"dp": xor(dp, stride << b)} for b in range(3)]
    along = [{"seq": xor(z, s)} for s in range(4)]
    rows, D = cot_ref.shape

    barrier = pltpu.get_barrier_semaphore()
    for peer in peers + along[1:]:
        pl.semaphore_signal(barrier, inc=1, device_id=peer, device_id_type=MESH)

    def remote(src, dst, ssem, rsem, device):
        return pltpu.make_async_remote_copy(src_ref=src, dst_ref=dst, send_sem=ssem, recv_sem=rsem,
                                            device_id=device, device_id_type=MESH)

    n_loads = [0]

    def load(src, dst):
        c = pltpu.make_async_copy(src, dst, load_sem.at[n_loads[0]])
        n_loads[0] += 1
        c.start()
        return c

    def load_mlp(j):
        s = j % 2
        return [load(wd_hbm.at[:, j], wd_ref.at[s])] + [
            load(wu_hbm.at[:, pl.ds(128 * (3 * b + j), 128)], wu_ref.at[s, :, pl.ds(128 * b, 128)]) for b in range(8)]

    wi_load, wo_load = load(wi_hbm, wi_ref), load(wo_hbm, wo_ref)
    mlp_loads = [load_mlp(0), load_mlp(1)]

    def outward(which, src, dst):
        def each(fn):
            for d in range(1, 4):
                at = lax.rem(z + d, 4)
                k = at - core

                @pl.when((k >= 0) & (k < 3))
                def _():
                    fn(remote(src(jnp.clip(k, 0, 2)), dst.at[d], g_s.at[4 * which + d], g_r.at[4 * which + d], {"seq": at}))

        def own():
            return pltpu.make_async_copy(src(slot), dst.at[0], g_s.at[4 * which])

        def arrived():
            @pl.when(owner)
            def _():
                own().wait()
                for d in range(1, 4):
                    remote(src(0), dst.at[d], g_s.at[4 * which + d], g_r.at[4 * which + d], {"seq": xor(z, 1)}).wait_recv()

        def begin():
            @pl.when(owner)
            def _():
                own().start()
            each(lambda c: c.start())

        return begin, arrived, lambda: each(lambda c: c.wait_send())

    length = patches.shape[1]
    wide = down_ref.at[0:SENT]
    wide[...] = jnp.zeros((SENT, D), F32)
    for k in range(3):
        wide[0:length] = patches[k].astype(F32)
        wide[length:length + 1, 0:length] = segments[k:k + 1].astype(F32)
        bo[k] = wide[...].astype(BF)

    @pl.when(jnp.logical_not(owner))
    def _():
        xparts[...] = jnp.zeros_like(xparts)
        cotparts[...] = jnp.zeros_like(cotparts)

    pl.semaphore_wait(barrier, 6)
    x_begin, x_arrived, x_sent = outward(0, lambda k: bo.at[k], xparts)
    c_begin, c_arrived, c_sent = outward(1, lambda k: cot_ref.at[pl.ds(pl.multiple_of(SENT * k, 16), SENT)], cotparts)
    x_begin()
    wide[length:length + 1] = jnp.zeros((1, D), F32)
    for k in range(3):
        wide[0:length] = cotangent[k].astype(F32)
        cot_ref[SENT * k:SENT * k + SENT] = wide[...].astype(BF)
    for i, v in enumerate((vec0, vec1, vec2, vec3, vec4, vec5, vec6, vec7)):
        par_ref[i:i + 1] = v[...].astype(F32).reshape(1, D)
    up = vec8[...].astype(F32).reshape(1, 4 * D)
    for i in range(4):
        par_ref[8 + i:9 + i] = up[:, D * i:D * i + D]
    x_sent()
    x_arrived()
    for peer in along[1:]:
        pl.semaphore_signal(go, inc=1, device_id=peer, device_id_type=MESH)

    def joined(parts):
        return jnp.concatenate([parts[d].astype(F32)[:PART] for d in range(4)], axis=0)

    row = lax.broadcasted_iota(jnp.int32, (PART, 128), 0)
    spot = lax.broadcasted_iota(jnp.int32, (PART, 128), 1)
    eqs, eks = [], []
    for d in range(4):
        ids = xparts[d, 128:144, 0:256].astype(F32).T[:PART, 5:6]
        ids = jnp.where(row >= length, 4.0, ids)
        same = ids == spot.astype(F32)
        eqs.append(jnp.where(same | (spot >= 5), 0.0, -1e30))
        eks.append(jnp.where((same & (spot < 5)) | ((spot >= 5) & (spot < 8)), 1.0, 0.0))
    eq_ref[...] = jnp.concatenate(eqs, axis=0).astype(BF)
    ek_ref[...] = jnp.concatenate(eks, axis=0).astype(BF)

    lane = lax.broadcasted_iota(jnp.int32, (rows, 128), 1)
    x = joined(xparts)
    xh, _r = norm_parts(x)
    nmid_ref[...] = (xh * par_ref[G1:G1 + 1] + par_ref[B1:B1 + 1]).astype(BF)
    res_ref[...] = x + par_ref[OB:OB + 1]
    lse_ref[...] = jnp.zeros_like(lse_ref)
    pl.semaphore_wait(go, 3)
    c_begin()
    wi_load.wait()
    wo_load.wait()

    @pl.loop(0, 3)
    def _(i):
        cut = lambda j: pl.ds(pl.multiple_of(768 * j + 256 * i, 256), 256)
        at = cut(0)
        nin = nmid_ref[...]
        q_ref[:, at] = (nn(nin, wi_ref[:, cut(0)]) + par_ref[QB:QB + 1, at]).astype(BF)
        k_ref[:, at] = nn(nin, wi_ref[:, cut(1)]).astype(BF)
        v_ref[:, at] = (nn(nin, wi_ref[:, cut(2)]) + par_ref[VB:VB + 1, at]).astype(BF)
        eq, ek = eq_ref[...], ek_ref[...]
        for pair in range(2):
            cols = pl.ds(pl.multiple_of(256 * i + 128 * pair, 128), 128)
            qp = q_ref[:, cols] * jnp.asarray(0.125, BF)
            kp = jnp.concatenate([k_ref[:, cols], ek], axis=1)
            zero = jnp.zeros_like(qp)
            both = jnp.concatenate([jnp.concatenate([jnp.where(lane < 64, qp, zero), eq], axis=1),
                                    jnp.concatenate([jnp.where(lane < 64, zero, qp), eq], axis=1)], axis=0)
            s = nt(both, kp)
            m = jnp.max(s, axis=-1, keepdims=True)
            e = jnp.exp(s - m)
            t = jnp.sum(e, axis=-1, keepdims=True)
            p = (e * (1.0 / t)).astype(BF)
            o = nn(p, v_ref[:, cols])
            log = m + jnp.log(t)
            head = 4 * i + 2 * pair
            lse_ref[...] = jnp.where(lane == head, log[:rows], jnp.where(lane == head + 1, log[rows:], lse_ref[...]))
            att_ref[:, cols] = jnp.where(lane < 64, o[:rows], o[rows:]).astype(BF)
        res_ref[...] += nn(att_ref[:, at], wo_ref[at, :])

    res = res_ref[...]
    xh, _r = norm_parts(res)
    nmid = (xh * par_ref[G2:G2 + 1] + par_ref[B2:B2 + 1]).astype(BF)
    nmid_ref[...] = nmid
    nmt[...] = nmid.T
    down_ref[...] = res + par_ref[DB:DB + 1]

    def cot_in():
        c_arrived()
        c_sent()
        cot = joined(cotparts).astype(BF)
        cot_ref[...] = cot
        cott[...] = cot.T

    def unit(n, wide, keep, got, one, two, **more):
        if wide:
            lo, hi = pl.ds(0, 384), pl.ds(384, 384)
            p = dict(a_send=[keep.at[1, :, lo], keep.at[:, 1, hi]], b_send=[keep.at[0, 1, lo], keep.at[1, 0, hi]],
                     a_keep=[[keep.at[0, k, lo] for k in range(2)], [keep.at[k, 0, hi] for k in range(2)]],
                     b_keep=[keep.at[0, 0, lo], keep.at[0, 0, hi]])
        else:
            p = dict(a_send=[keep.at[0, 1], keep.at[1, :, 1]], b_send=[keep.at[0, 0, 1], keep.at[1, 1, 0]],
                     a_keep=[[keep.at[0, 0, k] for k in range(2)], [keep.at[1, k, 0] for k in range(2)]],
                     b_keep=[keep.at[0, 0, 0], keep.at[1, 0, 0]])
        return dict(p, n=n, keep=keep, got=got, one=one, two=two, **more)

    mlp = [[unit(2 * j + u, True, mk.at[j, u], mc.at[j % 2, u], m1.at[j, u], m2.at[j, u], j=j, u=u) for u in range(2)]
           for j in range(3)]
    io = [unit(6 + c, False, ik.at[c], ic.at[(c + 1) % 2], i1.at[c], i2.at[c]) for c in range(4)]
    sends = []

    def start(c):
        c.start()
        sends.append(c)
        return c

    def place(s):
        return (s & 1) * 2 + (s >> 1)

    def core_start(p, src):
        if p["n"] in AFTER:
            pl.semaphore_wait(credit.at[AFTER[p["n"]]], 1)
        p["c"] = remote(src, p["got"], core_s.at[p["n"]], core_r.at[p["n"]], peers[0])
        p["c"].start()
        p["open"] = True

    def core_sent(p):
        if p.pop("open", False):
            p["c"].wait_send()

    def core_done(p):
        n = p["n"]
        p["c"].wait_recv()
        keep, got = p["keep"], p["got"]
        for a in range(2):
            for b in range(2):
                if "j" in p:
                    keep[a, b] += got[a, b]
                else:
                    keep[:, a, b] += got[:, a, b]
        if n in AFTER.values():
            pl.semaphore_signal(credit.at[n], inc=1, device_id=peers[0], device_id_type=MESH)

    def one_start(p):
        n = p["n"]
        p["a"] = [start(remote(p["a_send"][h], p["one"].at[h], a_s.at[2 * n + h], a_r.at[2 * n + h], peers[1 + h])) for h in range(2)]

    def one_done(p):
        n = p["n"]
        for h in range(2):
            p["a"][h].wait_recv()
            for k in range(2):
                p["a_keep"][h][k][...] += p["one"][h, k]
        p["b"] = [start(remote(p["b_send"][h], p["two"].at[h], b_s.at[2 * n + h], b_r.at[2 * n + h], peers[2 - h])) for h in range(2)]

    def two_done(p):
        n = p["n"]
        for h in range(2):
            p["b"][h].wait_recv()
            p["b_keep"][h][...] += p["two"][h]
        if "j" in p:
            src, dst = mk.at[p["j"], p["u"], 0, 0, pl.ds(384, 384)], m3.at[p["j"], p["u"]]
        else:
            c = n - 6
            for b in range(4):
                for t, tile in enumerate(TILES[c][b]):
                    izs[c, place(xor(b, z)), t] = ik[c, tile // 3, 0, 0, :, 128 * (tile % 3):128 * (tile % 3) + 128]
            src, dst = izs.at[c, pl.ds(2, 2)], iz1.at[c]
        p["z"] = start(remote(src, dst, z_s.at[2 * n], z_r.at[2 * n], along[1]))

    def near_done(p):
        n = p["n"]
        p["z"].wait_recv()
        if "j" in p:
            j, u = p["j"], p["u"]
            mk[j, u, 0, 0, 0:384] += m3[j, u]
            src, dst = mk.at[j, u, 0, 0, pl.ds(192, 192)], m4.at[j, u]
        else:
            c = n - 6
            for k in range(2):
                izs[c, k] += iz1[c, k]
            src, dst = izs.at[c, 1], iz2.at[c]
        p["z"] = start(remote(src, dst, z_s.at[2 * n + 1], z_r.at[2 * n + 1], along[2]))

    def far_done(p):
        p["z"].wait_recv()
        if "j" in p:
            j, u = p["j"], p["u"]
            mlp_out[j, u] = mk[j, u, 0, 0, 0:192].astype(F32) + m4[j, u].astype(F32)
        else:
            c = p["n"] - 6
            io_out[c] = izs[c, 0].astype(F32) + iz2[c].astype(F32)

    vec = vs.at[0]
    vec[12:16] = jnp.zeros((4, D), F32)

    def hidden_bias(t):
        return par_ref[8 + t // 6:9 + t // 6, 128 * (t % 6):128 * (t % 6) + 128]

    def mlp_forward(j, i):
        s = j % 2
        wu = wu_ref[s, :, 512 * i:512 * i + 512]
        wd = wd_ref[s, 4 * i:4 * i + 4].reshape(512, D)
        ub = jnp.concatenate([hidden_bias(3 * b + j) for b in range(4 * i, 4 * i + 4)], axis=1)
        act, der = gelu_parts(nn(nmid_ref[...], wu) + ub)
        hid = act.astype(BF)
        hid_ref[:, 512 * i:512 * i + 512] = hid
        der_ref[:, 512 * i:512 * i + 512] = der
        down_ref[...] += nn(hid, wd)

    def mlp_down_grad(j):
        if j:
            core_sent(mlp[j - 1][1])
        else:
            cot_in()
        for i in range(2):
            tmp[...] = nn(cott[...], hid_ref[:, 512 * i:512 * i + 512]).astype(BF)
            for k in range(2):
                for p in range(2):
                    out = (mk.at[j], ms)[p]
                    h = xor(inner & 1, p)
                    rel = xor(2 * (2 * i + k) + h, inner)
                    xb, yb = (rel >> 1) & 1, rel >> 2
                    for b in range(4):
                        to = pl.ds(pl.multiple_of(place(xor(b, z)) * 192, 64), 192)
                        out[1, xb, yb, to, :] = tmp[192 * b:192 * b + 192, pl.ds(pl.multiple_of(256 * k + 128 * h, 128), 128)]
        core_start(mlp[j][1], ms.at[1])

    def mlp_backward(j, i):
        s = j % 2
        wu = wu_ref[s, :, 512 * i:512 * i + 512]
        wd = wd_ref[s, 4 * i:4 * i + 4].reshape(512, D)
        gu = (nt(cot_ref[...], wd) * der_ref[:, 512 * i:512 * i + 512]).astype(BF)
        part = nt(gu, wu)
        dn_ref[...] = part if j == 0 and i == 0 else dn_ref[...] + part
        sums = col(gu.astype(F32))
        for b in range(4):
            t = 3 * (4 * i + b) + j
            vec[8 + t // 6:9 + t // 6, 128 * (t % 6):128 * (t % 6) + 128] = sums[:, 128 * b:128 * b + 128]
        if i == 0 and j:
            core_sent(mlp[j - 1][0])
        tmp[...] = nn(nmt[...], gu).astype(BF)
        for r in range(8):
            out = mk.at[j] if r % 2 == 0 else ms
            xb, yb = r >> 1 & 1, r >> 2
            rows_at = pl.ds(pl.multiple_of(xor(inner, r) * 96, 32), 96)
            for k in range(2):
                to = place(xor(2 * i + k, z)) * 192
                for h in range(2):
                    out[0, xb, yb, pl.ds(pl.multiple_of(to + 96 * h, 32), 96), :] = tmp[rows_at, 256 * k + 128 * h:256 * k + 128 * h + 128]

    def forward(j, i):
        if i == 0:
            for c in mlp_loads[j]:
                c.wait()
        mlp_forward(j, i)

    def backward(j, i):
        mlp_backward(j, i)
        if i == 1:
            core_start(mlp[j][0], ms.at[0])
            if j == 0:
                mlp_loads.append(load_mlp(2))

    def homeward(which, src, dst):
        def parts(d):
            return remote(src.at[d], dst.at[slot], h_s.at[4 * which + d], h_r.at[3 * which + slot], {"seq": lax.rem(z - d + 4, 4)})

        own = pltpu.make_async_copy(src.at[0], dst.at[slot], h_s.at[4 * which])

        @pl.when(owner)
        def _():
            for d in range(1, 4):
                parts(d).start()
            own.start()

        def finish():
            @pl.when(owner)
            def _():
                for d in range(1, 4):
                    parts(d).wait_send()
                own.wait()

            for k in range(3):
                @pl.when(k + core != z)
                def _():
                    remote(src.at[0], dst.at[k], h_s.at[4 * which], h_r.at[3 * which + k], {"seq": xor(z, 1)}).wait_recv()
        return finish

    ends = []

    def block_home():
        down = down_ref[...]
        for d in range(4):
            bo[d, 0:PART] = down[PART * d:PART * d + PART].astype(BF)
        ends.append(homeward(0, bo, bo_home))


    def scatter(c, val):
        for before in {3: mlp[2], 0: [io[3]], 1: [io[0]], 2: [io[1]]}[c]:
            core_sent(before)
        for half in range(2):
            tmp[:, 0:384] = val[:, 384 * half:384 * half + 384].astype(BF)
            for r in range(8):
                xb, yb = r >> 1 & 1, r >> 2
                rows_at = pl.ds(pl.multiple_of(xor(inner, r) * 96, 32), 96)
                if r % 2:
                    isnd[half, xb, yb] = tmp[rows_at, 0:384]
                else:
                    ik[c, half, xb, yb] = tmp[rows_at, 0:384]
        core_start(io[c], isnd)

    gproj, nint, dm, acc = nmid_ref, nmt, cot_ref, dn_ref

    def middle():
        cot = cot_ref[...].astype(F32)
        dy = dn_ref[...]
        xh, r = norm_parts(res_ref[...])
        g = cot + norm_back(dy, par_ref[G2:G2 + 1], xh, r)
        res_ref[...] = g
        gb = g.astype(BF)
        gproj[...] = gb
        vec[4:5] = col(gb.astype(F32))
        vec[5:6] = col(dy * xh)
        vec[6:7] = col(dy)
        vec[7:8] = col(cot)
        scatter(3, tn(att_ref[...], gb))
        xh, r = norm_parts(joined(xparts))
        nint[...] = (xh * par_ref[G1:G1 + 1] + par_ref[B1:B1 + 1]).astype(BF).T

    def pair_back(i, pair, da):
        cols = slice(256 * i + 128 * pair, 256 * i + 128 * pair + 128)
        qp = q_ref[:, cols] * jnp.asarray(0.125, BF)
        kp = k_ref[:, cols]
        zero = jnp.zeros_like(qp)
        qm = jnp.concatenate([jnp.where(lane < 64, qp, zero), jnp.where(lane < 64, zero, qp)], axis=0)
        ext = []
        for h in range(2):
            at = 4 * i + 2 * pair + h
            l = lse_ref[:, at:at + 1]
            hi = l.astype(BF)
            l = l - hi.astype(F32)
            mid = l.astype(BF)
            lo = (l - mid.astype(F32)).astype(BF)
            ext.append(jnp.where(lane == 5, -hi, jnp.where(lane == 6, -mid, jnp.where(lane == 7, -lo, eq_ref[...]))))
        st = nt(jnp.concatenate([kp, ek_ref[...]], axis=1), jnp.concatenate([qm, jnp.concatenate(ext, axis=0)], axis=1))
        p = jnp.exp(st)
        dap = da[:, 128 * pair:128 * pair + 128]
        dob = jnp.concatenate([jnp.where(lane < 64, dap, zero), jnp.where(lane < 64, zero, dap)], axis=0)
        dpt = nt(v_ref[:, cols], dob)
        dv = nn(p.astype(BF), dob)
        inside = jnp.sum(p * dpt, axis=0, keepdims=True)
        ds = (p * (dpt - inside)).astype(BF)
        dk = nn(ds, qm)
        dq = tn(ds, kp) * 0.125
        at = 128 * pair
        dm[:, at:at + 128] = jnp.where(lane < 64, dq[:rows], dq[rows:]).astype(BF)
        dm[:, 256 + at:256 + at + 128] = dk.astype(BF)
        dm[:, 512 + at:512 + at + 128] = dv.astype(BF)

    grad_att = {}

    def head_group(i):
        grad_att[i] = nt(gproj[...], wo_ref[256 * i:256 * i + 256]).astype(BF)

    def group_input(i):
        w = jnp.concatenate([wi_ref[:, 768 * j + 256 * i:768 * j + 256 * i + 256] for j in range(3)], axis=1)
        part = nt(dm[...], w)
        acc[...] = part if i == 0 else acc[...] + part
        vec[2:3, 256 * i:256 * i + 256] = col(dm[:, 0:256].astype(F32))
        vec[3:4, 256 * i:256 * i + 256] = col(dm[:, 512:768].astype(F32))

    def group_weight(i):
        scatter(i, nn(nint[...], dm[...]))

    vcopies = []

    def vsend(stage):
        if stage < 3:
            vcopies.append([start(remote(vs.at[stage], vr.at[stage], v_s.at[stage], v_r.at[stage], peers[stage]))])
        else:
            vcopies.append([start(remote(vs.at[3], vr.at[2 + s], v_s.at[2 + s], v_r.at[2 + s], along[s])) for s in range(1, 4)])

    def vadd(stage):
        for c in vcopies[stage]:
            c.wait_recv()
        if stage < 3:
            vs[stage + 1] = vs[stage] + vr[stage]
            vsend(stage + 1)
        else:
            vec_out[...] = (vs[3] + vr[3]) + (vr[4] + vr[5])

    def last():
        xh, r = norm_parts(joined(xparts))
        dy = acc[...]
        vec[0:1] = col(dy * xh)
        vec[1:2] = col(dy)
        vsend(0)
        gi = res_ref[...] + norm_back(dy, par_ref[G1:G1 + 1], xh, r)
        ing = cotparts
        for d in range(4):
            ing[d, 0:PART] = gi[PART * d:PART * d + PART].astype(BF)
        ends.append(homeward(1, ing, ing_home))

    number = {"F": [(j, i) for j in range(3) for i in range(2)], "B": [(j, i) for j in range(3) for i in range(2)],
              "P": [(i, pair) for i in range(3) for pair in range(2)], "G": range(3), "N": range(3)}
    number = {k: iter(v) for k, v in number.items()}

    simple = {"bo": block_home, "M": middle, "L": last}
    indexed = {"D": mlp_down_grad, "W": group_weight, "v": vadd}
    staged = {"c": core_done, "s": one_start, "a": one_done, "b": two_done, "d": near_done, "e": far_done}
    units = {"I%d" % c: io[c] for c in range(4)}
    units.update({"UD"[u] + "%d" % j: mlp[j][u] for j in range(3) for u in range(2)})
    for step in PLAN:
        if step in simple:
            simple[step]()
        elif step == "F":
            forward(*next(number["F"]))
        elif step == "B":
            backward(*next(number["B"]))
        elif step == "G":
            head_group(next(number["G"]))
        elif step == "P":
            i, pair = next(number["P"])
            pair_back(i, pair, grad_att[i])
        elif step == "N":
            group_input(next(number["N"]))
        elif len(step) == 3:
            staged[step[0]](units[step[1:]])
        else:
            indexed[step[0]](int(step[1]))
    for end in ends:
        end()
    for p in units.values():
        core_sent(p)
    for c in sends:
        c.wait_send()


def layer(stride, patches, segments, cotangent, vectors, wi, wo, wu, wd):
    D = patches.shape[2]
    rows = 4 * PART
    S = jax.ShapeDtypeStruct
    V = pltpu.VMEM
    hbm = pl.BlockSpec(memory_space=pl.ANY)
    vm = pl.BlockSpec(memory_space=pltpu.VMEM)
    wide = lambda t=BF: V((rows, D), t)
    dma = lambda n: pltpu.SemaphoreType.DMA((n,))
    return pl.pallas_call(
        functools.partial(layer_kernel, stride),
        in_specs=[vm] * 12 + [hbm] * 4,
        out_specs=[hbm, hbm, vm, vm, vm],
        out_shape=[S((3, SENT, D), BF), S((3, SENT, D), BF), S((3, 2, 192, 128), F32), S((4, 2, 96, 128), F32), S((16, D), F32)],
        scratch_shapes=[V((16, D), F32), V((4, SENT, D), BF), V((4, SENT, D), BF), wide(), V((D, rows), BF), wide(), wide(), wide(), wide(),
                        V((rows, 128), F32), V((rows, 128), BF), V((rows, 128), BF), wide(F32), wide(F32), wide(F32),
                        wide(), V((D, rows), BF), V((D, 512), BF), V((4, SENT, D), BF),
                        V((D, 3 * D), BF), V((D, D), BF), V((2, D, 1024), BF), V((2, 8, 128, D), BF),
                        V((rows, 1024), BF), V((rows, 1024), F32),
                        V((3, 2, 2, 2, 768, 128), BF), V((2, 2, 2, 768, 128), BF), V((2, 2, 2, 2, 768, 128), BF),
                        V((3, 2, 2, 2, 384, 128), BF), V((3, 2, 2, 384, 128), BF), V((3, 2, 384, 128), BF), V((3, 2, 192, 128), BF),
                        V((4, 2, 2, 2, 96, 384), BF), V((2, 2, 2, 96, 384), BF), V((2, 2, 2, 2, 96, 384), BF),
                        V((4, 2, 2, 96, 384), BF), V((4, 2, 96, 384), BF),
                        V((4, 4, 2, 96, 128), BF), V((4, 2, 2, 96, 128), BF), V((4, 2, 96, 128), BF),
                        V((4, 16, D), F32), V((6, 16, D), F32),
                        dma(29), dma(10), dma(10), dma(20), dma(20), dma(20), dma(20), dma(20), dma(20),
                        dma(6), dma(6), dma(8), dma(6), dma(8), dma(8), pltpu.SemaphoreType.REGULAR((10,)), pltpu.SemaphoreType.REGULAR],
        name="layer",
        compiler_params=pltpu.CompilerParams(vmem_limit_bytes=VL, collective_id=0, has_side_effects=True),
        cost_estimate=pl.CostEstimate(flops=30_000_000 * 1000, bytes_accessed=16_000_000, transcendentals=0),
    )(patches, segments, cotangent, *vectors, wi, wo, wu, wd)


def outputs_kernel(bo_hbm, ing_hbm, mlp_hbm, io_hbm, vec_hbm, *refs):
    results, vec_outs, refs = refs[:6], refs[6:15], refs[15:]
    (bo, ing, mlp, io, vec), (bo_out, ing_out, wi_out, wo_out, wu_out, wd_out), arrive, leave = refs[:5], refs[5:11], refs[11], refs[12]
    length = bo_out.shape[1]
    ins = [pltpu.make_async_copy(ing_hbm.at[k], ing.at[k], arrive.at[k]) for k in range(3)]
    ins += [pltpu.make_async_copy(bo_hbm.at[k], bo.at[k], arrive.at[3 + k]) for k in range(3)]
    ins += [pltpu.make_async_copy(a, b, arrive.at[6 + k]) for k, (a, b) in enumerate(((mlp_hbm, mlp), (io_hbm, io), (vec_hbm, vec)))]
    for c in ins:
        c.start()
    outs = []

    def write(src, dst):
        c = pltpu.make_async_copy(src, dst, leave.at[len(outs)])
        c.start()
        outs.append(c)

    for k in range(3):
        ins[k].wait()
        ing_out[k] = ing[k].astype(F32)[:length]
        write(ing_out.at[k], results[1].at[k])
    for k in range(3):
        ins[3 + k].wait()
        bo_out[k] = bo[k].astype(F32)[:length].astype(BF)
        write(bo_out.at[k], results[0].at[k])
    ins[6].wait()
    for j in range(3):
        for h in range(2):
            wu_out[:, 384 * h + 128 * j:384 * h + 128 * j + 128] = mlp[j, 0, 96 * h:96 * h + 96]
        wd_out[:, 128 * j:128 * j + 128] = mlp[j, 1]
    write(wu_out, results[4])
    write(wd_out, results[5])
    ins[7].wait()
    z = lax.axis_index("seq")
    order = (((0, 0), (0, 1), (1, 0), (1, 1), (2, 0)), ((2, 0), (2, 1), (0, 0), (0, 1), (1, 0)),
             ((1, 0), (2, 0), (2, 1), (0, 0), (0, 1)), ((0, 0), (1, 0), (1, 1), (2, 0), (2, 1)))
    for b in range(4):
        @pl.when(z == b)
        def _():
            wi = jnp.concatenate([io[c, t] for c, t in order[b]], axis=1)
            wo = jnp.concatenate([io[3, 0], io[3, 1]], axis=1)
            if b % 2:
                wi, wo = pltpu.roll(wi, 640 - 64, 1), pltpu.roll(wo, 256 - 64, 1)
            wi_out[...] = wi[:, :576]
            wo_out[...] = wo[:, :192]

    write(wi_out, results[2])
    write(wo_out, results[3])
    ins[8].wait()
    for i, out in enumerate(vec_outs[:8]):
        out[...] = vec[i:i + 1].reshape(out.shape)
    vec_outs[8][...] = jnp.concatenate([vec[8 + i:9 + i] for i in range(4)], axis=1).reshape(vec_outs[8].shape)
    for c in outs:
        c.wait()


def outputs(length, bo, ing, mlp, io, vec):
    D = bo.shape[2]
    S = jax.ShapeDtypeStruct
    vm = pl.BlockSpec(memory_space=pltpu.VMEM)
    hbm = pl.BlockSpec(memory_space=pl.ANY)
    big = [S((3, length, D), BF), S((3, length, D), F32), S((96, 576), F32), S((96, 192), F32), S((96, D), F32), S((192, 384), F32)]
    held = [pltpu.VMEM(a.shape, a.dtype) for a in (bo, ing, mlp, io, vec, *big)]
    return pl.pallas_call(outputs_kernel, in_specs=[hbm] * 5, out_specs=[hbm] * 6 + [vm] * 9,
                          out_shape=big + [S((D,), F32)] * 8 + [S((4 * D,), F32)], name="outputs",
                          scratch_shapes=held + [pltpu.SemaphoreType.DMA((9,)), pltpu.SemaphoreType.DMA((10,))],
                          compiler_params=pltpu.CompilerParams(vmem_limit_bytes=VL))(bo, ing, mlp, io, vec)


def on_device(n_dp, patches, segments, first_gain, first_bias, input_weight, query_bias, value_bias, output_weight,
              output_bias, second_gain, second_bias, up_weight, up_bias, down_weight, down_bias, cotangent):
    strips, length, D = patches.shape
    stride = n_dp // 8
    vectors = (first_gain, first_bias, query_bias, value_bias, output_bias, second_gain, second_bias, down_bias, up_bias)
    bo, ing, mlp, io, vec = layer(stride, patches, segments, cotangent, vectors, input_weight, output_weight, up_weight,
                                  down_weight.reshape(8, 3, 128, D))
    (block_output, input_grad, in_grad, out_grad, up_grad, down_grad, *vecs) = outputs(length, bo, ing, mlp, io, vec)
    weights = [in_grad, out_grad, up_grad, down_grad.T]
    if stride > 1:
        groups = [[g * stride + t for t in range(stride)] for g in range(8)]
        weights = [lax.psum_scatter(w, "dp", scatter_dimension=0, axis_index_groups=groups, tiled=True) for w in weights]
        vecs = lax.psum(vecs, "dp", axis_index_groups=groups)
    in_grad, out_grad, up_grad, down_grad = weights
    return (block_output, input_grad, vecs[0], vecs[1], in_grad, vecs[2], vecs[3], out_grad, vecs[4], vecs[5], vecs[6], up_grad,
            vecs[8], down_grad, vecs[7])


def solution(mesh):
    rep = P()
    rows = P("dp", "seq", None)
    cut = P("dp", "seq")
    return jax.shard_map(
        functools.partial(on_device, mesh.shape["dp"]),
        mesh=mesh,
        in_specs=(rows, cut) + (rep,) * 13 + (rows,),
        out_specs=(rows, rows, rep, rep, cut, rep, rep, cut, rep, rep, rep, cut, rep, cut, rep),
        check_vma=False,
    )
```
